32 devices in a mesh: group: 8 (over z, core), tensor: 4 (over y, x).
Axes of the slice: x: 2, y: 2, z: 4, core: 2. Of those that a mesh axis runs over, the one named last changes fastest.
Arguments:
- hidden_rows: bfloat16 [3072, 8192], P('group', 'tensor'), may hold values from -6 to 6
- attn_rows: bfloat16 [3072, 8192], P('group', 'tensor'), may hold values from -6 to 6
- q_weight: bfloat16 [8192, 8192], P(None, 'tensor'), may hold values from -0.0625 to 0.0625
- o_weight: bfloat16 [8192, 8192], P('tensor'), may hold values from -0.0625 to 0.0625
- owner_table: int32 [64], replicated, may hold values from 0 to 63, as said below
- group_adapters: int32 [8, 8], replicated, may hold values from 0 to 63, as said below
- req_slot: int32 [8, 16], P('group'), may hold values from 0 to 7
- req_len: int32 [8, 16], P('group'), may hold values from 1 to 96, 384 in all within a row
- qa_store: bfloat16 [64, 8192, 64], P('group', 'tensor'), may hold values from -0.0625 to 0.0625
- qb_store: bfloat16 [64, 64, 8192], P('group', None, 'tensor'), may hold values from -0.75 to 0.75
- oa_store: bfloat16 [64, 8192, 64], P('group', 'tensor'), may hold values from -0.0625 to 0.0625
- ob_store: bfloat16 [64, 64, 8192], P('group', None, 'tensor'), may hold values from -0.75 to 0.75
Outputs:
- queries: bfloat16 [3072, 8192], P('group', 'tensor')
- attn_out: bfloat16 [3072, 8192], P('group')
The draws below stay inside these ranges and needn't reach their ends.
Inputs may be any that keep to these rules, and one draw needn't show every extreme that they name: A permutation: adapter a sits at storage index owner_table[a], held by index owner_table[a] // 8 of group. `group_adapters`: each row names 8 distinct adapters, exactly 1 of them held by each index of group; different groups may name the same adapter.
All inputs are finite; a program needn't handle non-finite values.
Results may differ from the reference program's by a relative error of at most 0.001.
Values may be sent and summed in bfloat16 or wider, within the bound.
No kernel may reach another device: no remote copies, remote signals or barrier semaphores. Data moves between devices by JAX's collectives and lax.ppermute only.
A program may use at most 192 MiB of HBM per device.

```python
import math
import jax
import jax.numpy as jnp
import numpy as np
from jax import lax

D = 8192
R = 64
SLOTS = 8
REQS = 16
ROWS = 384
ADP_DEV = 8
GROUPS = 8
ADAPTERS = 64
MOST = 96
ROWS_ALL = 3072


def layout(key):
    base_product = jax.random.fold_in(key, 11)
    key_table, key_order, key_local = jax.random.split(base_product, 3)
    table = jax.random.permutation(key_table, ADAPTERS).astype(jnp.int32)
    holder = jnp.argsort(table).astype(jnp.int32)
    slot_start_offset = jnp.arange(SLOTS, dtype=jnp.int32)
    owners = slot_start_offset % GROUPS
    member_rank = slot_start_offset // GROUPS

    def local_draw(subkey):
        return jax.random.permutation(subkey, ADP_DEV).astype(jnp.int32)

    def order_draw(subkey):
        return jax.random.permutation(subkey, SLOTS).astype(jnp.int32)
    local_perm = jax.vmap(local_draw)(jax.random.split(key_local, GROUPS))
    chosen = jnp.take(local_perm, member_rank, axis=1)
    storage = owners[None, :] * ADP_DEV + chosen
    orders = jax.vmap(order_draw)(jax.random.split(key_order, GROUPS))
    storage = jnp.take_along_axis(storage, orders, axis=1)
    return (table, jnp.take(holder, storage, axis=0).astype(jnp.int32))


def draw_owner_table(key, part):
    return layout(key)[0]


def draw_group_adapters(key, part):
    return layout(key)[1]


def set_ends(drawn, rng, least, top_value):
    dims = drawn.shape
    spot = [jax.random.randint(jax.random.fold_in(rng, axis), (), 0, dims[axis]) for axis in range(len(dims))]
    drawn = drawn.at[tuple(spot)].set(least)
    longest = dims.index(max(dims))
    spot[longest] = (spot[longest] + 1) % dims[longest]
    return drawn.at[tuple(spot)].set(top_value)


def levels(own_key, extent, shards, least, top_value):
    def one(dim, parts):
        draws = jax.random.uniform(jax.random.fold_in(jax.random.fold_in(own_key, 6), dim), (parts,), jnp.float32, least / len(shards), top_value / len(shards))
        return jnp.repeat(jnp.exp(draws), extent[dim] // parts).reshape((-1,) + (1,) * (len(extent) - dim - 1))

    gain = one(*shards[0])
    for cut in shards[1:]:
        gain = gain * one(*cut)
    return gain


def cumulative_ranks(number_of, slope):
    loads = [(1 << 20) // math.isqrt(rank ** slope) + 1 for rank in range(1, number_of + 1)]
    deviation = 1 + sum(loads) // (1 << 30)
    return np.cumsum(np.array([max(1, weight // deviation) for weight in loads]))


def ranked(rng, extent, count, skew):
    grid = cumulative_ranks(count, skew)
    pick = jax.random.randint(jax.random.fold_in(rng, 1), extent, 0, int(grid[count - 1]))
    standing = jnp.searchsorted(jnp.asarray(grid, jnp.int32), pick, side="right")
    return jax.random.permutation(jax.random.fold_in(rng, 2), count)[standing].astype(jnp.int32)


def profile(count, total, limit, skew):
    weights = [(1 << 20) // math.isqrt(standing ** skew) + 1 for standing in range(2, count + 1)]
    surplus, given = total - limit - (count - 1), [1] * (count - 1)
    while surplus > 0:
        candidates = [i for i in range(count - 1) if given[i] < limit]
        whole, budget = sum([weights[i] for i in candidates]), surplus
        for i in candidates:
            more = min(limit - given[i], max(1, budget * weights[i] // whole), surplus)
            given[i] = given[i] + more
            surplus = surplus - more
    return np.array([limit] + given)


def uneven(own_key, count, total, most, skew):
    if count == 2:
        one = jax.random.randint(own_key, (), max(1, total - most), min(most, total - 1) + 1)
        return jnp.stack([one, total - one])
    tallies = jnp.asarray(profile(count, total, most, skew), jnp.int32)
    pairs = (count - 1) // 2
    donor, taker = tallies[1:1 + 2 * pairs:2], tallies[2:2 + 2 * pairs:2]
    margin = jnp.minimum(donor - 1, most - taker)
    shifted = jax.random.randint(jax.random.fold_in(own_key, 1), (pairs,), 0, 1 << 20) % (margin + 1)
    tallies = tallies.at[1:1 + 2 * pairs:2].set(donor - shifted).at[2:2 + 2 * pairs:2].set(taker + shifted)
    return tallies[jax.random.permutation(jax.random.fold_in(own_key, 2), count)]


def normal_values(rng, dims, scale, limit, cuts=(), held_as=jnp.bfloat16):
    level = levels(rng, dims, cuts, -0.22, 0.18) if cuts else 1.0
    drawn = jax.random.normal(rng, dims, jnp.float32) * scale * level
    return jnp.minimum(jnp.maximum(drawn, -limit), limit).astype(held_as)


def setup_inputs(seed: int = 0) -> dict:
    arg_keys = jax.random.split(jax.random.key(seed), 13)
    hidden_rows = normal_values(arg_keys[0], (ROWS_ALL, D), 1.0, 6.0, ((0, 8), (1, 4)))
    attn_rows = normal_values(arg_keys[1], (ROWS_ALL, D), 1.0, 6.0, ((0, 8), (1, 4)))
    q_weight = normal_values(arg_keys[2], (D, D), D ** -0.5, 0.0625, ((1, 4),))
    o_weight = normal_values(arg_keys[3], (D, D), D ** -0.5, 0.0625, ((0, 4),))
    owner_table = draw_owner_table(jax.random.fold_in(arg_keys[12], 71), 0)
    group_adapters = draw_group_adapters(jax.random.fold_in(arg_keys[12], 71), 0)
    req_slot = set_ends(ranked(arg_keys[6], (GROUPS, REQS), SLOTS, 2), jax.random.fold_in(arg_keys[6], 3), 0, SLOTS - 1).astype(jnp.int32)
    req_len = jax.vmap(lambda own: uneven(own, REQS, ROWS, MOST, 2))(jax.random.split(arg_keys[7], GROUPS)).reshape((GROUPS, REQS)).astype(jnp.int32)
    qa_store = normal_values(arg_keys[8], (ADAPTERS, D, R), D ** -0.5, 0.0625, ((0, 8), (1, 4)))
    qb_store = normal_values(arg_keys[9], (ADAPTERS, R, D), R ** -0.5, 0.75, ((0, 8), (2, 4)))
    oa_store = normal_values(arg_keys[10], (ADAPTERS, D, R), D ** -0.5, 0.0625, ((0, 8), (1, 4)))
    ob_store = normal_values(arg_keys[11], (ADAPTERS, R, D), R ** -0.5, 0.75, ((0, 8), (2, 4)))
    return {"hidden_rows": hidden_rows, "attn_rows": attn_rows, "q_weight": q_weight, "o_weight": o_weight, "owner_table": owner_table, "group_adapters": group_adapters, "req_slot": req_slot, "req_len": req_len, "qa_store": qa_store, "qb_store": qb_store, "oa_store": oa_store, "ob_store": ob_store}


ADAPTER_SCALE = 0.5


def slot_onehot(lengths, slot_ids):
    req_ends = jnp.cumsum(lengths).astype(jnp.int32)
    req_starts = (req_ends - lengths).astype(jnp.int32)
    position = jnp.arange(ROWS, dtype=jnp.int32)[:, None]
    inside = ((position >= req_starts[None, :]) & (position < req_ends[None, :])).astype(jnp.int32)
    slot_row = jnp.sum(inside * slot_ids[None, :], axis=1).astype(jnp.int32)
    return slot_row[:, None] == jnp.arange(SLOTS, dtype=jnp.int32)[None, :]


def adapted(rows_in, weight, down_all, up_all, onehot):
    down_flat = jnp.transpose(down_all, (1, 0, 2)).reshape(down_all.shape[1], SLOTS * R)
    up_weight_flat = up_all.reshape(SLOTS * R, up_all.shape[2]).astype(jnp.float32)
    partial_down = jnp.dot(rows_in, down_flat, preferred_element_type=jnp.float32).reshape(ROWS, SLOTS, R)
    chosen = jnp.sum(onehot.astype(jnp.float32)[:, :, None] * partial_down, axis=1)
    expanded_rows = (onehot.astype(jnp.float32)[:, :, None] * chosen[:, None, :]).reshape(ROWS, SLOTS * R)
    base_product = jnp.dot(rows_in, weight, preferred_element_type=jnp.float32)
    up_term = jnp.dot(expanded_rows, up_weight_flat, precision=lax.Precision.HIGHEST, preferred_element_type=jnp.float32)
    return (base_product + ADAPTER_SCALE * up_term).astype(jnp.bfloat16)


def reference(hidden_rows, attn_rows, q_weight, o_weight, owner_table, group_adapters, req_slot, req_len, qa_store, qb_store, oa_store, ob_store):
    query_parts = []
    output_parts = []
    for group_id in range(GROUPS):
        storage = jnp.take(owner_table, group_adapters[group_id], axis=0).astype(jnp.int32)
        onehot = slot_onehot(req_len[group_id], req_slot[group_id])
        hidden_block = hidden_rows[group_id * ROWS:(group_id + 1) * ROWS]
        attn_block = attn_rows[group_id * ROWS:(group_id + 1) * ROWS]
        query_parts.append(adapted(hidden_block, q_weight, jnp.take(qa_store, storage, axis=0), jnp.take(qb_store, storage, axis=0), onehot))
        output_parts.append(adapted(attn_block, o_weight, jnp.take(oa_store, storage, axis=0), jnp.take(ob_store, storage, axis=0), onehot))
    return jnp.concatenate(query_parts, axis=0), jnp.concatenate(output_parts, axis=0)
```

```python
import functools

import jax
import jax.numpy as jnp
from jax import lax
from jax.experimental import pallas as pl
from jax.experimental.pallas import tpu as pltpu
from jax.sharding import PartitionSpec as P

ADAPTER_SCALE = 0.5
VMEM_BYTES = 48 * 1024 * 1024
ANY = pl.BlockSpec(memory_space=pl.ANY)
SMEM = pl.BlockSpec(memory_space=pltpu.SMEM)
VMEM = pl.BlockSpec(memory_space=pltpu.VMEM)


def params():
    return pltpu.CompilerParams(vmem_limit_bytes=VMEM_BYTES)


def cost(flops, nbytes):
    return pl.CostEstimate(flops=flops, bytes_accessed=nbytes, transcendentals=0)


def send(value, axis, offset):
    size = lax.axis_size(axis)
    return lax.ppermute(value, axis, [(i, i ^ offset) for i in range(size)])


def bits(size):
    out = []
    bit = 1
    while bit < size:
        out.append(bit)
        bit *= 2
    return out


def pack_kernel(stacked, table_ref, adapters_ref, *refs):
    groups = adapters_ref.shape[0]
    slots = adapters_ref.shape[1]
    stores = refs[:stacked]
    outs = refs[-1 - groups : -1]
    sems = refs[-1]
    held = stores[0].shape[0]
    rank = stores[0].shape[1]
    me = lax.axis_index("group")
    copies = []
    for dist in range(groups):
        dest = me ^ dist
        pick = jnp.int32(0)
        for slot in range(slots):
            place = table_ref[adapters_ref[dest, slot]]
            owner = lax.div(place, jnp.int32(held))
            pick = jnp.where(owner == me, place - owner * held, pick)
        for part in range(stacked):
            copy = pltpu.make_async_copy(
                stores[part].at[pick],
                outs[dist].at[pl.ds(part * rank, rank)],
                sems.at[dist, part],
            )
            copy.start()
            copies.append(copy)
    for copy in copies:
        copy.wait()


def pack(table, adapters, stores, after=()):
    groups = adapters.shape[0]
    held, rank, width = stores[0].shape
    stacked = len(stores)
    shape = jax.ShapeDtypeStruct((stacked * rank, width), stores[0].dtype)
    moved = 2 * groups * stacked * rank * width * 2
    return pl.pallas_call(
        functools.partial(pack_kernel, stacked),
        out_shape=[shape] * groups,
        in_specs=[SMEM, SMEM] + [ANY] * (stacked + len(after)),
        out_specs=[ANY] * groups,
        scratch_shapes=[pltpu.SemaphoreType.DMA((groups, stacked))],
        compiler_params=params(),
        cost_estimate=cost(0, moved),
    )(table, adapters, *stores, *after)


def row_distance(table_ref, adapters_ref, slot_ref, len_ref, held, shape):
    me = lax.axis_index("group")
    position = lax.broadcasted_iota(jnp.int32, shape, 0)
    found = jnp.zeros(shape, jnp.int32)
    start = jnp.int32(0)
    for req in range(len_ref.shape[1]):
        place = table_ref[adapters_ref[me, slot_ref[0, req]]]
        dist = lax.div(place, jnp.int32(held)) ^ me
        end = start + len_ref[0, req]
        found = jnp.where((position >= start) & (position < end), dist, found)
        start = end
    return found


def down_kernel(held, groups, table_ref, adapters_ref, slot_ref, len_ref, attn_ref, hidden_ref, *refs):
    pieces = refs[:groups]
    out_ref, o_all, q_all, sems = refs[groups:]
    rank = pieces[0].shape[0] // 2
    copies = []
    for part, whole in enumerate((o_all, q_all)):
        for dist in range(groups):
            copy = pltpu.make_async_copy(
                pieces[dist].at[pl.ds(part * rank, rank)],
                whole.at[pl.ds(dist * rank, rank)],
                sems.at[part, dist],
            )
            copy.start()
            copies.append(copy)
    rows = attn_ref.shape[0]
    shape = (rows, 2 * rank)
    found = row_distance(table_ref, adapters_ref, slot_ref, len_ref, held, shape)
    lane = lax.broadcasted_iota(jnp.int32, shape, 1)
    high = (lane >= rank).astype(jnp.int32)
    folded = []
    for part, (rows_ref, whole) in enumerate(((attn_ref, o_all), (hidden_ref, q_all))):
        for dist in range(groups):
            copies[part * groups + dist].wait()
        full = lax.dot_general(
            rows_ref[...], whole[...], (((1,), (1,)), ((), ())), preferred_element_type=jnp.float32
        )
        picked = jnp.zeros(shape, jnp.float32)
        for pair in range(groups // 2):
            piece = full[:, pair * 2 * rank : (pair + 1) * 2 * rank]
            picked = picked + jnp.where(found == 2 * pair + high, piece, 0.0)
        folded.append(picked + pltpu.roll(picked, rank, 1))
    out_ref[...] = jnp.where(lane < rank, folded[0], folded[1])


def down(routing, held, attn, hidden, pieces):
    rows, width = attn.shape
    groups = len(pieces)
    rank = pieces[0].shape[0] // 2
    return pl.pallas_call(
        functools.partial(down_kernel, held, groups),
        out_shape=jax.ShapeDtypeStruct((rows, 2 * rank), jnp.float32),
        in_specs=[SMEM] * 4 + [VMEM] * 2 + [ANY] * groups,
        out_specs=VMEM,
        scratch_shapes=[
            pltpu.VMEM((groups * rank, width), attn.dtype),
            pltpu.VMEM((groups * rank, width), attn.dtype),
            pltpu.SemaphoreType.DMA((2, groups)),
        ],
        compiler_params=params(),
        cost_estimate=cost(4 * rows * width * groups * rank, 4 * rows * width + 4 * groups * rank * width),
    )(*routing, attn, hidden, *pieces)


def up_kernel(held, groups, part, split, table_ref, adapters_ref, slot_ref, len_ref, down_ref, *refs):
    pieces = refs[:groups]
    bases = refs[groups : groups + split]
    outs = refs[groups + split : groups + 2 * split]
    terms = refs[-1]
    rank = pieces[0].shape[0]
    rows = down_ref.shape[0]

    @pl.when(pl.program_id(0) == 0)
    def _():
        shape = (rows, 2 * rank)
        found = row_distance(table_ref, adapters_ref, slot_ref, len_ref, held, shape)
        lane = lax.broadcasted_iota(jnp.int32, shape, 1)
        high = (lane >= rank).astype(jnp.int32)
        values = down_ref[...]
        other = pltpu.roll(values, rank, 1)
        both = jnp.where((lane < rank) == (part == 0), values, other) * ADAPTER_SCALE
        first = both.astype(jnp.bfloat16)
        rest = both - first.astype(jnp.float32)
        second = rest.astype(jnp.bfloat16)
        third = (rest - second.astype(jnp.float32)).astype(jnp.bfloat16)
        for number, term in enumerate((first, second, third)):
            for pair in range(groups // 2):
                chosen = jnp.where(found == 2 * pair + high, term.astype(jnp.float32), 0.0)
                terms[number, :, pair * 2 * rank : (pair + 1) * 2 * rank] = chosen.astype(jnp.bfloat16)

    whole = jnp.concatenate([piece[...] for piece in pieces], axis=0)
    total = jnp.dot(terms[2], whole, preferred_element_type=jnp.float32)
    total = total + jnp.dot(terms[1], whole, preferred_element_type=jnp.float32)
    total = total + jnp.dot(terms[0], whole, preferred_element_type=jnp.float32)
    size = rows // split
    for number in range(split):
        value = bases[number][...] + total[number * size : (number + 1) * size]
        outs[number][...] = value.astype(outs[number].dtype)


def up(routing, held, part, downs, pieces, bases, out_dtype):
    groups = len(pieces)
    rank, width = pieces[0].shape
    rows = downs.shape[0]
    split = len(bases)
    tile = min(512, width)
    column = lambda step: (0, step)
    size = rows // split
    return pl.pallas_call(
        functools.partial(up_kernel, held, groups, part, split),
        grid=(width // tile,),
        out_shape=[jax.ShapeDtypeStruct((size, width), out_dtype)] * split,
        in_specs=[SMEM] * 4
        + [pl.BlockSpec(downs.shape, lambda step: (0, 0))]
        + [pl.BlockSpec((rank, tile), column)] * groups
        + [pl.BlockSpec((size, tile), column)] * split,
        out_specs=[pl.BlockSpec((size, tile), column)] * split,
        scratch_shapes=[pltpu.VMEM((3, rows, groups * rank), jnp.bfloat16)],
        compiler_params=params(),
        cost_estimate=cost(6 * rows * width * groups * rank, 8 * rows * width + 2 * groups * rank * width),
    )(*routing, downs, *pieces, *bases)


def o_kernel(block_ref, rows_ref, weight_ref, low_ref, high_ref):
    del block_ref
    half = low_ref.shape[0]
    total = jnp.dot(rows_ref[...], weight_ref[...], preferred_element_type=jnp.float32)
    low_ref[...] = total[:half]
    high_ref[...] = total[half:]


def o_block(block, rows_in, weight, width):
    rows, depth = rows_in.shape
    tile = min(512, width)
    tiles = width // tile
    half = jax.ShapeDtypeStruct((rows // 2, width), jnp.float32)
    out_spec = pl.BlockSpec((rows // 2, tile), lambda step, ref: (0, step))
    return pl.pallas_call(
        o_kernel,
        grid_spec=pltpu.PrefetchScalarGridSpec(
            num_scalar_prefetch=1,
            grid=(tiles,),
            in_specs=[
                pl.BlockSpec((rows, depth), lambda step, ref: (0, 0)),
                pl.BlockSpec((depth, tile), lambda step, ref: (0, ref[0] * tiles + step)),
            ],
            out_specs=[out_spec, out_spec],
        ),
        out_shape=[half, half],
        compiler_params=params(),
        cost_estimate=cost(2 * rows * depth * width, 2 * depth * width + 2 * rows * depth + 4 * rows * width),
    )(block, rows_in, weight)


def q_kernel(has_total, block_ref, low_ref, high_ref, weight_ref, *refs):
    del block_ref
    out_ref = refs[-1]
    half = low_ref.shape[0]
    for number, rows_ref in enumerate((low_ref, high_ref)):
        total = jnp.dot(rows_ref[...], weight_ref[...], preferred_element_type=jnp.float32)
        span = slice(number * half, (number + 1) * half)
        if has_total:
            total = total + refs[0][span]
        out_ref[span] = total


def q_block(block, low, high, weight, total):
    half, depth = low.shape
    width = weight.shape[1]
    tile = min(512, width)
    has_total = total is not None
    whole = pl.BlockSpec((half, depth), lambda step, ref: (0, 0))
    column = pl.BlockSpec((2 * half, tile), lambda step, ref: (0, step))
    return pl.pallas_call(
        functools.partial(q_kernel, has_total),
        grid_spec=pltpu.PrefetchScalarGridSpec(
            num_scalar_prefetch=1,
            grid=(width // tile,),
            in_specs=[
                whole,
                whole,
                pl.BlockSpec((depth, tile), lambda step, ref: (ref[0], step)),
            ]
            + [column] * has_total,
            out_specs=column,
        ),
        out_shape=jax.ShapeDtypeStruct((2 * half, width), jnp.float32),
        input_output_aliases={4: 0} if has_total else {},
        compiler_params=params(),
        cost_estimate=cost(4 * half * depth * width, 2 * depth * width + 4 * half * depth + 16 * half * width),
    )(block, low, high, weight, *([total] * has_total))


def gather_halves(halves):
    size = lax.axis_size("tensor")
    orders = (bits(size), bits(size)[::-1])
    held = [{0: halves[0]}, {0: halves[1]}]
    for step in range(len(orders[0])):
        for number in range(2):
            bit = orders[number][step]
            arrived = {dist ^ bit: send(value, "tensor", bit) for dist, value in held[number].items()}
            held[number].update(arrived)
    return {dist: [held[0][dist], held[1][dist]] for dist in range(size)}


def scatter_halves(partial):
    size = lax.axis_size("tensor")
    orders = (bits(size)[::-1], bits(size))
    held = [{dist: pair[number] for dist, pair in partial.items()} for number in range(2)]
    for step in range(len(orders[0])):
        for number in range(2):
            bit = orders[number][step]
            leaving = [dist for dist in held[number] if dist & bit]
            for dist in sorted(leaving, reverse=True):
                arrived = send(held[number].pop(dist), "tensor", bit)
                held[number][dist ^ bit] = held[number][dist ^ bit] + arrived
    return [held[0][0], held[1][0]]


def place_kernel(count, column_ref, *refs):
    pieces = refs[:count]
    out_ref, sems = refs[-2:]
    half, width = pieces[0].shape
    copies = []
    for number in range(count):
        start = pl.multiple_of(column_ref[number // 2] * width, width)
        copy = pltpu.make_async_copy(
            pieces[number],
            out_ref.at[pl.ds(number % 2 * half, half), pl.ds(start, width)],
            sems.at[number],
        )
        copy.start()
        copies.append(copy)
    for copy in copies:
        copy.wait()


def place(blocks, pieces, into, out_shape):
    count = len(pieces)
    old = [] if into is None else [into]
    moved = 2 * count * pieces[0].size * 2
    return pl.pallas_call(
        functools.partial(place_kernel, count),
        out_shape=out_shape,
        in_specs=[SMEM] + [ANY] * (count + len(old)),
        out_specs=ANY,
        scratch_shapes=[pltpu.SemaphoreType.DMA((count,))],
        input_output_aliases={count + 1: 0} if old else {},
        compiler_params=params(),
        cost_estimate=cost(0, moved),
    )(blocks, *pieces, *old)


def body(
    hidden_rows,
    attn_rows,
    q_weight,
    o_weight,
    owner_table,
    group_adapters,
    req_slot,
    req_len,
    qa_store,
    qb_store,
    oa_store,
    ob_store,
):
    groups = lax.axis_size("group")
    size = lax.axis_size("tensor")
    mine = lax.axis_index("tensor")
    held = qa_store.shape[0]
    rows, part_width = hidden_rows.shape
    width = o_weight.shape[1] // size
    half = rows // 2
    routing = (owner_table, group_adapters, req_slot, req_len)
    block = [jnp.reshape(mine ^ dist, (1,)).astype(jnp.int32) for dist in range(size)]

    halves = [hidden_rows[:half], hidden_rows[half:]]
    hidden = gather_halves(halves)

    oa_turned = jnp.swapaxes(oa_store, 1, 2)
    qa_turned = jnp.swapaxes(qa_store, 1, 2)
    sent = pack(owner_table, group_adapters, (oa_turned, qa_turned))
    downs_used = [sent[0]] + [send(sent[dist], "group", dist) for dist in range(1, groups)]

    partial = {}
    for dist in sorted(range(size), reverse=True):
        partial[dist] = o_block(block[dist], attn_rows, o_weight, width)

    downs = down(routing, held, attn_rows, hidden_rows, downs_used)
    sent = pack(owner_table, group_adapters, (ob_store,), (downs_used[groups - 1],))
    ob_used = [sent[0]] + [send(sent[dist], "group", dist) for dist in range(1, groups)]
    for bit in bits(size):
        downs = downs + send(downs, "tensor", bit)
    sent = pack(owner_table, group_adapters, (qb_store,), (ob_used[groups - 1],))
    qb_used = [sent[0]] + [send(sent[dist], "group", dist) for dist in range(1, groups)]

    partial[0] = up(routing, held, 0, downs, ob_used, partial[0], jnp.float32)
    shares = scatter_halves(partial)
    finished = gather_halves([share.astype(jnp.bfloat16) for share in shares])

    total = None
    for dist in range(size):
        total = q_block(block[dist], *hidden[dist], q_weight, total)
    (queries,) = up(routing, held, 1, downs, qb_used, [total], jnp.bfloat16)

    out_shape = jax.ShapeDtypeStruct((rows, width * size), jnp.bfloat16)
    last = size - 1
    early = place(
        jnp.concatenate(block[:last]), [piece for dist in range(last) for piece in finished[dist]], None, out_shape
    )
    attn_out = place(block[last], finished[last], early, out_shape)
    return (queries, attn_out)


def solution(mesh):
    return jax.shard_map(
        body,
        mesh=mesh,
        in_specs=(
            P("group", "tensor"),
            P("group", "tensor"),
            P(None, "tensor"),
            P("tensor", None),
            P(),
            P(),
            P("group", None),
            P("group", None),
            P("group", "tensor", None),
            P("group", None, "tensor"),
            P("group", "tensor", None),
            P("group", None, "tensor"),
        ),
        out_specs=(P("group", "tensor"), P("group", None)),
        check_vma=False,
    )
```

```python
import functools
import math

import jax
import jax.numpy as jnp
from jax import lax
from jax.experimental import pallas as pl
from jax.experimental.pallas import tpu as pltpu
from jax.sharding import PartitionSpec as P

ADAPTER_SCALE = 0.5
LANES = 128
LEVELS = 8
STEPS = 32767.0
VMEM_BYTES = 48 * 1024 * 1024
ANY = pl.BlockSpec(memory_space=pl.ANY)
SMEM = pl.BlockSpec(memory_space=pltpu.SMEM)
VMEM = pl.BlockSpec(memory_space=pltpu.VMEM)


def params():
    return pltpu.CompilerParams(vmem_limit_bytes=VMEM_BYTES)


def cost(flops, nbytes):
    return pl.CostEstimate(flops=flops // 1000, bytes_accessed=nbytes // 1000, transcendentals=0)


def send(value, axis, offset):
    size = lax.axis_size(axis)
    return lax.ppermute(value, axis, [(i, i ^ offset) for i in range(size)])


def after(value, *others):
    return lax.optimization_barrier((value, *others))[0]


def at(values, *numbers):
    return [values[number] for number in numbers if number < len(values)]


class Chain:
    def __init__(self, axis):
        self.axis = axis
        self.done = []

    def send(self, value, offset, *pins):
        pins = (*self.done[-1:], *pins)
        if pins:
            value = after(value, *pins)
        arrived = send(value, self.axis, offset)
        self.done.append(arrived)
        return arrived


class Groups:
    def __init__(self, axis, ends):
        self.axis = axis
        self.ends = ends
        self.done = []

    def upto(self, step):
        start = self.ends[step - 1] if step else 0
        return self.done[start : self.ends[step]]

    def send(self, value, offset):
        number = len(self.done)
        step = sum(end <= number for end in self.ends)
        if step:
            value = after(value, *self.upto(step - 1))
        arrived = send(value, self.axis, offset)
        self.done.append(arrived)
        return arrived


def bits(size):
    out = []
    bit = 1
    while bit < size:
        out.append(bit)
        bit *= 2
    return out


def pack_kernel(plan, table_ref, adapters_ref, *refs):
    stores = refs[:2]
    outs = refs[-3 - len(plan) : -3]
    staged, in_sems, out_sems = refs[-3:]
    groups, slots = adapters_ref.shape
    held, rank, _ = stores[0].shape
    me = lax.axis_index("group")
    loads = []
    for dist in range(groups):
        dest = me ^ dist
        pick = jnp.int32(0)
        for slot in range(slots):
            place = table_ref[adapters_ref[dest, slot]]
            owner = lax.div(place, jnp.int32(held))
            pick = jnp.where(owner == me, place - owner * held, pick)
        for part in range(2):
            load = pltpu.make_async_copy(stores[part].at[pick], staged.at[dist, part], in_sems.at[dist, part])
            load.start()
            loads.append(load)
    for load in loads:
        load.wait()
    copies = []
    for number, (dist, parts) in enumerate(plan):
        for place, part in enumerate(parts):
            copy = pltpu.make_async_copy(
                staged.at[dist, part], outs[number].at[pl.ds(place * rank, rank)], out_sems.at[dist, part]
            )
            copy.start()
            copies.append(copy)
    for copy in copies:
        copy.wait()


def pack(plan, table, adapters, stores, order=()):
    groups = adapters.shape[0]
    held, rank, width = stores[0].shape
    dtype = stores[0].dtype
    moved = 8 * groups * rank * width
    return pl.pallas_call(
        functools.partial(pack_kernel, plan),
        out_shape=[jax.ShapeDtypeStruct((len(parts) * rank, width), dtype) for _, parts in plan],
        in_specs=[SMEM, SMEM] + [ANY] * (2 + len(order)),
        out_specs=[ANY] * len(plan),
        scratch_shapes=[
            pltpu.VMEM((groups, 2, rank, width), dtype),
            pltpu.SemaphoreType.DMA((groups, 2)),
            pltpu.SemaphoreType.DMA((groups, 2)),
        ],
        compiler_params=params(),
        cost_estimate=cost(0, moved),
    )(table, adapters, *stores, *order)


def row_distance(table_ref, adapters_ref, slot_ref, len_ref, held, shape):
    me = lax.axis_index("group")
    position = lax.broadcasted_iota(jnp.int32, shape, 0)
    found = jnp.zeros(shape, jnp.int32)
    start = jnp.int32(0)
    for req in range(len_ref.shape[1]):
        place = table_ref[adapters_ref[me, slot_ref[0, req]]]
        dist = lax.div(place, jnp.int32(held)) ^ me
        end = start + len_ref[0, req]
        found = jnp.where((position >= start) & (position < end), dist, found)
        start = end
    return found


def down_kernel(held, rank, places, table_ref, adapters_ref, slot_ref, len_ref, rows_ref, *refs):
    groups = len(places)
    pieces = refs[:groups]
    out_ref, whole, sems = refs[groups:]
    copies = []
    for dist in range(groups):
        copy = pltpu.make_async_copy(
            pieces[dist].at[pl.ds(places[dist] * rank, rank)], whole.at[pl.ds(dist * rank, rank)], sems.at[dist]
        )
        copy.start()
        copies.append(copy)
    shape = (rows_ref.shape[0], 2 * rank)
    found = row_distance(table_ref, adapters_ref, slot_ref, len_ref, held, shape)
    high = (lax.broadcasted_iota(jnp.int32, shape, 1) >= rank).astype(jnp.int32)
    for copy in copies:
        copy.wait()
    full = lax.dot_general(
        rows_ref[...], whole[...], (((1,), (1,)), ((), ())), preferred_element_type=jnp.float32
    )
    picked = jnp.zeros(shape, jnp.float32)
    for pair in range(groups // 2):
        piece = full[:, pair * 2 * rank : (pair + 1) * 2 * rank]
        picked = picked + jnp.where(found == 2 * pair + high, piece, 0.0)
    out_ref[...] = picked + pltpu.roll(picked, rank, 1)


def down(routing, held, rank, rows_in, pieces):
    rows, width = rows_in.shape
    groups = len(pieces)
    return pl.pallas_call(
        functools.partial(down_kernel, held, rank, [place for _, place in pieces]),
        out_shape=jax.ShapeDtypeStruct((rows, 2 * rank), jnp.float32),
        in_specs=[SMEM] * 4 + [VMEM] + [ANY] * groups,
        out_specs=VMEM,
        scratch_shapes=[
            pltpu.VMEM((groups * rank, width), rows_in.dtype),
            pltpu.SemaphoreType.DMA((groups,)),
        ],
        compiler_params=params(),
        cost_estimate=cost(2 * rows * width * groups * rank, 2 * rows * width + 2 * groups * rank * width),
    )(*routing, rows_in, *[piece for piece, _ in pieces])


def up_kernel(held, dists, split, table_ref, adapters_ref, slot_ref, len_ref, down_ref, *refs):
    groups = len(dists)
    pieces = refs[:groups]
    bases = refs[groups : groups + split]
    outs = refs[groups + split : groups + 2 * split]
    terms = refs[-1]
    rank = pieces[0].shape[0]
    rows = down_ref.shape[0]

    @pl.when(pl.program_id(0) == 0)
    def _():
        shape = (rows, 2 * rank)
        found = row_distance(table_ref, adapters_ref, slot_ref, len_ref, held, shape)
        low = lax.broadcasted_iota(jnp.int32, shape, 1) < rank
        both = down_ref[...] * ADAPTER_SCALE
        first = both.astype(jnp.bfloat16)
        rest = both - first.astype(jnp.float32)
        second = rest.astype(jnp.bfloat16)
        third = (rest - second.astype(jnp.float32)).astype(jnp.bfloat16)
        for number, term in enumerate((first, second, third)):
            for pair in range(groups // 2):
                wanted = jnp.where(low, dists[2 * pair], dists[2 * pair + 1])
                chosen = jnp.where(found == wanted, term.astype(jnp.float32), 0.0)
                terms[number, :, pair * 2 * rank : (pair + 1) * 2 * rank] = chosen.astype(jnp.bfloat16)

    whole = jnp.concatenate([piece[...] for piece in pieces], axis=0)
    total = jnp.dot(terms[2], whole, preferred_element_type=jnp.float32)
    total = total + jnp.dot(terms[1], whole, preferred_element_type=jnp.float32)
    total = total + jnp.dot(terms[0], whole, preferred_element_type=jnp.float32)
    size = rows // split
    for number in range(split):
        value = bases[number][...] + total[number * size : (number + 1) * size]
        outs[number][...] = value.astype(outs[number].dtype)


def up(routing, held, rank, downs, used, dists, bases, out_dtype):
    pieces = [used[dist] for dist in dists]
    groups = len(dists)
    width = pieces[0][0].shape[1]
    rows = downs.shape[0]
    split = len(bases)
    tile = min(512, width)
    column = lambda step: (0, step)
    size = rows // split
    piece_specs = [
        pl.BlockSpec((rank, tile), functools.partial(lambda place, step: (place, step), place)) for _, place in pieces
    ]
    return pl.pallas_call(
        functools.partial(up_kernel, held, dists, split),
        grid=(width // tile,),
        out_shape=[jax.ShapeDtypeStruct((size, width), out_dtype)] * split,
        in_specs=[SMEM] * 4
        + [pl.BlockSpec(downs.shape, lambda step: (0, 0))]
        + piece_specs
        + [pl.BlockSpec((size, tile), column)] * split,
        out_specs=[pl.BlockSpec((size, tile), column)] * split,
        scratch_shapes=[pltpu.VMEM((3, rows, groups * rank), jnp.bfloat16)],
        compiler_params=params(),
        cost_estimate=cost(6 * rows * width * groups * rank, 8 * rows * width + 2 * groups * rank * width),
    )(*routing, downs, *[piece for piece, _ in pieces], *bases)


def tile_of(width):
    return min(512, width)


def encode(value, out_ref, step):
    half, tile = value.shape
    width = out_ref.shape[1] - LANES
    peak = jnp.max(jnp.abs(value), axis=1, keepdims=True)
    level = jnp.ceil(jnp.log(jnp.maximum(peak, 1e-30)) * (LEVELS / math.log(2.0)))
    coded = jnp.round(value * (jnp.exp2(level * (-1.0 / LEVELS)) * STEPS))
    coded = jnp.minimum(jnp.maximum(coded, -STEPS), STEPS)
    start = step * tile if isinstance(step, int) else pl.multiple_of(step * tile, tile)
    out_ref[:, pl.ds(start, tile)] = coded.astype(jnp.int32).astype(jnp.int16)
    lane = lax.broadcasted_iota(jnp.int32, (half, LANES), 1)
    kept = jnp.where(lane < step, out_ref[:, width:].astype(jnp.int32), 0)
    out_ref[:, width:] = jnp.where(lane == step, level.astype(jnp.int32), kept).astype(jnp.int16)


def decode(coded_ref, step, tile):
    width = coded_ref.shape[1] - LANES
    levels = coded_ref[:, width:].astype(jnp.int32)
    lane = lax.broadcasted_iota(jnp.int32, levels.shape, 1)
    level = jnp.sum(jnp.where(lane == step, levels, 0).astype(jnp.float32), axis=1, keepdims=True)
    value = coded_ref[:, step * tile : (step + 1) * tile].astype(jnp.int32).astype(jnp.float32)
    return value * (jnp.exp2(level * (1.0 / LEVELS)) * (1.0 / STEPS))


def merge_kernel(counts, coded_out, *refs):
    out_ref = refs[-1]
    inputs = refs[:-1]
    for number, count in enumerate(counts):
        base, coded = inputs[0], inputs[1 : 1 + count]
        inputs = inputs[1 + count :]
        half, width = base.shape
        tile = tile_of(width)
        for step in range(width // tile):
            columns = slice(step * tile, (step + 1) * tile)
            total = base[:, columns]
            for one in coded:
                total = total + decode(one, step, tile)
            if coded_out:
                encode(total, out_ref, step)
            else:
                out_ref[number * half : (number + 1) * half, columns] = total.astype(out_ref.dtype)


def merge(sums, coded_out):
    half, width = sums[0][0].shape
    counts = [len(coded) for _, coded in sums]
    if coded_out:
        out_shape = jax.ShapeDtypeStruct((half, width + LANES), jnp.int16)
    else:
        out_shape = jax.ShapeDtypeStruct((len(sums) * half, width), jnp.bfloat16)
    values = [value for base, coded in sums for value in (base, *coded)]
    return pl.pallas_call(
        functools.partial(merge_kernel, counts, coded_out),
        out_shape=out_shape,
        in_specs=[VMEM] * len(values),
        out_specs=VMEM,
        compiler_params=params(),
        cost_estimate=cost(0, 2 * sum(value.size for value in values) + 4 * half * width),
    )(*values)


def o_kernel(block_ref, rows_ref, weight_ref, *outs):
    del block_ref
    total = jnp.dot(rows_ref[...], weight_ref[...], preferred_element_type=jnp.float32)
    half = outs[0].shape[0]
    for number, out_ref in enumerate(outs):
        value = total[number * half : (number + 1) * half]
        if out_ref.dtype == jnp.int16:
            encode(value, out_ref, pl.program_id(0))
        else:
            out_ref[...] = value


def o_block(block, rows_in, weight, width, coded):
    rows, depth = rows_in.shape
    half = rows // 2
    tile = tile_of(width)
    tiles = width // tile
    shapes, specs = [], []
    for one in coded:
        if one:
            shapes.append(jax.ShapeDtypeStruct((half, width + LANES), jnp.int16))
            specs.append(pl.BlockSpec((half, width + LANES), lambda step, ref: (0, 0)))
        else:
            shapes.append(jax.ShapeDtypeStruct((half, width), jnp.float32))
            specs.append(pl.BlockSpec((half, tile), lambda step, ref: (0, step)))
    return pl.pallas_call(
        o_kernel,
        grid_spec=pltpu.PrefetchScalarGridSpec(
            num_scalar_prefetch=1,
            grid=(tiles,),
            in_specs=[
                pl.BlockSpec((rows, depth), lambda step, ref: (0, 0)),
                pl.BlockSpec((depth, tile), lambda step, ref: (0, ref[0] * tiles + step)),
            ],
            out_specs=specs,
        ),
        out_shape=shapes,
        compiler_params=params(),
        cost_estimate=cost(2 * rows * depth * width, 2 * depth * width + 2 * rows * depth + 4 * rows * width),
    )(block, rows_in, weight)


def q_kernel(count, has_total, block_ref, *refs):
    del block_ref
    pieces = refs[:count]
    weight_ref = refs[count]
    out_ref = refs[-1]
    size = pieces[0].shape[0]
    for number, rows_ref in enumerate(pieces):
        total = jnp.dot(rows_ref[...], weight_ref[...], preferred_element_type=jnp.float32)
        span = slice(number * size, (number + 1) * size)
        if has_total:
            total = total + refs[count + 1][span]
        out_ref[span] = total


def q_block(block, pieces, weight, total):
    count = len(pieces)
    size, depth = pieces[0].shape
    rows = count * size
    width = weight.shape[1]
    tile = tile_of(width)
    has_total = total is not None
    column = pl.BlockSpec((rows, tile), lambda step, ref: (0, step))
    return pl.pallas_call(
        functools.partial(q_kernel, count, has_total),
        grid_spec=pltpu.PrefetchScalarGridSpec(
            num_scalar_prefetch=1,
            grid=(width // tile,),
            in_specs=[pl.BlockSpec((size, depth), lambda step, ref: (0, 0))] * count
            + [pl.BlockSpec((depth, tile), lambda step, ref: (ref[0], step))]
            + [column] * has_total,
            out_specs=column,
        ),
        out_shape=jax.ShapeDtypeStruct((rows, width), jnp.float32),
        input_output_aliases={count + 2: 0} if has_total else {},
        compiler_params=params(),
        cost_estimate=cost(2 * rows * depth * width, 2 * depth * width + 2 * rows * depth + 8 * rows * width),
    )(block, *pieces, weight, *([total] * has_total))


def share(block, chains, *pins):
    whole = {0: block}
    for bit in chains:
        whole[bit] = chains[bit].send(block, bit, *pins)
    return whole


def forward(whole, chains, *pins):
    order = list(chains)
    half = whole[0].shape[0] // 2
    parts = [{}, {}]
    for step in range(len(order)):
        for number in range(2):
            bits_used = order if number == 0 else order[::-1]
            bit = bits_used[step]
            held = [0]
            for used in bits_used[:step]:
                held = held + [dist ^ used for dist in held]
            for dist in held[1:]:
                if dist in whole:
                    piece = whole[dist][number * half : (number + 1) * half]
                else:
                    piece = parts[number][dist]
                parts[number][dist ^ bit] = chains[bit].send(piece, bit, *pins)
    pieces = {dist: [value] for dist, value in whole.items()}
    for dist in parts[0]:
        pieces[dist] = [parts[0][dist], parts[1][dist]]
    return pieces


def place_kernel(blocks, column_ref, *refs):
    out_ref, sems = refs[-2:]
    width = refs[0].shape[1]
    copies = []
    number = 0
    for block, count in enumerate(blocks):
        start = pl.multiple_of(column_ref[block] * width, width)
        for part in range(count):
            size = refs[number].shape[0]
            copy = pltpu.make_async_copy(
                refs[number], out_ref.at[pl.ds(part * size, size), pl.ds(start, width)], sems.at[number]
            )
            copy.start()
            copies.append(copy)
            number += 1
    for copy in copies:
        copy.wait()


def place(columns, blocks, into, out_shape):
    counts = [len(pieces) for pieces in blocks]
    pieces = [piece for block in blocks for piece in block]
    old = [] if into is None else [into]
    return pl.pallas_call(
        functools.partial(place_kernel, counts),
        out_shape=out_shape,
        in_specs=[SMEM] + [VMEM] * len(pieces) + [ANY] * len(old),
        out_specs=ANY,
        scratch_shapes=[pltpu.SemaphoreType.DMA((len(pieces),))],
        input_output_aliases={len(pieces) + 1: 0} if old else {},
        compiler_params=params(),
        cost_estimate=cost(0, 4 * sum(piece.size for piece in pieces)),
    )(columns, *pieces, *old)


def body(
    hidden_rows,
    attn_rows,
    q_weight,
    o_weight,
    owner_table,
    group_adapters,
    req_slot,
    req_len,
    qa_store,
    qb_store,
    oa_store,
    ob_store,
):
    groups = lax.axis_size("group")
    size = lax.axis_size("tensor")
    mine = lax.axis_index("tensor")
    held, _, rank = qa_store.shape
    rows, _ = hidden_rows.shape
    width = o_weight.shape[1] // size
    routing = (owner_table, group_adapters, req_slot, req_len)
    block = [jnp.reshape(mine ^ dist, (1,)).astype(jnp.int32) for dist in range(size)]
    order = bits(size)

    far = Groups("group", [groups // 2 * 4 * part // 16 for part in (3, 5, 7, 9, 11, 14, 16)])
    near = Chain("group")
    chains = {bit: Chain("tensor") for bit in order}
    far_dists = list(range(groups // 2, groups))
    near_dists = list(range(groups // 2 - 1, 0, -1))
    all_dists = list(range(groups))
    plan = [(dist, (part,)) for part in range(2) for dist in far_dists]
    plan = plan + [(dist, (0, 1)) for dist in near_dists + [0]]

    def packed(down_store, up_store, *pins):
        return pack(plan, owner_table, group_adapters, (jnp.swapaxes(down_store, 1, 2), up_store), pins)

    def fetch_near(values, used, pins):
        for part in range(2):
            used[part][0] = (values[-1], part)
        for number, (value, dist) in enumerate(zip(values[2 * len(far_dists) :], near_dists)):
            arrived = near.send(value, dist, *(pins if number == 0 else ()))
            for part in range(2):
                used[part][dist] = (arrived, part)

    def fetch_far(values, used, part):
        for number, dist in enumerate(far_dists):
            value = values[part * len(far_dists) + number]
            used[part][dist] = (far.send(value, dist), 0)

    def summed(value):
        for bit in order:
            value = value + send(value, "tensor", bit)
        return value

    halving = (order, order[::-1])
    sums = [{}, {}]

    def reduce_step(step, first, *pins):
        for number in range(2):
            bit = halving[number][step]
            dists = sorted((one for one in sums[number] if one & bit), reverse=True)
            for dist in dists[:1] if first else dists:
                base, coded = sums[number].pop(dist)
                value = base if step == 0 else merge([(base, coded)], True)
                arrived = chains[bit].send(value, bit, *pins)
                sums[number][dist ^ bit][1].append(arrived)

    hidden = share(hidden_rows, chains)
    values = packed(oa_store, ob_store)
    o_used = [{}, {}]
    fetch_far(values, o_used, 0)
    fetch_far(values, o_used, 1)
    fetch_near(values, o_used, far.upto(0))

    ready = []
    for dist in sorted(range(size), reverse=True):
        coded = [bool(dist & bit_order[0]) for bit_order in halving]
        for number, value in enumerate(o_block(block[dist], attn_rows, o_weight, width, coded)):
            sums[number][dist] = (value, [])
        ready.append(value)
    hidden = forward(hidden, chains, *far.upto(0), *ready)

    totals = []
    for dist in range(size):
        totals.append(q_block(block[dist], hidden[dist], q_weight, totals[-1] if totals else None))
    values = packed(qa_store, qb_store, *far.upto(0))
    q_used = [{}, {}]
    seen = len(near.done)
    fetch_far(values, q_used, 0)
    fetch_far(values, q_used, 1)
    fetch_near(values, q_used, far.upto(2))

    reduce_step(0, True, *far.upto(1), near.done[0], *totals[:1])
    reduce_step(0, False, *far.upto(2), *near.done[:seen], *totals[1:2])
    o_half = down(routing, held, rank, attn_rows, [o_used[0][dist] for dist in all_dists])
    for step in range(1, len(order)):
        reduce_step(step, False, *far.upto(3), *near.done[seen : seen + 1], o_half, *totals[2:3])
    o_down = summed(o_half)
    bases = up(routing, held, rank, o_down, o_used[1], all_dists, [one[0][0] for one in sums], jnp.float32)
    rounded = merge([(base, one[0][1]) for base, one in zip(bases, sums)], False)
    finished = share(rounded, chains, *far.upto(4), *near.done[seen:], totals[-1])
    q_half = down(routing, held, rank, hidden_rows, [q_used[0][dist] for dist in all_dists])
    q_down = summed(q_half)
    finished = forward(finished, chains, *far.upto(5))

    last = far_dists[-2:]
    first = [dist for dist in all_dists if dist not in last]
    (total,) = up(routing, held, rank, q_down, q_used[1], first, [totals[-1]], jnp.float32)
    (queries,) = up(routing, held, rank, q_down, q_used[1], last, [total], jnp.bfloat16)

    out_shape = jax.ShapeDtypeStruct((rows, width * size), jnp.bfloat16)
    early = [dist for dist in range(size) if len(finished[dist]) == 1]
    late = [dist for dist in range(size) if len(finished[dist]) > 1]
    attn_out = None
    for some in (early, late):
        columns = jnp.concatenate([block[dist] for dist in some])
        attn_out = place(columns, [finished[dist] for dist in some], attn_out, out_shape)
    return (queries, attn_out)


def solution(mesh):
    return jax.shard_map(
        body,
        mesh=mesh,
        in_specs=(
            P("group", "tensor"),
            P("group", "tensor"),
            P(None, "tensor"),
            P("tensor", None),
            P(),
            P(),
            P("group", None),
            P("group", None),
            P("group", "tensor", None),
            P("group", None, "tensor"),
            P("group", "tensor", None),
            P("group", None, "tensor"),
        ),
        out_specs=(P("group", "tensor"), P("group", None)),
        check_vma=False,
    )
```

```python
import functools
import math

import jax
import jax.numpy as jnp
from jax import lax
from jax.experimental import pallas as pl
from jax.experimental.pallas import tpu as pltpu
from jax.sharding import PartitionSpec as P

ADAPTER_SCALE = 0.5
LANES = 128
LEVELS = 8
STEPS = 32767.0
MIB = 1024 * 1024
ANY = pl.BlockSpec(memory_space=pl.ANY)
SMEM = pl.BlockSpec(memory_space=pltpu.SMEM)
VMEM = pl.BlockSpec(memory_space=pltpu.VMEM)
HBM = pl.BlockSpec(memory_space=pltpu.HBM)


def params(mebibytes):
    return pltpu.CompilerParams(vmem_limit_bytes=mebibytes * MIB)


def cost(flops, nbytes):
    return pl.CostEstimate(flops=flops // 1000, bytes_accessed=nbytes // 1000, transcendentals=0)


def send(value, axis, offset):
    size = lax.axis_size(axis)
    return lax.ppermute(value, axis, [(i, i ^ offset) for i in range(size)])


def after(value, *others):
    return lax.optimization_barrier((value, *others))[0]


def at(values, *numbers):
    return [values[number] for number in numbers if number < len(values)]


class Chain:
    def __init__(self, axis):
        self.axis = axis
        self.done = []

    def send(self, value, offset, *pins):
        pins = (*self.done[-1:], *pins)
        if pins:
            value = after(value, *pins)
        arrived = send(value, self.axis, offset)
        self.done.append(arrived)
        return arrived


class Groups:
    def __init__(self, axis, ends):
        self.axis = axis
        self.ends = ends
        self.done = []

    def upto(self, step):
        start = self.ends[step - 1] if step else 0
        return self.done[start : self.ends[step]]

    def send(self, value, offset):
        number = len(self.done)
        step = sum(end <= number for end in self.ends)
        if step:
            value = after(value, *self.upto(step - 1))
        arrived = send(value, self.axis, offset)
        self.done.append(arrived)
        return arrived


def bits(size):
    out = []
    bit = 1
    while bit < size:
        out.append(bit)
        bit *= 2
    return out


def pack_kernel(plan, table_ref, adapters_ref, *refs):
    stores = refs[:2]
    outs = refs[-3 - len(plan) : -3]
    staged, in_sems, out_sems = refs[-3:]
    slots = adapters_ref.shape[1]
    held, rank, _ = stores[0].shape
    me = lax.axis_index("group")
    loads = []
    for dist, parts in plan:
        dest = me ^ dist
        pick = jnp.int32(0)
        for slot in range(slots):
            place = table_ref[adapters_ref[dest, slot]]
            owner = lax.div(place, jnp.int32(held))
            pick = jnp.where(owner == me, place - owner * held, pick)
        for part in parts:
            load = pltpu.make_async_copy(stores[part].at[pick], staged.at[dist, part], in_sems.at[dist, part])
            load.start()
            loads.append(load)
    copies = []
    for number, (dist, parts) in enumerate(plan):
        for row, part in enumerate(parts):
            loads[len(copies)].wait()
            copy = pltpu.make_async_copy(
                staged.at[dist, part], outs[number].at[pl.ds(row * rank, rank)], out_sems.at[dist, part]
            )
            copy.start()
            copies.append(copy)
    for copy in copies:
        copy.wait()


def pack(plan, table, adapters, stores, order=()):
    groups = adapters.shape[0]
    _, rank, width = stores[0].shape
    dtype = stores[0].dtype
    return pl.pallas_call(
        functools.partial(pack_kernel, plan),
        out_shape=[pltpu.HBM((len(parts) * rank, width), dtype) for _, parts in plan],
        in_specs=[SMEM, SMEM] + [ANY] * (2 + len(order)),
        out_specs=[HBM] * len(plan),
        scratch_shapes=[
            pltpu.VMEM((groups, 2, rank, width), dtype),
            pltpu.SemaphoreType.DMA((groups, 2)),
            pltpu.SemaphoreType.DMA((groups, 2)),
        ],
        compiler_params=params(8),
        cost_estimate=cost(0, 8 * groups * rank * width),
    )(table, adapters, *stores, *order)


def distance_kernel(held, table_ref, adapters_ref, slot_ref, len_ref, out_ref):
    me = lax.axis_index("group")
    position = lax.broadcasted_iota(jnp.int32, out_ref.shape, 0)
    found = jnp.zeros(out_ref.shape, jnp.int32)
    start = jnp.int32(0)
    for req in range(len_ref.shape[1]):
        place = table_ref[adapters_ref[me, slot_ref[0, req]]]
        dist = lax.div(place, jnp.int32(held)) ^ me
        end = start + len_ref[0, req]
        found = jnp.where((position >= start) & (position < end), dist, found)
        start = end
    out_ref[...] = found


def row_distances(routing, held, rows, lanes):
    return pl.pallas_call(
        functools.partial(distance_kernel, held),
        out_shape=jax.ShapeDtypeStruct((rows, lanes), jnp.int32),
        in_specs=[SMEM] * 4,
        out_specs=VMEM,
        compiler_params=params(4),
        cost_estimate=cost(0, 4 * rows * lanes),
    )(*routing)


def down_kernel(rank, places, found_ref, rows_ref, *refs):
    groups = len(places)
    pieces = refs[:groups]
    out_ref, whole, sems = refs[groups:]
    copies = []
    for dist in range(groups):
        copy = pltpu.make_async_copy(
            pieces[dist].at[pl.ds(places[dist] * rank, rank)], whole.at[pl.ds(dist * rank, rank)], sems.at[dist]
        )
        copy.start()
        copies.append(copy)
    shape = (rows_ref.shape[0], 2 * rank)
    found = found_ref[...]
    high = (lax.broadcasted_iota(jnp.int32, shape, 1) >= rank).astype(jnp.int32)
    for copy in copies:
        copy.wait()
    full = lax.dot_general(
        rows_ref[...], whole[...], (((1,), (1,)), ((), ())), preferred_element_type=jnp.float32
    )
    picked = jnp.zeros(shape, jnp.float32)
    for pair in range(groups // 2):
        piece = full[:, pair * 2 * rank : (pair + 1) * 2 * rank]
        picked = picked + jnp.where(found == 2 * pair + high, piece, 0.0)
    out_ref[...] = picked + pltpu.roll(picked, rank, 1)


def down(found, rank, rows_in, pieces):
    rows, width = rows_in.shape
    groups = len(pieces)
    return pl.pallas_call(
        functools.partial(down_kernel, rank, [row for _, row in pieces]),
        out_shape=jax.ShapeDtypeStruct((rows, 2 * rank), jnp.float32),
        in_specs=[VMEM] * 2 + [ANY] * groups,
        out_specs=VMEM,
        scratch_shapes=[
            pltpu.VMEM((groups * rank, width), rows_in.dtype),
            pltpu.SemaphoreType.DMA((groups,)),
        ],
        compiler_params=params(12),
        cost_estimate=cost(2 * rows * width * groups * rank, 2 * rows * width + 2 * groups * rank * width),
    )(found, rows_in, *[piece for piece, _ in pieces])


def up_kernel(dists, split, found_ref, down_ref, *refs):
    groups = len(dists)
    pieces = refs[:groups]
    bases = refs[groups : groups + split]
    outs = refs[groups + split : groups + 2 * split]
    terms = refs[-1]
    rank = pieces[0].shape[0]
    rows = down_ref.shape[0]

    @pl.when(pl.program_id(0) == 0)
    def _():
        shape = (rows, 2 * rank)
        found = found_ref[...]
        low = lax.broadcasted_iota(jnp.int32, shape, 1) < rank
        both = down_ref[...] * ADAPTER_SCALE
        first = both.astype(jnp.bfloat16)
        rest = both - first.astype(jnp.float32)
        second = rest.astype(jnp.bfloat16)
        third = (rest - second.astype(jnp.float32)).astype(jnp.bfloat16)
        for number, term in enumerate((first, second, third)):
            for pair in range(groups // 2):
                wanted = jnp.where(low, dists[2 * pair], dists[2 * pair + 1])
                chosen = jnp.where(found == wanted, term.astype(jnp.float32), 0.0)
                terms[number, :, pair * 2 * rank : (pair + 1) * 2 * rank] = chosen.astype(jnp.bfloat16)

    whole = jnp.concatenate([piece[...] for piece in pieces], axis=0)
    total = jnp.dot(terms[2], whole, preferred_element_type=jnp.float32)
    total = total + jnp.dot(terms[1], whole, preferred_element_type=jnp.float32)
    total = total + jnp.dot(terms[0], whole, preferred_element_type=jnp.float32)
    size = rows // split
    for number in range(split):
        value = bases[number][...] + total[number * size : (number + 1) * size]
        outs[number][...] = value.astype(outs[number].dtype)


def up(found, rank, downs, used, dists, bases, out_dtype):
    pieces = [used[dist] for dist in dists]
    groups = len(dists)
    width = pieces[0][0].shape[1]
    rows = downs.shape[0]
    split = len(bases)
    tile = min(512, width)
    column = lambda step: (0, step)
    size = rows // split
    piece_specs = [
        pl.BlockSpec((rank, tile), functools.partial(lambda place, step: (place, step), place)) for _, place in pieces
    ]
    return pl.pallas_call(
        functools.partial(up_kernel, dists, split),
        grid=(width // tile,),
        out_shape=[jax.ShapeDtypeStruct((size, width), out_dtype)] * split,
        in_specs=[pl.BlockSpec(downs.shape, lambda step: (0, 0))] * 2
        + piece_specs
        + [pl.BlockSpec((size, tile), column)] * split,
        out_specs=[pl.BlockSpec((size, tile), column)] * split,
        scratch_shapes=[pltpu.VMEM((3, rows, groups * rank), jnp.bfloat16)],
        compiler_params=params(16),
        cost_estimate=cost(6 * rows * width * groups * rank, 8 * rows * width + 2 * groups * rank * width),
    )(found, downs, *[piece for piece, _ in pieces], *bases)


def tile_of(width):
    return min(512, width)


def encode(value, out_ref, step):
    half, tile = value.shape
    width = out_ref.shape[1] - LANES
    peak = jnp.max(jnp.abs(value), axis=1, keepdims=True)
    level = jnp.ceil(jnp.log(jnp.maximum(peak, 1e-30)) * (LEVELS / math.log(2.0)))
    coded = jnp.round(value * (jnp.exp2(level * (-1.0 / LEVELS)) * STEPS))
    coded = jnp.minimum(jnp.maximum(coded, -STEPS), STEPS)
    start = step * tile if isinstance(step, int) else pl.multiple_of(step * tile, tile)
    out_ref[:, pl.ds(start, tile)] = coded.astype(jnp.int32).astype(jnp.int16)
    lane = lax.broadcasted_iota(jnp.int32, (half, LANES), 1)
    kept = jnp.where(lane < step, out_ref[:, width:].astype(jnp.int32), 0)
    out_ref[:, width:] = jnp.where(lane == step, level.astype(jnp.int32), kept).astype(jnp.int16)


def decode(coded_ref, step, tile):
    width = coded_ref.shape[1] - LANES
    levels = coded_ref[:, width:].astype(jnp.int32)
    lane = lax.broadcasted_iota(jnp.int32, levels.shape, 1)
    level = jnp.sum(jnp.where(lane == step, levels, 0).astype(jnp.float32), axis=1, keepdims=True)
    value = coded_ref[:, step * tile : (step + 1) * tile].astype(jnp.int32).astype(jnp.float32)
    return value * (jnp.exp2(level * (1.0 / LEVELS)) * (1.0 / STEPS))


def merge_kernel(counts, coded_out, *refs):
    out_ref = refs[-1]
    inputs = refs[:-1]
    for number, count in enumerate(counts):
        base, coded = inputs[0], inputs[1 : 1 + count]
        inputs = inputs[1 + count :]
        half, width = base.shape
        tile = tile_of(width)
        for step in range(width // tile):
            columns = slice(step * tile, (step + 1) * tile)
            total = base[:, columns]
            for one in coded:
                total = total + decode(one, step, tile)
            if coded_out:
                encode(total, out_ref, step)
            else:
                out_ref[number * half : (number + 1) * half, columns] = total.astype(out_ref.dtype)


def merge(sums, coded_out, dtype=jnp.bfloat16):
    half, width = sums[0][0].shape
    counts = [len(coded) for _, coded in sums]
    if coded_out:
        out_shape = jax.ShapeDtypeStruct((half, width + LANES), jnp.int16)
    else:
        out_shape = jax.ShapeDtypeStruct((len(sums) * half, width), dtype)
    values = [value for base, coded in sums for value in (base, *coded)]
    return pl.pallas_call(
        functools.partial(merge_kernel, counts, coded_out),
        out_shape=out_shape,
        in_specs=[VMEM] * len(values),
        out_specs=VMEM,
        compiler_params=params(16),
        cost_estimate=cost(0, 2 * sum(value.size for value in values) + 4 * half * width),
    )(*values)


def o_kernel(block_ref, rows_ref, weight_ref, *outs):
    del block_ref
    total = jnp.dot(rows_ref[...], weight_ref[...], preferred_element_type=jnp.float32)
    half = outs[0].shape[0]
    for number, out_ref in enumerate(outs):
        value = total[number * half : (number + 1) * half]
        if out_ref.dtype == jnp.int16:
            encode(value, out_ref, pl.program_id(0))
        else:
            out_ref[...] = value


def o_block(block, rows_in, weight, width, coded):
    rows, depth = rows_in.shape
    half = rows // 2
    tile = tile_of(width)
    tiles = width // tile
    shapes, specs = [], []
    for one in coded:
        if one:
            shapes.append(jax.ShapeDtypeStruct((half, width + LANES), jnp.int16))
            specs.append(pl.BlockSpec((half, width + LANES), lambda step, ref: (0, 0)))
        else:
            shapes.append(jax.ShapeDtypeStruct((half, width), jnp.float32))
            specs.append(pl.BlockSpec((half, tile), lambda step, ref: (0, step)))
    return pl.pallas_call(
        o_kernel,
        grid_spec=pltpu.PrefetchScalarGridSpec(
            num_scalar_prefetch=1,
            grid=(tiles,),
            in_specs=[
                pl.BlockSpec((rows, depth), lambda step, ref: (0, 0)),
                pl.BlockSpec((depth, tile), lambda step, ref: (0, ref[0] * tiles + step)),
            ],
            out_specs=specs,
        ),
        out_shape=shapes,
        compiler_params=params(36),
        cost_estimate=cost(2 * rows * depth * width, 2 * depth * width + 2 * rows * depth + 4 * rows * width),
    )(block, rows_in, weight)


def q_kernel(count, has_total, block_ref, *refs):
    del block_ref
    pieces = refs[:count]
    weight_ref = refs[count]
    out_ref, token_ref = refs[-2:]
    size = pieces[0].shape[0]
    token_ref[...] = jnp.zeros_like(token_ref)
    for number, rows_ref in enumerate(pieces):
        total = jnp.dot(rows_ref[...], weight_ref[...], preferred_element_type=jnp.float32)
        span = slice(number * size, (number + 1) * size)
        if has_total:
            total = total + refs[count + 1][span]
        out_ref[span] = total


def q_block(block, pieces, weight, total):
    count = len(pieces)
    size, depth = pieces[0].shape
    rows = count * size
    width = weight.shape[1]
    tile = tile_of(width)
    has_total = total is not None
    column = pl.BlockSpec((rows, tile), lambda step, ref: (0, step))
    return pl.pallas_call(
        functools.partial(q_kernel, count, has_total),
        grid_spec=pltpu.PrefetchScalarGridSpec(
            num_scalar_prefetch=1,
            grid=(width // tile,),
            in_specs=[pl.BlockSpec((size, depth), lambda step, ref: (0, 0))] * count
            + [pl.BlockSpec((depth, tile), lambda step, ref: (ref[0], step))]
            + [column] * has_total,
            out_specs=[column, pl.BlockSpec((8, LANES), lambda step, ref: (0, 0))],
        ),
        out_shape=[jax.ShapeDtypeStruct((rows, width), jnp.float32), jax.ShapeDtypeStruct((8, LANES), jnp.float32)],
        input_output_aliases={count + 2: 0} if has_total else {},
        compiler_params=params(36),
        cost_estimate=cost(2 * rows * depth * width, 2 * depth * width + 2 * rows * depth + 8 * rows * width),
    )(block, *pieces, weight, *([total] * has_total))


def share(block, chains, *pins):
    whole = {0: block}
    for bit in chains:
        whole[bit] = chains[bit].send(block, bit, *pins)
    return whole


def forward(whole, chains, *pins):
    order = list(chains)
    half = whole[0].shape[0] // 2
    parts = [{}, {}]
    for step in range(len(order)):
        for number in range(2):
            bits_used = order if number == 0 else order[::-1]
            bit = bits_used[step]
            held = [0]
            for used in bits_used[:step]:
                held = held + [dist ^ used for dist in held]
            for dist in held[1:]:
                if dist in whole:
                    piece = whole[dist][number * half : (number + 1) * half]
                else:
                    piece = parts[number][dist]
                parts[number][dist ^ bit] = chains[bit].send(piece, bit, *pins)
    pieces = {dist: [value] for dist, value in whole.items()}
    for dist in parts[0]:
        pieces[dist] = [parts[0][dist], parts[1][dist]]
    return pieces


def place_kernel(blocks, column_ref, *refs):
    out_ref, sems = refs[-2:]
    width = refs[0].shape[1]
    copies = []
    number = 0
    for block, count in enumerate(blocks):
        start = pl.multiple_of(column_ref[block] * width, width)
        for part in range(count):
            size = refs[number].shape[0]
            copy = pltpu.make_async_copy(
                refs[number], out_ref.at[pl.ds(part * size, size), pl.ds(start, width)], sems.at[number]
            )
            copy.start()
            copies.append(copy)
            number += 1
    for copy in copies:
        copy.wait()


def place(columns, blocks, into, out_shape):
    counts = [len(pieces) for pieces in blocks]
    pieces = [piece for block in blocks for piece in block]
    old = [] if into is None else [into]
    return pl.pallas_call(
        functools.partial(place_kernel, counts),
        out_shape=out_shape,
        in_specs=[SMEM] + [VMEM] * len(pieces) + [ANY] * len(old),
        out_specs=ANY,
        scratch_shapes=[pltpu.SemaphoreType.DMA((len(pieces),))],
        input_output_aliases={len(pieces) + 1: 0} if old else {},
        compiler_params=params(10),
        cost_estimate=cost(0, 4 * sum(piece.size for piece in pieces)),
    )(columns, *pieces, *old)


def body(
    hidden_rows,
    attn_rows,
    q_weight,
    o_weight,
    owner_table,
    group_adapters,
    req_slot,
    req_len,
    qa_store,
    qb_store,
    oa_store,
    ob_store,
):
    groups = lax.axis_size("group")
    size = lax.axis_size("tensor")
    mine = lax.axis_index("tensor")
    held, _, rank = qa_store.shape
    rows, _ = hidden_rows.shape
    width = o_weight.shape[1] // size
    routing = (owner_table, group_adapters, req_slot, req_len)
    block = [jnp.reshape(mine ^ dist, (1,)).astype(jnp.int32) for dist in range(size)]
    order = bits(size)

    far = Groups("group", [groups // 2 * 4 * part // 16 for part in (3, 5, 7, 9, 11, 14, 16)])
    near = Chain("group")
    chains = {bit: Chain("tensor") for bit in order}
    far_dists = list(range(groups // 2, groups))
    near_dists = [groups // 2 - 1, *range(1, groups // 2 - 1)]
    all_dists = list(range(groups))
    plan = [(dist, (part,)) for part in range(2) for dist in far_dists]
    plan = plan + [(dist, (0, 1)) for dist in near_dists + [0]]

    def packed(down_store, up_store, *pins):
        return pack(plan, owner_table, group_adapters, (jnp.swapaxes(down_store, 1, 2), up_store), pins)

    near = Chain("group")
    chains = {bit: Chain("tensor") for bit in order}
    far_dists = list(range(groups // 2, groups))
    near_dists = [groups // 2 - 1, *range(1, groups // 2 - 1)]
    all_dists = list(range(groups))
    plan = [(dist, (part,)) for part in range(2) for dist in far_dists]
    plan = plan + [(dist, (0, 1)) for dist in near_dists + [0]]

    def packed(down_store, up_store, *pins):
        return pack(plan, owner_table, group_adapters, (jnp.swapaxes(down_store, 1, 2), up_store), pins)

    def fetch_near(values, used, pins):
        for part in range(2):
            used[part][0] = (values[-1], part)
        for number, (value, dist) in enumerate(zip(values[2 * len(far_dists) :], near_dists)):
            arrived = near.send(value, dist, *pins[min(number, len(pins) - 1)])
            for part in range(2):
                used[part][dist] = (arrived, part)

    def fetch_far(values, used, part):
        for number, dist in enumerate(far_dists):
            value = values[part * len(far_dists) + number]
            used[part][dist] = (far.send(value, dist), 0)

    def exchange(value, *pins):
        if pins:
            value = after(value, *pins)
        return [send(value, "tensor", dist) for dist in range(1, size)]

    def pieces_of(used, dists):
        return [used[dist] for dist in dists]

    halving = (order, order[::-1])
    sums = [{}, {}]

    def reduce_step(step, first, *pins):
        for number in range(2):
            bit = halving[number][step]
            dists = sorted((one for one in sums[number] if one & bit), reverse=True)
            for dist in dists[:1] if first else dists:
                base, coded = sums[number].pop(dist)
                value = base if step == 0 else merge([(base, coded)], True)
                arrived = chains[bit].send(value, bit, *pins)
                sums[number][dist ^ bit][1].append(arrived)

    def o_sums(dist):
        coded = [bool(dist & bit_order[0]) for bit_order in halving]
        values = o_block(block[dist], attn_rows, o_weight, width, coded)
        for number, value in enumerate(values):
            sums[number][dist] = (value, [])
        return values[0]

    hidden = share(hidden_rows, chains)
    values = packed(oa_store, ob_store)
    o_used = [{}, {}]
    fetch_far(values, o_used, 0)
    fetch_far(values, o_used, 1)
    fetch_near(values, o_used, [far.upto(0), far.upto(1)])
    found = row_distances(routing, held, rows, 2 * rank)
    ready = [o_sums(dist) for dist in sorted(range(1, size), reverse=True)]

    hidden = forward(hidden, chains, *far.upto(0), *ready, found)
    ready = [o_sums(0)]
    q_total = None
    q_ready = []
    for dist in range(size):
        q_total, token = q_block(block[dist], hidden[dist], q_weight, q_total)
        q_ready.append(token)
    values = packed(qa_store, qb_store, *far.upto(0))
    q_used = [{}, {}]
    seen = len(near.done)
    fetch_far(values, q_used, 0)
    fetch_far(values, q_used, 1)
    fetch_near(values, q_used, [far.upto(2), far.upto(3)])

    reduce_step(0, True, *far.upto(1), near.done[0], *ready, values[0], *q_ready[:1])
    reduce_step(0, False, *far.upto(2), *near.done[:seen], *q_ready[1 : size // 2 + 1])
    o_half = down(found, rank, attn_rows, pieces_of(o_used[0], all_dists))
    o_others = exchange(o_half, *far.upto(3)[:1], *[chain.done[-1] for chain in chains.values()], q_ready[-1])
    for step in range(1, len(order)):
        reduce_step(step, False, *far.upto(3), near.done[seen], *o_others)
    o_down = functools.reduce(jnp.add, o_others, o_half)
    bases = up(found, rank, o_down, o_used[1], all_dists, [one[0][0] for one in sums], jnp.float32)
    rounded = merge([(base, one[0][1]) for base, one in zip(bases, sums)], False)

    finished = share(rounded, chains, *far.upto(4), *near.done[seen:])

    q_half = down(found, rank, hidden_rows, pieces_of(q_used[0], all_dists))
    q_others = exchange(q_half)
    q_down = functools.reduce(jnp.add, q_others, q_half)
    finished = forward(finished, chains, *far.upto(5), *q_others)

    out_shape = jax.ShapeDtypeStruct((rows, width * size), jnp.bfloat16)
    early = [dist for dist in range(size) if len(finished[dist]) == 1]
    late = [dist for dist in range(size) if len(finished[dist]) > 1]

    def placed(dists, into):
        columns = jnp.concatenate([block[dist] for dist in dists])
        return place(columns, [finished[dist] for dist in dists], into, out_shape)

    attn_out = placed(early, None)
    last = far_dists[-2:]
    first = [dist for dist in all_dists if dist not in last]
    (total,) = up(found, rank, q_down, q_used[1], first, [after(q_total, attn_out)], jnp.float32)
    (queries,) = up(found, rank, q_down, q_used[1], last, [total], jnp.bfloat16)
    attn_out = placed(late, attn_out)
    return (queries, attn_out)


def solution(mesh):
    return jax.shard_map(
        body,
        mesh=mesh,
        in_specs=(
            P("group", "tensor"),
            P("group", "tensor"),
            P(None, "tensor"),
            P("tensor", None),
            P(),
            P(),
            P("group", None),
            P("group", None),
            P("group", "tensor", None),
            P("group", None, "tensor"),
            P("group", "tensor", None),
            P("group", None, "tensor"),
        ),
        out_specs=(P("group", "tensor"), P("group", None)),
        check_vma=False,
    )
```

```python
import functools
import math

import jax
import jax.numpy as jnp
from jax import lax
from jax.experimental import pallas as pl
from jax.experimental.pallas import tpu as pltpu
from jax.sharding import PartitionSpec as P

ADAPTER_SCALE = 0.5
LANES = 128
LEVELS = 8
STEPS = 32767.0
MIB = 1024 * 1024
ANY = pl.BlockSpec(memory_space=pl.ANY)
SMEM = pl.BlockSpec(memory_space=pltpu.SMEM)
VMEM = pl.BlockSpec(memory_space=pltpu.VMEM)
HBM = pl.BlockSpec(memory_space=pltpu.HBM)


def params(mebibytes):
    return pltpu.CompilerParams(vmem_limit_bytes=mebibytes * MIB)


def cost(flops, nbytes):
    return pl.CostEstimate(flops=flops // 1000, bytes_accessed=nbytes // 1000, transcendentals=0)


def send(value, axis, offset):
    size = lax.axis_size(axis)
    return lax.ppermute(value, axis, [(i, i ^ offset) for i in range(size)])


def after(value, *others):
    return lax.optimization_barrier((value, *others))[0]


def at(values, *numbers):
    return [values[number] for number in numbers if number < len(values)]


class Chain:
    def __init__(self, axis):
        self.axis = axis
        self.done = []

    def send(self, value, offset, *pins):
        pins = (*self.done[-1:], *pins)
        if pins:
            value = after(value, *pins)
        arrived = send(value, self.axis, offset)
        self.done.append(arrived)
        return arrived


class Groups:
    def __init__(self, axis, ends):
        self.axis = axis
        self.ends = ends
        self.done = []

    def upto(self, step):
        start = self.ends[step - 1] if step else 0
        return self.done[start : self.ends[step]]

    def send(self, value, offset):
        number = len(self.done)
        step = sum(end <= number for end in self.ends)
        if step:
            value = after(value, *self.upto(step - 1))
        arrived = send(value, self.axis, offset)
        self.done.append(arrived)
        return arrived


def bits(size):
    out = []
    bit = 1
    while bit < size:
        out.append(bit)
        bit *= 2
    return out


def pack_kernel(plan, count, table_ref, adapters_ref, *refs):
    stores = refs[:count]
    outs = refs[-3 - len(plan) : -3]
    staged, in_sems, out_sems = refs[-3:]
    slots = adapters_ref.shape[1]
    held, rank, _ = stores[0].shape
    me = lax.axis_index("group")
    loads = []
    for dist, parts in plan:
        dest = me ^ dist
        pick = jnp.int32(0)
        for slot in range(slots):
            place = table_ref[adapters_ref[dest, slot]]
            owner = lax.div(place, jnp.int32(held))
            pick = jnp.where(owner == me, place - owner * held, pick)
        for part in parts:
            number = len(loads)
            load = pltpu.make_async_copy(stores[part].at[pick], staged.at[number], in_sems.at[number])
            load.start()
            loads.append(load)
    copies = []
    for out_ref, (_, parts) in zip(outs, plan):
        for row in range(len(parts)):
            number = len(copies)
            loads[number].wait()
            copy = pltpu.make_async_copy(
                staged.at[number], out_ref.at[pl.ds(row * rank, rank)], out_sems.at[number]
            )
            copy.start()
            copies.append(copy)
    for copy in copies:
        copy.wait()


def pack(plan, table, adapters, stores, order, mebibytes):
    _, rank, width = stores[0].shape
    dtype = stores[0].dtype
    total = sum(len(parts) for _, parts in plan)
    return pl.pallas_call(
        functools.partial(pack_kernel, plan, len(stores)),
        out_shape=[pltpu.HBM((len(parts) * rank, width), dtype) for _, parts in plan],
        in_specs=[SMEM, SMEM] + [HBM] * len(stores) + [ANY] * len(order),
        out_specs=[HBM] * len(plan),
        scratch_shapes=[
            pltpu.VMEM((total, rank, width), dtype),
            pltpu.SemaphoreType.DMA((total,)),
            pltpu.SemaphoreType.DMA((total,)),
        ],
        compiler_params=params(mebibytes),
        cost_estimate=cost(0, 4 * total * rank * width),
    )(table, adapters, *stores, *order)


def distance_kernel(held, table_ref, adapters_ref, slot_ref, len_ref, out_ref):
    me = lax.axis_index("group")
    position = lax.broadcasted_iota(jnp.int32, out_ref.shape, 0)
    found = jnp.zeros(out_ref.shape, jnp.int32)
    start = jnp.int32(0)
    for req in range(len_ref.shape[1]):
        place = table_ref[adapters_ref[me, slot_ref[0, req]]]
        dist = lax.div(place, jnp.int32(held)) ^ me
        end = start + len_ref[0, req]
        found = jnp.where((position >= start) & (position < end), dist, found)
        start = end
    out_ref[...] = found


def row_distances(routing, held, rows, lanes):
    return pl.pallas_call(
        functools.partial(distance_kernel, held),
        out_shape=jax.ShapeDtypeStruct((rows, lanes), jnp.int32),
        in_specs=[SMEM] * 4,
        out_specs=VMEM,
        compiler_params=params(4),
        cost_estimate=cost(0, 4 * rows * lanes),
    )(*routing)


def down_kernel(rank, places, found_ref, rows_ref, *refs):
    groups = len(places)
    pieces = refs[:groups]
    out_ref, whole, sems = refs[groups:]
    copies = []
    for dist in range(groups):
        copy = pltpu.make_async_copy(
            pieces[dist].at[pl.ds(places[dist] * rank, rank)], whole.at[pl.ds(dist * rank, rank)], sems.at[dist]
        )
        copy.start()
        copies.append(copy)
    shape = (rows_ref.shape[0], 2 * rank)
    found = found_ref[...]
    high = (lax.broadcasted_iota(jnp.int32, shape, 1) >= rank).astype(jnp.int32)
    for copy in copies:
        copy.wait()
    full = lax.dot_general(
        rows_ref[...], whole[...], (((1,), (1,)), ((), ())), preferred_element_type=jnp.float32
    )
    picked = jnp.zeros(shape, jnp.float32)
    for pair in range(groups // 2):
        piece = full[:, pair * 2 * rank : (pair + 1) * 2 * rank]
        picked = picked + jnp.where(found == 2 * pair + high, piece, 0.0)
    out_ref[...] = picked + pltpu.roll(picked, rank, 1)


def down(found, rank, rows_in, pieces):
    rows, width = rows_in.shape
    groups = len(pieces)
    return pl.pallas_call(
        functools.partial(down_kernel, rank, [row for _, row in pieces]),
        out_shape=jax.ShapeDtypeStruct((rows, 2 * rank), jnp.float32),
        in_specs=[VMEM] * 2 + [ANY] * groups,
        out_specs=VMEM,
        scratch_shapes=[
            pltpu.VMEM((groups * rank, width), rows_in.dtype),
            pltpu.SemaphoreType.DMA((groups,)),
        ],
        compiler_params=params(12),
        cost_estimate=cost(2 * rows * width * groups * rank, 2 * rows * width + 2 * groups * rank * width),
    )(found, rows_in, *[piece for piece, _ in pieces])


def up_kernel(dists, split, found_ref, down_ref, *refs):
    groups = len(dists)
    pieces = refs[:groups]
    bases = refs[groups : groups + split]
    outs = refs[groups + split : groups + 2 * split]
    terms = refs[-1]
    rank = pieces[0].shape[0]
    rows = down_ref.shape[0]

    @pl.when(pl.program_id(0) == 0)
    def _():
        shape = (rows, 2 * rank)
        found = found_ref[...]
        low = lax.broadcasted_iota(jnp.int32, shape, 1) < rank
        both = down_ref[...] * ADAPTER_SCALE
        first = both.astype(jnp.bfloat16)
        rest = both - first.astype(jnp.float32)
        second = rest.astype(jnp.bfloat16)
        third = (rest - second.astype(jnp.float32)).astype(jnp.bfloat16)
        for number, term in enumerate((first, second, third)):
            for pair in range(groups // 2):
                wanted = jnp.where(low, dists[2 * pair], dists[2 * pair + 1])
                chosen = jnp.where(found == wanted, term.astype(jnp.float32), 0.0)
                terms[number, :, pair * 2 * rank : (pair + 1) * 2 * rank] = chosen.astype(jnp.bfloat16)

    whole = jnp.concatenate([piece[...] for piece in pieces], axis=0)
    total = jnp.dot(terms[2], whole, preferred_element_type=jnp.float32)
    total = total + jnp.dot(terms[1], whole, preferred_element_type=jnp.float32)
    total = total + jnp.dot(terms[0], whole, preferred_element_type=jnp.float32)
    size = rows // split
    for number in range(split):
        value = bases[number][...] + total[number * size : (number + 1) * size]
        outs[number][...] = value.astype(outs[number].dtype)


def up(found, rank, downs, used, dists, bases, out_dtype):
    pieces = [used[dist] for dist in dists]
    groups = len(dists)
    width = pieces[0][0].shape[1]
    rows = downs.shape[0]
    split = len(bases)
    tile = min(512, width)
    column = lambda step: (0, step)
    size = rows // split
    piece_specs = [
        pl.BlockSpec((rank, tile), functools.partial(lambda place, step: (place, step), place)) for _, place in pieces
    ]
    return pl.pallas_call(
        functools.partial(up_kernel, dists, split),
        grid=(width // tile,),
        out_shape=[jax.ShapeDtypeStruct((size, width), out_dtype)] * split,
        in_specs=[pl.BlockSpec(downs.shape, lambda step: (0, 0))] * 2
        + piece_specs
        + [pl.BlockSpec((size, tile), column)] * split,
        out_specs=[pl.BlockSpec((size, tile), column)] * split,
        scratch_shapes=[pltpu.VMEM((3, rows, groups * rank), jnp.bfloat16)],
        compiler_params=params(16),
        cost_estimate=cost(6 * rows * width * groups * rank, 8 * rows * width + 2 * groups * rank * width),
    )(found, downs, *[piece for piece, _ in pieces], *bases)


def tile_of(width):
    return min(512, width)


def encode(value, out_ref, step):
    half, tile = value.shape
    width = out_ref.shape[1] - LANES
    peak = jnp.max(jnp.abs(value), axis=1, keepdims=True)
    level = jnp.ceil(jnp.log(jnp.maximum(peak, 1e-30)) * (LEVELS / math.log(2.0)))
    coded = jnp.round(value * (jnp.exp2(level * (-1.0 / LEVELS)) * STEPS))
    coded = jnp.minimum(jnp.maximum(coded, -STEPS), STEPS)
    start = step * tile if isinstance(step, int) else pl.multiple_of(step * tile, tile)
    out_ref[:, pl.ds(start, tile)] = coded.astype(jnp.int32).astype(jnp.int16)
    lane = lax.broadcasted_iota(jnp.int32, (half, LANES), 1)
    kept = jnp.where(lane < step, out_ref[:, width:].astype(jnp.int32), 0)
    out_ref[:, width:] = jnp.where(lane == step, level.astype(jnp.int32), kept).astype(jnp.int16)


def decode(coded_ref, step, tile):
    width = coded_ref.shape[1] - LANES
    levels = coded_ref[:, width:].astype(jnp.int32)
    lane = lax.broadcasted_iota(jnp.int32, levels.shape, 1)
    level = jnp.sum(jnp.where(lane == step, levels, 0).astype(jnp.float32), axis=1, keepdims=True)
    value = coded_ref[:, step * tile : (step + 1) * tile].astype(jnp.int32).astype(jnp.float32)
    return value * (jnp.exp2(level * (1.0 / LEVELS)) * (1.0 / STEPS))


def merge_kernel(counts, coded_out, *refs):
    out_ref = refs[-1]
    inputs = refs[:-1]
    for number, count in enumerate(counts):
        base, coded = inputs[0], inputs[1 : 1 + count]
        inputs = inputs[1 + count :]
        half, width = base.shape
        tile = tile_of(width)
        for step in range(width // tile):
            columns = slice(step * tile, (step + 1) * tile)
            total = base[:, columns]
            for one in coded:
                total = total + decode(one, step, tile)
            if coded_out:
                encode(total, out_ref, step)
            else:
                out_ref[number * half : (number + 1) * half, columns] = total.astype(out_ref.dtype)


def merge(sums, coded_out, dtype=jnp.bfloat16):
    half, width = sums[0][0].shape
    counts = [len(coded) for _, coded in sums]
    if coded_out:
        out_shape = jax.ShapeDtypeStruct((half, width + LANES), jnp.int16)
    else:
        out_shape = jax.ShapeDtypeStruct((len(sums) * half, width), dtype)
    values = [value for base, coded in sums for value in (base, *coded)]
    return pl.pallas_call(
        functools.partial(merge_kernel, counts, coded_out),
        out_shape=out_shape,
        in_specs=[VMEM] * len(values),
        out_specs=VMEM,
        compiler_params=params(16),
        cost_estimate=cost(0, 2 * sum(value.size for value in values) + 4 * half * width),
    )(*values)


def o_kernel(block_ref, rows_ref, weight_ref, *outs):
    del block_ref
    total = jnp.dot(rows_ref[...], weight_ref[...], preferred_element_type=jnp.float32)
    half = outs[0].shape[0]
    for number, out_ref in enumerate(outs):
        value = total[number * half : (number + 1) * half]
        if out_ref.dtype == jnp.int16:
            encode(value, out_ref, pl.program_id(0))
        else:
            out_ref[...] = value


def o_block(block, rows_in, weight, width, coded):
    rows, depth = rows_in.shape
    half = rows // 2
    tile = tile_of(width)
    tiles = width // tile
    shapes, specs = [], []
    for one in coded:
        if one:
            shapes.append(jax.ShapeDtypeStruct((half, width + LANES), jnp.int16))
            specs.append(pl.BlockSpec((half, width + LANES), lambda step, ref: (0, 0)))
        else:
            shapes.append(jax.ShapeDtypeStruct((half, width), jnp.float32))
            specs.append(pl.BlockSpec((half, tile), lambda step, ref: (0, step)))
    return pl.pallas_call(
        o_kernel,
        grid_spec=pltpu.PrefetchScalarGridSpec(
            num_scalar_prefetch=1,
            grid=(tiles,),
            in_specs=[
                pl.BlockSpec((rows, depth), lambda step, ref: (0, 0)),
                pl.BlockSpec((depth, tile), lambda step, ref: (0, ref[0] * tiles + step)),
            ],
            out_specs=specs,
        ),
        out_shape=shapes,
        compiler_params=params(36),
        cost_estimate=cost(2 * rows * depth * width, 2 * depth * width + 2 * rows * depth + 4 * rows * width),
    )(block, rows_in, weight)


def q_kernel(count, has_total, block_ref, *refs):
    del block_ref
    pieces = refs[:count]
    weight_ref = refs[count]
    out_ref, token_ref = refs[-2:]
    size = pieces[0].shape[0]
    token_ref[...] = jnp.zeros_like(token_ref)
    for number, rows_ref in enumerate(pieces):
        total = jnp.dot(rows_ref[...], weight_ref[...], preferred_element_type=jnp.float32)
        span = slice(number * size, (number + 1) * size)
        if has_total:
            total = total + refs[count + 1][span]
        out_ref[span] = total


def q_block(block, pieces, weight, total):
    count = len(pieces)
    size, depth = pieces[0].shape
    rows = count * size
    width = weight.shape[1]
    tile = tile_of(width)
    has_total = total is not None
    column = pl.BlockSpec((rows, tile), lambda step, ref: (0, step))
    return pl.pallas_call(
        functools.partial(q_kernel, count, has_total),
        grid_spec=pltpu.PrefetchScalarGridSpec(
            num_scalar_prefetch=1,
            grid=(width // tile,),
            in_specs=[pl.BlockSpec((size, depth), lambda step, ref: (0, 0))] * count
            + [pl.BlockSpec((depth, tile), lambda step, ref: (ref[0], step))]
            + [column] * has_total,
            out_specs=[column, pl.BlockSpec((8, LANES), lambda step, ref: (0, 0))],
        ),
        out_shape=[jax.ShapeDtypeStruct((rows, width), jnp.float32), jax.ShapeDtypeStruct((8, LANES), jnp.float32)],
        input_output_aliases={count + 2: 0} if has_total else {},
        compiler_params=params(36),
        cost_estimate=cost(2 * rows * depth * width, 2 * depth * width + 2 * rows * depth + 8 * rows * width),
    )(block, *pieces, weight, *([total] * has_total))


def share(block, chains, *pins):
    whole = {0: block}
    for bit in chains:
        whole[bit] = chains[bit].send(block, bit, *pins)
    return whole


def forward(whole, chains, *pins):
    order = list(chains)
    half = whole[0].shape[0] // 2
    parts = [{}, {}]
    for step in range(len(order)):
        for number in range(2):
            bits_used = order if number == 0 else order[::-1]
            bit = bits_used[step]
            held = [0]
            for used in bits_used[:step]:
                held = held + [dist ^ used for dist in held]
            for dist in held[1:]:
                if dist in whole:
                    piece = whole[dist][number * half : (number + 1) * half]
                else:
                    piece = parts[number][dist]
                parts[number][dist ^ bit] = chains[bit].send(piece, bit, *pins)
    pieces = {dist: [value] for dist, value in whole.items()}
    for dist in parts[0]:
        pieces[dist] = [parts[0][dist], parts[1][dist]]
    return pieces


def place_kernel(blocks, column_ref, *refs):
    out_ref, sems = refs[-2:]
    width = refs[0].shape[1]
    copies = []
    number = 0
    for block, count in enumerate(blocks):
        start = pl.multiple_of(column_ref[block] * width, width)
        for part in range(count):
            size = refs[number].shape[0]
            copy = pltpu.make_async_copy(
                refs[number], out_ref.at[pl.ds(part * size, size), pl.ds(start, width)], sems.at[number]
            )
            copy.start()
            copies.append(copy)
            number += 1
    for copy in copies:
        copy.wait()


def place(columns, blocks, into, out_shape):
    counts = [len(pieces) for pieces in blocks]
    pieces = [piece for block in blocks for piece in block]
    old = [] if into is None else [into]
    return pl.pallas_call(
        functools.partial(place_kernel, counts),
        out_shape=out_shape,
        in_specs=[SMEM] + [VMEM] * len(pieces) + [ANY] * len(old),
        out_specs=ANY,
        scratch_shapes=[pltpu.SemaphoreType.DMA((len(pieces),))],
        input_output_aliases={len(pieces) + 1: 0} if old else {},
        compiler_params=params(10),
        cost_estimate=cost(0, 4 * sum(piece.size for piece in pieces)),
    )(columns, *pieces, *old)


def body(
    hidden_rows,
    attn_rows,
    q_weight,
    o_weight,
    owner_table,
    group_adapters,
    req_slot,
    req_len,
    qa_store,
    qb_store,
    oa_store,
    ob_store,
):
    groups = lax.axis_size("group")
    size = lax.axis_size("tensor")
    mine = lax.axis_index("tensor")
    held, _, rank = qa_store.shape
    rows, _ = hidden_rows.shape
    width = o_weight.shape[1] // size
    routing = (owner_table, group_adapters, req_slot, req_len)
    block = [jnp.reshape(mine ^ dist, (1,)).astype(jnp.int32) for dist in range(size)]
    order = bits(size)

    far = Groups("group", [groups // 2 * 4 * part // 16 for part in (2, 4, 6, 8, 10, 11, 12, 14, 16)])
    near = Chain("group")
    chains = {bit: Chain("tensor") for bit in order}
    far_dists = list(range(groups // 2, groups))
    near_dists = list(range(groups // 2 - 1, 1, -1))
    all_dists = list(range(groups))
    stores = [jnp.swapaxes(oa_store, 1, 2), ob_store, jnp.swapaxes(qa_store, 1, 2), qb_store]
    used = [{}, {}, {}, {}]

    def packed(plan, mebibytes, *pins):
        wanted = sorted({part for _, parts in plan for part in parts})
        plan = [(dist, [wanted.index(part) for part in parts]) for dist, parts in plan]
        return pack(plan, owner_table, group_adapters, [stores[part] for part in wanted], pins, mebibytes)

    def fetch_far(values, part, dists):
        for value, dist in zip(values, dists):
            used[part][dist] = (far.send(value, dist), 0)

    def fetch_near(values, parts, pins, dists):
        for value, dist, some in zip(values, dists, pins):
            arrived = near.send(value, dist, *some)
            for row, part in enumerate(parts):
                used[part][dist] = (arrived, row)

    def pieces_of(part, dists):
        return [used[part][dist] for dist in dists]

    halving = (order, order[::-1])
    sums = [{}, {}]

    def reduce_step(step, first, *pins):
        for number in range(2):
            bit = halving[number][step]
            dists = sorted((one for one in sums[number] if one & bit), reverse=True)
            for dist in dists[:1] if first else dists:
                base, coded = sums[number].pop(dist)
                value = base if step == 0 else merge([(base, coded)], True)
                arrived = chains[bit].send(value, bit, *pins)
                sums[number][dist ^ bit][1].append(arrived)

    def o_sums(dist):
        coded = [bool(dist & bit_order[0]) for bit_order in halving]
        values = o_block(block[dist], attn_rows, o_weight, width, coded)
        for number, value in enumerate(values):
            sums[number][dist] = (value, [])
        return values[0]

    hidden = share(hidden_rows, chains)
    lead = far_dists[:2]
    early = packed([(dist, (0,)) for dist in lead], 60)
    fetch_far(early, 0, lead)
    rest = [(dist, (0,)) for dist in far_dists[2:]] + [(dist, (1,)) for dist in far_dists]
    own = [(1, (0, 1, 2, 3)), (0, (0, 1, 2, 3))]
    values = packed(rest + [(dist, (0, 1)) for dist in near_dists] + own, 60, *early)
    fetch_far(values, 0, far_dists[2:])
    fetch_far(values[len(far_dists) - 2 :], 1, far_dists)
    beside = send(values[-2], "group", 1)
    for part in range(4):
        used[part][1] = (beside, part)
        used[part][0] = (values[-1], part)
    fetch_near(values[len(rest) :], (0, 1), [[*far.upto(0), beside], far.upto(1)], near_dists)
    found = row_distances(routing, held, rows, 2 * rank)
    ready = [o_sums(dist) for dist in sorted(range(1, size), reverse=True)]

    hidden = forward(hidden, chains, *far.upto(0), beside, *ready, found)
    ready = [o_sums(0)]
    q_total = None
    q_ready = []
    for dist in range(size):
        q_total, token = q_block(block[dist], hidden[dist], q_weight, q_total)
        q_ready.append(token)
    plan = [(dist, (part,)) for part in (2, 3) for dist in far_dists] + [(dist, (2, 3)) for dist in near_dists]
    values = packed(plan, 10, *far.upto(0))
    seen = len(near.done)
    fetch_near(values[2 * len(far_dists) :], (2, 3), [far.upto(2)], near_dists[:1])

    def arrivals():
        return [chain.done[-1] for chain in chains.values()]

    def summed(value, *pins):
        arrived = send(after(value, *pins) if pins else value, "tensor", order[0])
        return value + arrived, arrived

    def summed_on(value, *pins):
        for bit in order[1:]:
            value = value + send(after(value, *pins) if pins else value, "tensor", bit)
        return value

    reduce_step(0, True, *far.upto(1), near.done[0], *ready, values[0], *q_ready[:1])
    reduce_step(0, False, *far.upto(2), near.done[seen - 1], *q_ready[1 : size // 2 + 1])
    o_half = down(found, rank, attn_rows, pieces_of(0, all_dists))
    o_down = summed_on(summed(o_half, *arrivals())[0])
    for step in range(1, len(order)):
        reduce_step(step, False, *far.upto(3), *near.done[seen : seen + 1], o_half, q_ready[-1])
    bases = up(found, rank, o_down, used[1], all_dists, [one[0][0] for one in sums], jnp.float32)
    rounded = merge([(base, one[0][1]) for base, one in zip(bases, sums)], False)
    fetch_far(values, 2, far_dists)
    fetch_far(values[len(far_dists) :], 3, far_dists)
    fetch_near(values[2 * len(far_dists) + 1 :], (2, 3), [far.upto(5)], near_dists[1:])

    finished = share(rounded, chains, *far.upto(5))
    q_half = down(after(found, o_down), rank, hidden_rows, pieces_of(2, all_dists))
    q_down, q_arrived = summed(q_half)

    q_down = summed_on(q_down, *arrivals())
    finished = forward(finished, chains, *far.upto(7), q_arrived)

    out_shape = jax.ShapeDtypeStruct((rows, width * size), jnp.bfloat16)
    early = [dist for dist in range(size) if len(finished[dist]) == 1]
    late = [dist for dist in range(size) if len(finished[dist]) > 1]

    def placed(dists, into):
        columns = jnp.concatenate([block[dist] for dist in dists])
        return place(columns, [finished[dist] for dist in dists], into, out_shape)

    attn_out = placed(early, None)
    last = far_dists[-2:]
    first = [dist for dist in all_dists if dist not in last]
    (total,) = up(found, rank, q_down, used[3], first, [after(q_total, attn_out)], jnp.float32)
    (queries,) = up(found, rank, q_down, used[3], last, [total], jnp.bfloat16)
    attn_out = placed(late, attn_out)
    return (queries, attn_out)


def solution(mesh):
    return jax.shard_map(
        body,
        mesh=mesh,
        in_specs=(
            P("group", "tensor"),
            P("group", "tensor"),
            P(None, "tensor"),
            P("tensor", None),
            P(),
            P(),
            P("group", None),
            P("group", None),
            P("group", "tensor", None),
            P("group", None, "tensor"),
            P("group", "tensor", None),
            P("group", None, "tensor"),
        ),
        out_specs=(P("group", "tensor"), P("group", None)),
        check_vma=False,
    )
```

```python
import functools
import math

import jax
import jax.numpy as jnp
from jax import lax
from jax.experimental import pallas as pl
from jax.experimental.pallas import tpu as pltpu
from jax.sharding import PartitionSpec as P

ADAPTER_SCALE = 0.5
LANES = 128
LEVELS = 8
STEPS = 32767.0
MIB = 1024 * 1024
ANY = pl.BlockSpec(memory_space=pl.ANY)
SMEM = pl.BlockSpec(memory_space=pltpu.SMEM)
VMEM = pl.BlockSpec(memory_space=pltpu.VMEM)
HBM = pl.BlockSpec(memory_space=pltpu.HBM)


def params(mebibytes):
    return pltpu.CompilerParams(vmem_limit_bytes=mebibytes * MIB)


def cost(flops, nbytes):
    return pl.CostEstimate(flops=flops // 1000, bytes_accessed=nbytes // 1000, transcendentals=0)


def send(value, axis, offset):
    size = lax.axis_size(axis)
    return lax.ppermute(value, axis, [(i, i ^ offset) for i in range(size)])


def after(value, *others):
    return lax.optimization_barrier((value, *others))[0]


def at(values, *numbers):
    return [values[number] for number in numbers if number < len(values)]


class Chain:
    def __init__(self, axis):
        self.axis = axis
        self.done = []

    def send(self, value, offset, *pins):
        pins = (*self.done[-1:], *pins)
        if pins:
            value = after(value, *pins)
        arrived = send(value, self.axis, offset)
        self.done.append(arrived)
        return arrived


class Groups:
    def __init__(self, axis, ends):
        self.axis = axis
        self.ends = ends
        self.done = []

    def upto(self, step):
        start = self.ends[step - 1] if step else 0
        return self.done[start : self.ends[step]]

    def send(self, value, offset, *pins):
        number = len(self.done)
        step = sum(end <= number for end in self.ends)
        if step:
            value = after(value, *self.upto(step - 1), *pins)
        arrived = send(value, self.axis, offset)
        self.done.append(arrived)
        return arrived


def bits(size):
    out = []
    bit = 1
    while bit < size:
        out.append(bit)
        bit *= 2
    return out


def pack_kernel(plan, count, table_ref, adapters_ref, *refs):
    stores = refs[:count]
    outs = refs[-3 - len(plan) : -3]
    staged, in_sems, out_sems = refs[-3:]
    slots = adapters_ref.shape[1]
    held, rank, _ = stores[0].shape
    me = lax.axis_index("group")
    loads = []
    for dist, parts in plan:
        dest = me ^ dist
        pick = jnp.int32(0)
        for slot in range(slots):
            place = table_ref[adapters_ref[dest, slot]]
            owner = lax.div(place, jnp.int32(held))
            pick = jnp.where(owner == me, place - owner * held, pick)
        for part in parts:
            number = len(loads)
            load = pltpu.make_async_copy(stores[part].at[pick], staged.at[number], in_sems.at[number])
            load.start()
            loads.append(load)
    copies = []
    for out_ref, (_, parts) in zip(outs, plan):
        for row in range(len(parts)):
            number = len(copies)
            loads[number].wait()
            copy = pltpu.make_async_copy(
                staged.at[number], out_ref.at[pl.ds(row * rank, rank)], out_sems.at[number]
            )
            copy.start()
            copies.append(copy)
    for copy in copies:
        copy.wait()


def pack(plan, table, adapters, stores, order, mebibytes):
    _, rank, width = stores[0].shape
    dtype = stores[0].dtype
    total = sum(len(parts) for _, parts in plan)
    return pl.pallas_call(
        functools.partial(pack_kernel, plan, len(stores)),
        out_shape=[pltpu.HBM((len(parts) * rank, width), dtype) for _, parts in plan],
        in_specs=[SMEM, SMEM] + [HBM] * len(stores) + [ANY] * len(order),
        out_specs=[HBM] * len(plan),
        scratch_shapes=[
            pltpu.VMEM((total, rank, width), dtype),
            pltpu.SemaphoreType.DMA((total,)),
            pltpu.SemaphoreType.DMA((total,)),
        ],
        compiler_params=params(mebibytes),
        cost_estimate=cost(0, 4 * total * rank * width),
    )(table, adapters, *stores, *order)


def distance_kernel(held, table_ref, adapters_ref, slot_ref, len_ref, out_ref):
    me = lax.axis_index("group")
    position = lax.broadcasted_iota(jnp.int32, out_ref.shape, 0)
    found = jnp.zeros(out_ref.shape, jnp.int32)
    start = jnp.int32(0)
    for req in range(len_ref.shape[1]):
        place = table_ref[adapters_ref[me, slot_ref[0, req]]]
        dist = lax.div(place, jnp.int32(held)) ^ me
        end = start + len_ref[0, req]
        found = jnp.where((position >= start) & (position < end), dist, found)
        start = end
    out_ref[...] = found


def row_distances(routing, held, rows, lanes):
    return pl.pallas_call(
        functools.partial(distance_kernel, held),
        out_shape=jax.ShapeDtypeStruct((rows, lanes), jnp.int32),
        in_specs=[SMEM] * 4,
        out_specs=VMEM,
        compiler_params=params(4),
        cost_estimate=cost(0, 4 * rows * lanes),
    )(*routing)


def down_kernel(rank, places, found_ref, rows_ref, *refs):
    groups = len(places)
    pieces = refs[:groups]
    out_ref, whole, sems = refs[groups:]
    copies = []
    for dist in range(groups):
        copy = pltpu.make_async_copy(
            pieces[dist].at[pl.ds(places[dist] * rank, rank)], whole.at[pl.ds(dist * rank, rank)], sems.at[dist]
        )
        copy.start()
        copies.append(copy)
    shape = (rows_ref.shape[0], 2 * rank)
    found = found_ref[...]
    high = (lax.broadcasted_iota(jnp.int32, shape, 1) >= rank).astype(jnp.int32)
    for copy in copies:
        copy.wait()
    full = lax.dot_general(
        rows_ref[...], whole[...], (((1,), (1,)), ((), ())), preferred_element_type=jnp.float32
    )
    picked = jnp.zeros(shape, jnp.float32)
    for pair in range(groups // 2):
        piece = full[:, pair * 2 * rank : (pair + 1) * 2 * rank]
        picked = picked + jnp.where(found == 2 * pair + high, piece, 0.0)
    out_ref[...] = picked + pltpu.roll(picked, rank, 1)


def down(found, rank, rows_in, pieces):
    rows, width = rows_in.shape
    groups = len(pieces)
    return pl.pallas_call(
        functools.partial(down_kernel, rank, [row for _, row in pieces]),
        out_shape=jax.ShapeDtypeStruct((rows, 2 * rank), jnp.float32),
        in_specs=[VMEM] * 2 + [ANY] * groups,
        out_specs=VMEM,
        scratch_shapes=[
            pltpu.VMEM((groups * rank, width), rows_in.dtype),
            pltpu.SemaphoreType.DMA((groups,)),
        ],
        compiler_params=params(12),
        cost_estimate=cost(2 * rows * width * groups * rank, 2 * rows * width + 2 * groups * rank * width),
    )(found, rows_in, *[piece for piece, _ in pieces])


def up_kernel(dists, split, found_ref, down_ref, *refs):
    groups = len(dists)
    pieces = refs[:groups]
    bases = refs[groups : groups + split]
    outs = refs[groups + split : groups + 2 * split]
    terms = refs[-1]
    rank = pieces[0].shape[0]
    rows = down_ref.shape[0]

    @pl.when(pl.program_id(0) == 0)
    def _():
        shape = (rows, 2 * rank)
        found = found_ref[...]
        low = lax.broadcasted_iota(jnp.int32, shape, 1) < rank
        both = down_ref[...] * ADAPTER_SCALE
        first = both.astype(jnp.bfloat16)
        rest = both - first.astype(jnp.float32)
        second = rest.astype(jnp.bfloat16)
        third = (rest - second.astype(jnp.float32)).astype(jnp.bfloat16)
        for number, term in enumerate((first, second, third)):
            for pair in range(groups // 2):
                wanted = jnp.where(low, dists[2 * pair], dists[2 * pair + 1])
                chosen = jnp.where(found == wanted, term.astype(jnp.float32), 0.0)
                terms[number, :, pair * 2 * rank : (pair + 1) * 2 * rank] = chosen.astype(jnp.bfloat16)

    whole = jnp.concatenate([piece[...] for piece in pieces], axis=0)
    total = jnp.dot(terms[2], whole, preferred_element_type=jnp.float32)
    total = total + jnp.dot(terms[1], whole, preferred_element_type=jnp.float32)
    total = total + jnp.dot(terms[0], whole, preferred_element_type=jnp.float32)
    size = rows // split
    for number in range(split):
        value = bases[number][...] + total[number * size : (number + 1) * size]
        outs[number][...] = value.astype(outs[number].dtype)


def up(found, rank, downs, used, dists, bases, out_dtype):
    pieces = [used[dist] for dist in dists]
    groups = len(dists)
    width = pieces[0][0].shape[1]
    rows = downs.shape[0]
    split = len(bases)
    tile = min(512, width)
    column = lambda step: (0, step)
    size = rows // split
    piece_specs = [
        pl.BlockSpec((rank, tile), functools.partial(lambda place, step: (place, step), place)) for _, place in pieces
    ]
    return pl.pallas_call(
        functools.partial(up_kernel, dists, split),
        grid=(width // tile,),
        out_shape=[jax.ShapeDtypeStruct((size, width), out_dtype)] * split,
        in_specs=[pl.BlockSpec(downs.shape, lambda step: (0, 0))] * 2
        + piece_specs
        + [pl.BlockSpec((size, tile), column)] * split,
        out_specs=[pl.BlockSpec((size, tile), column)] * split,
        scratch_shapes=[pltpu.VMEM((3, rows, groups * rank), jnp.bfloat16)],
        compiler_params=params(16),
        cost_estimate=cost(6 * rows * width * groups * rank, 8 * rows * width + 2 * groups * rank * width),
    )(found, downs, *[piece for piece, _ in pieces], *bases)


def tile_of(width):
    return min(512, width)


def encode(value, out_ref, step):
    half, tile = value.shape
    width = out_ref.shape[1] - LANES
    peak = jnp.max(jnp.abs(value), axis=1, keepdims=True)
    level = jnp.ceil(jnp.log(jnp.maximum(peak, 1e-30)) * (LEVELS / math.log(2.0)))
    coded = jnp.round(value * (jnp.exp2(level * (-1.0 / LEVELS)) * STEPS))
    coded = jnp.minimum(jnp.maximum(coded, -STEPS), STEPS)
    start = step * tile if isinstance(step, int) else pl.multiple_of(step * tile, tile)
    out_ref[:, pl.ds(start, tile)] = coded.astype(jnp.int32).astype(jnp.int16)
    lane = lax.broadcasted_iota(jnp.int32, (half, LANES), 1)
    kept = jnp.where(lane < step, out_ref[:, width:].astype(jnp.int32), 0)
    out_ref[:, width:] = jnp.where(lane == step, level.astype(jnp.int32), kept).astype(jnp.int16)


def decode(coded_ref, row, half, step, tile):
    width = coded_ref.shape[1] - LANES
    levels = coded_ref[row : row + half, width:].astype(jnp.int32)
    lane = lax.broadcasted_iota(jnp.int32, levels.shape, 1)
    level = jnp.sum(jnp.where(lane == step, levels, 0).astype(jnp.float32), axis=1, keepdims=True)
    value = coded_ref[row : row + half, step * tile : (step + 1) * tile].astype(jnp.int32).astype(jnp.float32)
    return value * (jnp.exp2(level * (1.0 / LEVELS)) * (1.0 / STEPS))


def merge_kernel(places, coded_out, *refs):
    out_ref = refs[-1]
    inputs = refs[:-1]
    for number, rows in enumerate(places):
        base, coded = inputs[0], inputs[1 : 1 + len(rows)]
        inputs = inputs[1 + len(rows) :]
        half, width = base.shape
        tile = tile_of(width)
        for step in range(width // tile):
            columns = slice(step * tile, (step + 1) * tile)
            total = base[:, columns]
            for one, row in zip(coded, rows):
                total = total + decode(one, row, half, step, tile)
            if coded_out:
                encode(total, out_ref, step)
            else:
                out_ref[number * half : (number + 1) * half, columns] = total.astype(out_ref.dtype)


def merge(sums, coded_out):
    half, width = sums[0][0].shape
    places = [[row for _, row in coded] for _, coded in sums]
    if coded_out:
        out_shape = jax.ShapeDtypeStruct((half, width + LANES), jnp.int16)
    else:
        out_shape = jax.ShapeDtypeStruct((len(sums) * half, width), jnp.bfloat16)
    values = []
    for base, coded in sums:
        values = values + [base] + [value for value, _ in coded]
    return pl.pallas_call(
        functools.partial(merge_kernel, places, coded_out),
        out_shape=out_shape,
        in_specs=[VMEM] * len(values),
        out_specs=VMEM,
        compiler_params=params(20),
        cost_estimate=cost(0, 2 * sum(value.size for value in values) + 4 * half * width),
    )(*values)


def o_kernel(block_ref, rows_ref, weight_ref, *refs):
    del block_ref
    outs = refs[-2:]
    total = jnp.dot(rows_ref[...], weight_ref[...], preferred_element_type=jnp.float32)
    half = outs[0].shape[0]
    for number, out_ref in enumerate(outs):
        value = total[number * half : (number + 1) * half]
        if out_ref.dtype == jnp.int16:
            encode(value, out_ref, pl.program_id(0))
        else:
            out_ref[...] = value


def o_block(block, rows_in, weight, width, leaving):
    rows, depth = rows_in.shape
    half = rows // 2
    tile = tile_of(width)
    tiles = width // tile
    shapes, specs, buffers, aliases = [], [], [], {}
    for number, one in enumerate(leaving):
        if one is None:
            shapes.append(jax.ShapeDtypeStruct((half, width), jnp.float32))
            specs.append(pl.BlockSpec((half, tile), lambda step, ref: (0, step)))
            continue
        buffer, place, places = one
        shapes.append(jax.ShapeDtypeStruct((places * half, width + LANES), jnp.int16))
        specs.append(
            pl.BlockSpec((half, width + LANES), functools.partial(lambda place, step, ref: (place, 0), place))
        )
        if buffer is not None:
            aliases[3 + len(buffers)] = number
            buffers.append(buffer)
    return pl.pallas_call(
        o_kernel,
        grid_spec=pltpu.PrefetchScalarGridSpec(
            num_scalar_prefetch=1,
            grid=(tiles,),
            in_specs=[
                pl.BlockSpec((rows, depth), lambda step, ref: (0, 0)),
                pl.BlockSpec((depth, tile), lambda step, ref: (0, ref[0] * tiles + step)),
            ]
            + [ANY] * len(buffers),
            out_specs=specs,
        ),
        out_shape=shapes,
        input_output_aliases=aliases,
        compiler_params=params(36),
        cost_estimate=cost(2 * rows * depth * width, 2 * depth * width + 2 * rows * depth + 4 * rows * width),
    )(block, rows_in, weight, *buffers)


def q_kernel(count, has_total, block_ref, *refs):
    del block_ref
    pieces = refs[:count]
    weight_ref = refs[count]
    out_ref, token_ref = refs[-2:]
    size = pieces[0].shape[0]
    token_ref[...] = jnp.zeros_like(token_ref)
    for number, rows_ref in enumerate(pieces):
        total = jnp.dot(rows_ref[...], weight_ref[...], preferred_element_type=jnp.float32)
        span = slice(number * size, (number + 1) * size)
        if has_total:
            total = total + refs[count + 1][span]
        out_ref[span] = total


def q_block(block, pieces, weight, total):
    count = len(pieces)
    size, depth = pieces[0].shape
    rows = count * size
    width = weight.shape[1]
    tile = tile_of(width)
    has_total = total is not None
    column = pl.BlockSpec((rows, tile), lambda step, ref: (0, step))
    return pl.pallas_call(
        functools.partial(q_kernel, count, has_total),
        grid_spec=pltpu.PrefetchScalarGridSpec(
            num_scalar_prefetch=1,
            grid=(width // tile,),
            in_specs=[pl.BlockSpec((size, depth), lambda step, ref: (0, 0))] * count
            + [pl.BlockSpec((depth, tile), lambda step, ref: (ref[0], step))]
            + [column] * has_total,
            out_specs=[column, pl.BlockSpec((8, LANES), lambda step, ref: (0, 0))],
        ),
        out_shape=[jax.ShapeDtypeStruct((rows, width), jnp.float32), jax.ShapeDtypeStruct((8, LANES), jnp.float32)],
        input_output_aliases={count + 2: 0} if has_total else {},
        compiler_params=params(36),
        cost_estimate=cost(2 * rows * depth * width, 2 * depth * width + 2 * rows * depth + 8 * rows * width),
    )(block, *pieces, weight, *([total] * has_total))


def share(block, chains, *pins):
    whole = {0: block}
    for bit in chains:
        whole[bit] = chains[bit].send(block, bit, *pins)
    return whole


def forward(whole, chains, *pins):
    order = list(chains)
    half = whole[0].shape[0] // 2
    parts = [{}, {}]
    for step in range(len(order)):
        for number in range(2):
            bits_used = order if number == 0 else order[::-1]
            bit = bits_used[step]
            held = [0]
            for used in bits_used[:step]:
                held = held + [dist ^ used for dist in held]
            for dist in held[1:]:
                if dist in whole:
                    piece = whole[dist][number * half : (number + 1) * half]
                else:
                    piece = parts[number][dist]
                parts[number][dist ^ bit] = chains[bit].send(piece, bit, *pins)
    pieces = {dist: [value] for dist, value in whole.items()}
    for dist in parts[0]:
        pieces[dist] = [parts[0][dist], parts[1][dist]]
    return pieces


def place_kernel(blocks, column_ref, *refs):
    out_ref, sems = refs[-2:]
    width = refs[0].shape[1]
    copies = []
    number = 0
    for block, count in enumerate(blocks):
        start = pl.multiple_of(column_ref[block] * width, width)
        for part in range(count):
            size = refs[number].shape[0]
            copy = pltpu.make_async_copy(
                refs[number], out_ref.at[pl.ds(part * size, size), pl.ds(start, width)], sems.at[number]
            )
            copy.start()
            copies.append(copy)
            number += 1
    for copy in copies:
        copy.wait()


def place(columns, blocks, into, out_shape):
    counts = [len(pieces) for pieces in blocks]
    pieces = [piece for block in blocks for piece in block]
    old = [] if into is None else [into]
    return pl.pallas_call(
        functools.partial(place_kernel, counts),
        out_shape=out_shape,
        in_specs=[SMEM] + [VMEM] * len(pieces) + [ANY] * len(old),
        out_specs=ANY,
        scratch_shapes=[pltpu.SemaphoreType.DMA((len(pieces),))],
        input_output_aliases={len(pieces) + 1: 0} if old else {},
        compiler_params=params(10),
        cost_estimate=cost(0, 4 * sum(piece.size for piece in pieces)),
    )(columns, *pieces, *old)


def body(
    hidden_rows,
    attn_rows,
    q_weight,
    o_weight,
    owner_table,
    group_adapters,
    req_slot,
    req_len,
    qa_store,
    qb_store,
    oa_store,
    ob_store,
):
    groups = lax.axis_size("group")
    size = lax.axis_size("tensor")
    mine = lax.axis_index("tensor")
    held, _, rank = qa_store.shape
    rows, _ = hidden_rows.shape
    width = o_weight.shape[1] // size
    half = rows // 2
    routing = (owner_table, group_adapters, req_slot, req_len)
    block = [jnp.reshape(mine ^ dist, (1,)).astype(jnp.int32) for dist in range(size)]
    order = bits(size)

    far = Groups("group", [groups // 2 * 4 * part // 16 for part in (2, 4, 6, 7, 9, 10, 12, 14, 16)])
    near = Chain("group")
    chains = {bit: Chain("tensor") for bit in order}
    far_dists = list(range(groups // 2, groups))
    near_dists = list(range(2, groups // 2))
    all_dists = list(range(groups))
    stores = [jnp.swapaxes(oa_store, 1, 2), ob_store, jnp.swapaxes(qa_store, 1, 2), qb_store]
    used = [{}, {}, {}, {}]

    def packed(plan, mebibytes, *pins):
        wanted = sorted({part for _, parts in plan for part in parts})
        plan = [(dist, [wanted.index(part) for part in parts]) for dist, parts in plan]
        return pack(plan, owner_table, group_adapters, [stores[part] for part in wanted], pins, mebibytes)

    def fetch_far(values, part, dists, *pins):
        for value, dist in zip(values, dists):
            used[part][dist] = (far.send(value, dist, *pins), 0)

    def fetch_near(values, parts, pins, dists):
        for value, dist, some in zip(values, dists, pins):
            arrived = near.send(value, dist, *some)
            for row, part in enumerate(parts):
                used[part][dist] = (arrived, row)

    def pieces_of(part, dists):
        return [used[part][dist] for dist in dists]

    def arrivals():
        return [chain.done[-1] for chain in chains.values()]

    def summed(value, *pins):
        arrived = send(after(value, *pins) if pins else value, "tensor", order[0])
        return value + arrived, arrived

    def summed_on(value, *pins):
        for bit in order[1:]:
            value = value + send(after(value, *pins) if pins else value, "tensor", bit)
        return value

    halving = (order, order[::-1])
    leaving = [sorted((dist for dist in range(size) if dist & halving[number][0]), reverse=True) for number in range(2)]
    buffers = [None, None]
    sums = [{}, {}]

    def o_sums(dist):
        wanted = []
        for number in range(2):
            if dist in leaving[number]:
                wanted.append((buffers[number], leaving[number].index(dist), len(leaving[number])))
            else:
                wanted.append(None)
        values = o_block(block[dist], attn_rows, o_weight, width, wanted)
        for number in range(2):
            if wanted[number] is None:
                sums[number][dist] = (values[number], [])
            else:
                buffers[number] = values[number]

    def reduce_first(*pins):
        for number in range(2):
            bit = halving[number][0]
            arrived = chains[bit].send(buffers[number], bit, *pins)
            for row, dist in enumerate(leaving[number]):
                sums[number][dist ^ bit][1].append((arrived, row * half))

    def reduce_step(step, *pins):
        for number in range(2):
            bit = halving[number][step]
            for dist in sorted((one for one in sums[number] if one & bit), reverse=True):
                arrived = chains[bit].send(merge([sums[number].pop(dist)], True), bit, *pins)
                sums[number][dist ^ bit][1].append((arrived, 0))

    hidden = share(hidden_rows, chains)
    lead = far_dists[:2]
    early = packed([(dist, (0,)) for dist in lead], 60)
    fetch_far(early, 0, lead)
    rest = [(dist, (0,)) for dist in far_dists[2:]] + [(dist, (1,)) for dist in far_dists]
    own = [(1, (0, 1, 2, 3)), (0, (0, 1, 2, 3))]
    values = packed(rest + [(dist, (0, 1)) for dist in near_dists] + own, 60, *early)
    fetch_far(values, 0, far_dists[2:])
    o_values = values[len(far_dists) - 2 :]
    fetch_far(o_values, 1, far_dists[:2])
    beside = send(values[-2], "group", 1)
    for part in range(4):
        used[part][1] = (beside, part)
        used[part][0] = (values[-1], part)
    fetch_near(values[len(rest) :], (0, 1), [[*far.upto(0), beside], far.upto(1)], near_dists)
    found = row_distances(routing, held, rows, 2 * rank)
    for dist in sorted(range(1, size), reverse=True):
        o_sums(dist)

    hidden = forward(hidden, chains, *far.upto(0), beside, *buffers, found)
    o_sums(0)
    q_total = None
    q_ready = []
    for dist in range(size):
        q_total, token = q_block(block[dist], hidden[dist], q_weight, q_total)
        q_ready.append(token)
    plan = [(dist, (part,)) for part in (2, 3) for dist in far_dists] + [(dist, (2, 3)) for dist in near_dists]
    values = packed(plan, 10, *far.upto(0))

    reduce_first(*far.upto(1), near.done[0], sums[0][0][0], values[0], *q_ready[:1])
    fetch_far(o_values[2:], 1, far_dists[2:], *q_ready[1 : size // 2 + 1])
    fetch_far(values, 2, far_dists[:1])
    fetch_far(values[1:], 2, far_dists[1:], q_ready[-1])
    fetch_far(values[len(far_dists) :], 3, far_dists)
    o_half = down(found, rank, attn_rows, pieces_of(0, all_dists))
    o_down, o_arrived = summed(o_half, *far.upto(2))
    pins = [*far.upto(3), o_arrived]
    o_down = summed_on(o_down, *arrivals())
    for step in range(1, len(order)):
        reduce_step(step, *pins)
    late = values[2 * len(far_dists) :][::-1]
    fetch_near(late, (2, 3), [far.upto(3), far.upto(5)], near_dists[::-1])
    bases = up(found, rank, o_down, used[1], all_dists, [one[0][0] for one in sums], jnp.float32)
    rounded = merge([(base, one[0][1]) for base, one in zip(bases, sums)], False)

    finished = share(rounded, chains, *far.upto(5), near.done[len(near_dists)], q_ready[-1])
    q_half = down(after(found, o_down), rank, hidden_rows, pieces_of(2, all_dists))
    q_down = summed_on(summed(q_half)[0])

    finished = forward(finished, chains, *far.upto(7), q_down)

    out_shape = jax.ShapeDtypeStruct((rows, width * size), jnp.bfloat16)
    soon = [dist for dist in range(size) if len(finished[dist]) == 1]
    late = [dist for dist in range(size) if len(finished[dist]) > 1]

    def placed(dists, into):
        columns = jnp.concatenate([block[dist] for dist in dists])
        return place(columns, [finished[dist] for dist in dists], into, out_shape)

    attn_out = placed(soon, None)
    last = far_dists[-2:]
    first = [dist for dist in all_dists if dist not in last]
    (total,) = up(found, rank, q_down, used[3], first, [after(q_total, attn_out)], jnp.float32)
    (queries,) = up(found, rank, q_down, used[3], last, [total], jnp.bfloat16)
    attn_out = placed(late, attn_out)
    return (queries, attn_out)


def solution(mesh):
    return jax.shard_map(
        body,
        mesh=mesh,
        in_specs=(
            P("group", "tensor"),
            P("group", "tensor"),
            P(None, "tensor"),
            P("tensor", None),
            P(),
            P(),
            P("group", None),
            P("group", None),
            P("group", "tensor", None),
            P("group", None, "tensor"),
            P("group", "tensor", None),
            P("group", None, "tensor"),
        ),
        out_specs=(P("group", "tensor"), P("group", None)),
        check_vma=False,
    )
```

```python
import functools
import math

import jax
import jax.numpy as jnp
from jax import lax
from jax.experimental import pallas as pl
from jax.experimental.pallas import tpu as pltpu
from jax.sharding import PartitionSpec as P

ADAPTER_SCALE = 0.5
LANES = 128
LEVELS = 8
STEPS = 32767.0
MIB = 1024 * 1024
ANY = pl.BlockSpec(memory_space=pl.ANY)
SMEM = pl.BlockSpec(memory_space=pltpu.SMEM)
VMEM = pl.BlockSpec(memory_space=pltpu.VMEM)
HBM = pl.BlockSpec(memory_space=pltpu.HBM)


def params(mebibytes):
    return pltpu.CompilerParams(vmem_limit_bytes=mebibytes * MIB)


def cost(flops, nbytes):
    return pl.CostEstimate(flops=flops // 1000, bytes_accessed=nbytes // 1000, transcendentals=0)


def send(value, axis, offset):
    size = lax.axis_size(axis)
    return lax.ppermute(value, axis, [(i, i ^ offset) for i in range(size)])


def after(value, *others):
    return lax.optimization_barrier((value, *others))[0]


def at(values, *numbers):
    return [values[number] for number in numbers if number < len(values)]


class Chain:
    def __init__(self, axis):
        self.axis = axis
        self.done = []

    def send(self, value, offset, *pins):
        pins = (*self.done[-1:], *pins)
        if pins:
            value = after(value, *pins)
        arrived = send(value, self.axis, offset)
        self.done.append(arrived)
        return arrived


class Groups:
    def __init__(self, axis, ends):
        self.axis = axis
        self.ends = ends
        self.done = []

    def upto(self, step):
        start = self.ends[step - 1] if step else 0
        return self.done[start : self.ends[step]]

    def send(self, value, offset, *pins):
        number = len(self.done)
        step = sum(end <= number for end in self.ends)
        if step:
            value = after(value, *self.upto(step - 1), *pins)
        arrived = send(value, self.axis, offset)
        self.done.append(arrived)
        return arrived


def bits(size):
    out = []
    bit = 1
    while bit < size:
        out.append(bit)
        bit *= 2
    return out


def pack_kernel(plan, count, table_ref, adapters_ref, *refs):
    stores = refs[:count]
    outs = refs[-3 - len(plan) : -3]
    staged, in_sems, out_sems = refs[-3:]
    slots = adapters_ref.shape[1]
    held, rank, _ = stores[0].shape
    me = lax.axis_index("group")
    loads = []
    for dist, parts in plan:
        dest = me ^ dist
        pick = jnp.int32(0)
        for slot in range(slots):
            place = table_ref[adapters_ref[dest, slot]]
            owner = lax.div(place, jnp.int32(held))
            pick = jnp.where(owner == me, place - owner * held, pick)
        for part in parts:
            number = len(loads)
            load = pltpu.make_async_copy(stores[part].at[pick], staged.at[number], in_sems.at[number])
            load.start()
            loads.append(load)
    copies = []
    for out_ref, (_, parts) in zip(outs, plan):
        for row in range(len(parts)):
            number = len(copies)
            loads[number].wait()
            copy = pltpu.make_async_copy(
                staged.at[number], out_ref.at[pl.ds(row * rank, rank)], out_sems.at[number]
            )
            copy.start()
            copies.append(copy)
    for copy in copies:
        copy.wait()


def pack(plan, table, adapters, stores, order, mebibytes):
    _, rank, width = stores[0].shape
    dtype = stores[0].dtype
    total = sum(len(parts) for _, parts in plan)
    return pl.pallas_call(
        functools.partial(pack_kernel, plan, len(stores)),
        out_shape=[pltpu.HBM((len(parts) * rank, width), dtype) for _, parts in plan],
        in_specs=[SMEM, SMEM] + [HBM] * len(stores) + [ANY] * len(order),
        out_specs=[HBM] * len(plan),
        scratch_shapes=[
            pltpu.VMEM((total, rank, width), dtype),
            pltpu.SemaphoreType.DMA((total,)),
            pltpu.SemaphoreType.DMA((total,)),
        ],
        compiler_params=params(mebibytes),
        cost_estimate=cost(0, 4 * total * rank * width),
    )(table, adapters, *stores, *order)


def distance_kernel(held, table_ref, adapters_ref, slot_ref, len_ref, out_ref):
    me = lax.axis_index("group")
    position = lax.broadcasted_iota(jnp.int32, out_ref.shape, 0)
    found = jnp.zeros(out_ref.shape, jnp.int32)
    start = jnp.int32(0)
    for req in range(len_ref.shape[1]):
        place = table_ref[adapters_ref[me, slot_ref[0, req]]]
        dist = lax.div(place, jnp.int32(held)) ^ me
        end = start + len_ref[0, req]
        found = jnp.where((position >= start) & (position < end), dist, found)
        start = end
    out_ref[...] = found


def row_distances(routing, held, rows, lanes):
    return pl.pallas_call(
        functools.partial(distance_kernel, held),
        out_shape=jax.ShapeDtypeStruct((rows, lanes), jnp.int32),
        in_specs=[SMEM] * 4,
        out_specs=VMEM,
        compiler_params=params(4),
        cost_estimate=cost(0, 4 * rows * lanes),
    )(*routing)


def down_kernel(rank, places, found_ref, rows_ref, *refs):
    groups = len(places)
    pieces = refs[:groups]
    out_ref, whole, sems = refs[-3:]
    copies = []
    for dist in range(groups):
        copy = pltpu.make_async_copy(
            pieces[dist].at[pl.ds(places[dist] * rank, rank)], whole.at[pl.ds(dist * rank, rank)], sems.at[dist]
        )
        copy.start()
        copies.append(copy)
    shape = (rows_ref.shape[0], 2 * rank)
    found = found_ref[...]
    high = (lax.broadcasted_iota(jnp.int32, shape, 1) >= rank).astype(jnp.int32)
    for copy in copies:
        copy.wait()
    full = lax.dot_general(
        rows_ref[...], whole[...], (((1,), (1,)), ((), ())), preferred_element_type=jnp.float32
    )
    picked = jnp.zeros(shape, jnp.float32)
    for pair in range(groups // 2):
        piece = full[:, pair * 2 * rank : (pair + 1) * 2 * rank]
        picked = picked + jnp.where(found == 2 * pair + high, piece, 0.0)
    out_ref[...] = picked + pltpu.roll(picked, rank, 1)


def down(found, rank, rows_in, pieces, order=()):
    rows, width = rows_in.shape
    groups = len(pieces)
    return pl.pallas_call(
        functools.partial(down_kernel, rank, [row for _, row in pieces]),
        out_shape=jax.ShapeDtypeStruct((rows, 2 * rank), jnp.float32),
        in_specs=[VMEM] * 2 + [ANY] * (groups + len(order)),
        out_specs=VMEM,
        scratch_shapes=[
            pltpu.VMEM((groups * rank, width), rows_in.dtype),
            pltpu.SemaphoreType.DMA((groups,)),
        ],
        compiler_params=params(12),
        cost_estimate=cost(2 * rows * width * groups * rank, 2 * rows * width + 2 * groups * rank * width),
    )(found, rows_in, *[piece for piece, _ in pieces], *order)


def up_kernel(dists, split, found_ref, down_ref, *refs):
    groups = len(dists)
    pieces = refs[:groups]
    bases = refs[groups : groups + split]
    outs = refs[groups + split : groups + 2 * split]
    terms = refs[-1]
    rank = pieces[0].shape[0]
    rows = down_ref.shape[0]

    @pl.when(pl.program_id(0) == 0)
    def _():
        shape = (rows, 2 * rank)
        found = found_ref[...]
        low = lax.broadcasted_iota(jnp.int32, shape, 1) < rank
        both = down_ref[...] * ADAPTER_SCALE
        first = both.astype(jnp.bfloat16)
        second = (both - first.astype(jnp.float32)).astype(jnp.bfloat16)
        for number, term in enumerate((first, second)):
            for pair in range(groups // 2):
                wanted = jnp.where(low, dists[2 * pair], dists[2 * pair + 1])
                chosen = jnp.where(found == wanted, term.astype(jnp.float32), 0.0)
                start = number * groups * rank + pair * 2 * rank
                terms[:, start : start + 2 * rank] = chosen.astype(jnp.bfloat16)

    whole = jnp.concatenate([piece[...] for piece in pieces] * 2, axis=0)
    total = jnp.dot(terms[...], whole, preferred_element_type=jnp.float32)
    size = rows // split
    for number in range(split):
        value = bases[number][...] + total[number * size : (number + 1) * size]
        outs[number][...] = value.astype(outs[number].dtype)


def up(found, rank, downs, used, dists, bases, out_dtype):
    pieces = [used[dist] for dist in dists]
    groups = len(dists)
    width = pieces[0][0].shape[1]
    rows = downs.shape[0]
    split = len(bases)
    tile = min(512, width)
    column = lambda step: (0, step)
    size = rows // split
    piece_specs = [
        pl.BlockSpec((rank, tile), functools.partial(lambda place, step: (place, step), place)) for _, place in pieces
    ]
    return pl.pallas_call(
        functools.partial(up_kernel, dists, split),
        grid=(width // tile,),
        out_shape=[jax.ShapeDtypeStruct((size, width), out_dtype)] * split,
        in_specs=[pl.BlockSpec(downs.shape, lambda step: (0, 0))] * 2
        + piece_specs
        + [pl.BlockSpec((size, tile), column)] * split,
        out_specs=[pl.BlockSpec((size, tile), column)] * split,
        scratch_shapes=[pltpu.VMEM((rows, 2 * groups * rank), jnp.bfloat16)],
        compiler_params=params(16),
        cost_estimate=cost(4 * rows * width * groups * rank, 8 * rows * width + 2 * groups * rank * width),
    )(found, downs, *[piece for piece, _ in pieces], *bases)


def tile_of(width):
    return min(512, width)


def encode(value, out_ref, step):
    half, tile = value.shape
    width = out_ref.shape[1] - LANES
    peak = jnp.max(jnp.abs(value), axis=1, keepdims=True)
    level = jnp.ceil(jnp.log(jnp.maximum(peak, 1e-30)) * (LEVELS / math.log(2.0)))
    coded = jnp.round(value * (jnp.exp2(level * (-1.0 / LEVELS)) * STEPS))
    coded = jnp.minimum(jnp.maximum(coded, -STEPS), STEPS)
    start = step * tile if isinstance(step, int) else pl.multiple_of(step * tile, tile)
    out_ref[:, pl.ds(start, tile)] = coded.astype(jnp.int32).astype(jnp.int16)
    lane = lax.broadcasted_iota(jnp.int32, (half, LANES), 1)
    kept = jnp.where(lane < step, out_ref[:, width:].astype(jnp.int32), 0)
    out_ref[:, width:] = jnp.where(lane == step, level.astype(jnp.int32), kept).astype(jnp.int16)


def decode(coded_ref, row, half, step, tile):
    width = coded_ref.shape[1] - LANES
    levels = coded_ref[row : row + half, width:].astype(jnp.int32)
    lane = lax.broadcasted_iota(jnp.int32, levels.shape, 1)
    level = jnp.sum(jnp.where(lane == step, levels, 0).astype(jnp.float32), axis=1, keepdims=True)
    value = coded_ref[row : row + half, step * tile : (step + 1) * tile].astype(jnp.int32).astype(jnp.float32)
    return value * (jnp.exp2(level * (1.0 / LEVELS)) * (1.0 / STEPS))


def merge_kernel(places, coded_out, *refs):
    out_ref = refs[-1]
    inputs = refs[:-1]
    for number, rows in enumerate(places):
        base, coded = inputs[0], inputs[1 : 1 + len(rows)]
        inputs = inputs[1 + len(rows) :]
        half, width = base.shape
        tile = tile_of(width)
        for step in range(width // tile):
            columns = slice(step * tile, (step + 1) * tile)
            total = base[:, columns]
            for one, row in zip(coded, rows):
                total = total + decode(one, row, half, step, tile)
            if coded_out:
                encode(total, out_ref, step)
            else:
                out_ref[number * half : (number + 1) * half, columns] = total.astype(out_ref.dtype)


def merge(sums, coded_out):
    half, width = sums[0][0].shape
    places = [[row for _, row in coded] for _, coded in sums]
    if coded_out:
        out_shape = jax.ShapeDtypeStruct((half, width + LANES), jnp.int16)
    else:
        out_shape = jax.ShapeDtypeStruct((len(sums) * half, width), jnp.bfloat16)
    values = []
    for base, coded in sums:
        values = values + [base] + [value for value, _ in coded]
    return pl.pallas_call(
        functools.partial(merge_kernel, places, coded_out),
        out_shape=out_shape,
        in_specs=[VMEM] * len(values),
        out_specs=VMEM,
        compiler_params=params(20),
        cost_estimate=cost(0, 2 * sum(value.size for value in values) + 4 * half * width),
    )(*values)


def o_kernel(block_ref, rows_ref, weight_ref, *refs):
    del block_ref
    outs = refs[-2:]
    total = jnp.dot(rows_ref[...], weight_ref[...], preferred_element_type=jnp.float32)
    half = outs[0].shape[0]
    for number, out_ref in enumerate(outs):
        value = total[number * half : (number + 1) * half]
        if out_ref.dtype == jnp.int16:
            encode(value, out_ref, pl.program_id(0))
        else:
            out_ref[...] = value


def o_block(block, rows_in, weight, width, leaving):
    rows, depth = rows_in.shape
    half = rows // 2
    tile = tile_of(width)
    tiles = width // tile
    shapes, specs, buffers, aliases = [], [], [], {}
    for number, one in enumerate(leaving):
        if one is None:
            shapes.append(jax.ShapeDtypeStruct((half, width), jnp.float32))
            specs.append(pl.BlockSpec((half, tile), lambda step, ref: (0, step)))
            continue
        buffer, place, places = one
        shapes.append(jax.ShapeDtypeStruct((places * half, width + LANES), jnp.int16))
        specs.append(
            pl.BlockSpec((half, width + LANES), functools.partial(lambda place, step, ref: (place, 0), place))
        )
        if buffer is not None:
            aliases[3 + len(buffers)] = number
            buffers.append(buffer)
    return pl.pallas_call(
        o_kernel,
        grid_spec=pltpu.PrefetchScalarGridSpec(
            num_scalar_prefetch=1,
            grid=(tiles,),
            in_specs=[
                pl.BlockSpec((rows, depth), lambda step, ref: (0, 0)),
                pl.BlockSpec((depth, tile), lambda step, ref: (0, ref[0] * tiles + step)),
            ]
            + [ANY] * len(buffers),
            out_specs=specs,
        ),
        out_shape=shapes,
        input_output_aliases=aliases,
        compiler_params=params(36),
        cost_estimate=cost(2 * rows * depth * width, 2 * depth * width + 2 * rows * depth + 4 * rows * width),
    )(block, rows_in, weight, *buffers)


def q_kernel(count, has_total, block_ref, *refs):
    del block_ref
    pieces = refs[:count]
    weight_ref = refs[count]
    out_ref, token_ref = refs[-2:]
    size = pieces[0].shape[0]
    token_ref[...] = jnp.zeros_like(token_ref)
    for number, rows_ref in enumerate(pieces):
        total = jnp.dot(rows_ref[...], weight_ref[...], preferred_element_type=jnp.float32)
        span = slice(number * size, (number + 1) * size)
        if has_total:
            total = total + refs[count + 1][span]
        out_ref[span] = total


def q_block(block, pieces, weight, total):
    count = len(pieces)
    size, depth = pieces[0].shape
    rows = count * size
    width = weight.shape[1]
    tile = tile_of(width)
    has_total = total is not None
    column = pl.BlockSpec((rows, tile), lambda step, ref: (0, step))
    return pl.pallas_call(
        functools.partial(q_kernel, count, has_total),
        grid_spec=pltpu.PrefetchScalarGridSpec(
            num_scalar_prefetch=1,
            grid=(width // tile,),
            in_specs=[pl.BlockSpec((size, depth), lambda step, ref: (0, 0))] * count
            + [pl.BlockSpec((depth, tile), lambda step, ref: (ref[0], step))]
            + [column] * has_total,
            out_specs=[column, pl.BlockSpec((8, LANES), lambda step, ref: (0, 0))],
        ),
        out_shape=[jax.ShapeDtypeStruct((rows, width), jnp.float32), jax.ShapeDtypeStruct((8, LANES), jnp.float32)],
        input_output_aliases={count + 2: 0} if has_total else {},
        compiler_params=params(36),
        cost_estimate=cost(2 * rows * depth * width, 2 * depth * width + 2 * rows * depth + 8 * rows * width),
    )(block, *pieces, weight, *([total] * has_total))


def share(block, chains, *pins):
    whole = {0: block}
    for bit in chains:
        whole[bit] = chains[bit].send(block, bit, *pins)
    return whole


def forward(whole, chains, *pins):
    order = list(chains)
    half = whole[0].shape[0] // 2
    parts = [{}, {}]
    for step in range(len(order)):
        for number in range(2):
            bits_used = order if number == 0 else order[::-1]
            bit = bits_used[step]
            held = [0]
            for used in bits_used[:step]:
                held = held + [dist ^ used for dist in held]
            for dist in held[1:]:
                if dist in whole:
                    piece = whole[dist][number * half : (number + 1) * half]
                else:
                    piece = parts[number][dist]
                parts[number][dist ^ bit] = chains[bit].send(piece, bit, *pins)
    pieces = {dist: [value] for dist, value in whole.items()}
    for dist in parts[0]:
        pieces[dist] = [parts[0][dist], parts[1][dist]]
    return pieces


def place_kernel(blocks, column_ref, *refs):
    out_ref, sems = refs[-2:]
    width = refs[0].shape[1]
    copies = []
    number = 0
    for block, count in enumerate(blocks):
        start = pl.multiple_of(column_ref[block] * width, width)
        for part in range(count):
            size = refs[number].shape[0]
            copy = pltpu.make_async_copy(
                refs[number], out_ref.at[pl.ds(part * size, size), pl.ds(start, width)], sems.at[number]
            )
            copy.start()
            copies.append(copy)
            number += 1
    for copy in copies:
        copy.wait()


def place(columns, blocks, into, out_shape):
    counts = [len(pieces) for pieces in blocks]
    pieces = [piece for block in blocks for piece in block]
    old = [] if into is None else [into]
    return pl.pallas_call(
        functools.partial(place_kernel, counts),
        out_shape=out_shape,
        in_specs=[SMEM] + [VMEM] * len(pieces) + [ANY] * len(old),
        out_specs=ANY,
        scratch_shapes=[pltpu.SemaphoreType.DMA((len(pieces),))],
        input_output_aliases={len(pieces) + 1: 0} if old else {},
        compiler_params=params(10),
        cost_estimate=cost(0, 4 * sum(piece.size for piece in pieces)),
    )(columns, *pieces, *old)


def body(
    hidden_rows,
    attn_rows,
    q_weight,
    o_weight,
    owner_table,
    group_adapters,
    req_slot,
    req_len,
    qa_store,
    qb_store,
    oa_store,
    ob_store,
):
    groups = lax.axis_size("group")
    size = lax.axis_size("tensor")
    mine = lax.axis_index("tensor")
    held, _, rank = qa_store.shape
    rows, _ = hidden_rows.shape
    width = o_weight.shape[1] // size
    half = rows // 2
    routing = (owner_table, group_adapters, req_slot, req_len)
    block = [jnp.reshape(mine ^ dist, (1,)).astype(jnp.int32) for dist in range(size)]
    order = bits(size)

    far = Groups("group", [groups // 2 * 4 * part // 16 for part in (2, 3, 5, 7, 8, 10, 12, 14, 16)])
    near = Chain("group")
    chains = {bit: Chain("tensor") for bit in order}
    far_dists = list(range(groups // 2, groups))
    near_dists = list(range(2, groups // 2))
    all_dists = list(range(groups))
    stores = [jnp.swapaxes(oa_store, 1, 2), ob_store, jnp.swapaxes(qa_store, 1, 2), qb_store]
    used = [{}, {}, {}, {}]

    def packed(plan, mebibytes, *pins):
        wanted = sorted({part for _, parts in plan for part in parts})
        plan = [(dist, [wanted.index(part) for part in parts]) for dist, parts in plan]
        return pack(plan, owner_table, group_adapters, [stores[part] for part in wanted], pins, mebibytes)

    def fetch_far(values, part, dists, *pins):
        for value, dist in zip(values, dists):
            used[part][dist] = (far.send(value, dist, *pins), 0)

    def fetch_near(values, parts, pins, dists):
        for value, dist, some in zip(values, dists, pins):
            arrived = near.send(value, dist, *some)
            for row, part in enumerate(parts):
                used[part][dist] = (arrived, row)

    def pieces_of(part, dists):
        return [used[part][dist] for dist in dists]

    def arrivals():
        return [chain.done[-1] for chain in chains.values()]

    def summed(value, *pins):
        arrived = send(after(value, *pins) if pins else value, "tensor", order[0])
        return value + arrived, arrived

    def summed_on(value, *pins):
        for bit in order[1:]:
            value = value + send(after(value, *pins) if pins else value, "tensor", bit)
        return value

    halving = (order, order[::-1])
    leaving = [sorted((dist for dist in range(size) if dist & halving[number][0]), reverse=True) for number in range(2)]
    buffers = [None, None]
    sums = [{}, {}]

    def o_sums(dist):
        wanted = []
        for number in range(2):
            if dist in leaving[number]:
                wanted.append((buffers[number], leaving[number].index(dist), len(leaving[number])))
            else:
                wanted.append(None)
        values = o_block(block[dist], attn_rows, o_weight, width, wanted)
        for number in range(2):
            if wanted[number] is None:
                sums[number][dist] = (values[number], [])
            else:
                buffers[number] = values[number]

    def reduce_first(*pins):
        for number in range(2):
            bit = halving[number][0]
            arrived = chains[bit].send(buffers[number], bit, *pins)
            for row, dist in enumerate(leaving[number]):
                sums[number][dist ^ bit][1].append((arrived, row * half))

    def reduce_step(step, *pins):
        for number in range(2):
            bit = halving[number][step]
            for dist in sorted((one for one in sums[number] if one & bit), reverse=True):
                arrived = chains[bit].send(merge([sums[number].pop(dist)], True), bit, *pins)
                sums[number][dist ^ bit][1].append((arrived, 0))

    hidden = share(hidden_rows, chains)
    lead, rest = far_dists[:3], far_dists[3:]
    values = packed([(dist, (0,)) for dist in lead] + [(near_dists[0], (0, 1))], 60)
    fetch_far(values[:2], 0, lead[:2])
    third = values[2:3]
    near_values = list(values[3:])
    plan = [(dist, (0,)) for dist in rest] + [(dist, (1,)) for dist in far_dists]
    plan = plan + [(dist, (0, 1)) for dist in near_dists[1:]] + [(1, (0, 1, 2, 3)), (0, (0, 1, 2, 3))]
    o_values = packed(plan, 60, *values)
    found = row_distances(routing, held, rows, 2 * rank)
    dists = sorted(range(1, size), reverse=True)
    for dist in dists[:-1]:
        o_sums(dist)
    pins = [found, *[buffer for buffer in buffers if buffer is not None]]
    fetch_near(near_values, (0, 1), [[*far.upto(0), *pins]], near_dists)
    fetch_far(third, 0, lead[2:], o_values[0], *pins)
    o_sums(dists[-1])
    beside = send(after(o_values[-2], *far.upto(0), *pins), "group", 1)
    for part in range(4):
        used[part][1] = (beside, part)
        used[part][0] = (o_values[-1], part)

    fetch_far(o_values, 0, rest)
    fetch_far(o_values[len(rest) :], 1, far_dists[:-1])
    fetch_near(o_values[len(rest) + len(far_dists) : -2], (0, 1), [far.upto(1)], near_dists[1:])
    hidden = forward(hidden, chains, *far.upto(1), beside, *buffers)
    o_sums(0)
    q_total = None
    q_ready = []
    for dist in range(size):
        q_total, token = q_block(block[dist], hidden[dist], q_weight, q_total)
        q_ready.append(token)
    plan = [(dist, (part,)) for part in (2, 3) for dist in far_dists] + [(dist, (2, 3)) for dist in near_dists]
    values = packed(plan, 10, *far.upto(1))

    reduce_first(*far.upto(2), *near.done[1:], sums[0][0][0], values[0], *q_ready[:1])
    fetch_near(values[2 * len(far_dists) :], (2, 3), [far.upto(2), far.upto(5)], near_dists)
    o_half = down(found, rank, attn_rows, pieces_of(0, all_dists), q_ready[1 : size // 2 + 1])
    last = len(rest) + len(far_dists) - 1
    fetch_far(o_values[last : last + 1], 1, far_dists[-1:], o_half)
    fetch_far(values, 2, far_dists)
    fetch_far(values[len(far_dists) :], 3, far_dists)
    o_down, o_arrived = summed(o_half, *far.upto(3))
    pins = [*far.upto(4), near.done[len(near_dists)], o_arrived]
    o_down = summed_on(o_down, *arrivals())
    for step in range(1, len(order)):
        reduce_step(step, *pins)
    bases = up(found, rank, o_down, used[1], all_dists, [one[0][0] for one in sums], jnp.float32)
    rounded = merge([(base, one[0][1]) for base, one in zip(bases, sums)], False)

    finished = share(rounded, chains, *far.upto(5), q_ready[-1])
    q_half = down(after(found, o_down), rank, hidden_rows, pieces_of(2, all_dists))
    q_down = summed_on(summed(q_half)[0])

    finished = forward(finished, chains, *far.upto(7), q_down)

    out_shape = jax.ShapeDtypeStruct((rows, width * size), jnp.bfloat16)
    soon = [dist for dist in range(size) if len(finished[dist]) == 1]
    late = [dist for dist in range(size) if len(finished[dist]) > 1]

    def placed(dists, into):
        columns = jnp.concatenate([block[dist] for dist in dists])
        return place(columns, [finished[dist] for dist in dists], into, out_shape)

    attn_out = placed(soon, None)
    last = far_dists[-2:]
    first = [dist for dist in all_dists if dist not in last]
    (total,) = up(found, rank, q_down, used[3], first, [after(q_total, attn_out)], jnp.float32)
    attn_out = placed(late, attn_out)
    (queries,) = up(found, rank, q_down, used[3], last, [after(total, attn_out)], jnp.bfloat16)
    return (queries, attn_out)


def solution(mesh):
    return jax.shard_map(
        body,
        mesh=mesh,
        in_specs=(
            P("group", "tensor"),
            P("group", "tensor"),
            P(None, "tensor"),
            P("tensor", None),
            P(),
            P(),
            P("group", None),
            P("group", None),
            P("group", "tensor", None),
            P("group", None, "tensor"),
            P("group", "tensor", None),
            P("group", None, "tensor"),
        ),
        out_specs=(P("group", "tensor"), P("group", None)),
        check_vma=False,
    )
```

```python
import functools
import math

import jax
import jax.numpy as jnp
from jax import lax
from jax.experimental import pallas as pl
from jax.experimental.pallas import tpu as pltpu
from jax.sharding import PartitionSpec as P

ADAPTER_SCALE = 0.5
LANES = 128
LEVELS = 8
STEPS = 32767.0
MIB = 1024 * 1024
ANY = pl.BlockSpec(memory_space=pl.ANY)
SMEM = pl.BlockSpec(memory_space=pltpu.SMEM)
VMEM = pl.BlockSpec(memory_space=pltpu.VMEM)
HBM = pl.BlockSpec(memory_space=pltpu.HBM)


def params(mebibytes):
    return pltpu.CompilerParams(vmem_limit_bytes=mebibytes * MIB)


def cost(flops, nbytes):
    return pl.CostEstimate(flops=flops // 1000, bytes_accessed=nbytes // 1000, transcendentals=0)


def send(value, axis, offset):
    size = lax.axis_size(axis)
    return lax.ppermute(value, axis, [(i, i ^ offset) for i in range(size)])


def after(value, *others):
    return lax.optimization_barrier((value, *others))[0]


def at(values, *numbers):
    return [values[number] for number in numbers if number < len(values)]


class Chain:
    def __init__(self, axis):
        self.axis = axis
        self.done = []

    def send(self, value, offset, *pins):
        pins = (*self.done[-1:], *pins)
        if pins:
            value = after(value, *pins)
        arrived = send(value, self.axis, offset)
        self.done.append(arrived)
        return arrived


class Groups:
    def __init__(self, axis, ends):
        self.axis = axis
        self.ends = ends
        self.done = []

    def upto(self, step):
        start = self.ends[step - 1] if step else 0
        return self.done[start : self.ends[step]]

    def send(self, value, offset, *pins):
        number = len(self.done)
        step = sum(end <= number for end in self.ends)
        if step:
            value = after(value, *self.upto(step - 1), *pins)
        arrived = send(value, self.axis, offset)
        self.done.append(arrived)
        return arrived


def bits(size):
    out = []
    bit = 1
    while bit < size:
        out.append(bit)
        bit *= 2
    return out


def pack_kernel(plan, count, table_ref, adapters_ref, *refs):
    stores = refs[:count]
    outs = refs[-3 - len(plan) : -3]
    staged, in_sems, out_sems = refs[-3:]
    slots = adapters_ref.shape[1]
    held, rank, _ = stores[0].shape
    me = lax.axis_index("group")
    loads = []
    for dist, parts in plan:
        dest = me ^ dist
        pick = jnp.int32(0)
        for slot in range(slots):
            place = table_ref[adapters_ref[dest, slot]]
            owner = lax.div(place, jnp.int32(held))
            pick = jnp.where(owner == me, place - owner * held, pick)
        for part in parts:
            number = len(loads)
            load = pltpu.make_async_copy(stores[part].at[pick], staged.at[number], in_sems.at[number])
            load.start()
            loads.append(load)
    copies = []
    for out_ref, (_, parts) in zip(outs, plan):
        for row in range(len(parts)):
            number = len(copies)
            loads[number].wait()
            copy = pltpu.make_async_copy(
                staged.at[number], out_ref.at[pl.ds(row * rank, rank)], out_sems.at[number]
            )
            copy.start()
            copies.append(copy)
    for copy in copies:
        copy.wait()


def pack(plan, table, adapters, stores, order, mebibytes):
    _, rank, width = stores[0].shape
    dtype = stores[0].dtype
    total = sum(len(parts) for _, parts in plan)
    return pl.pallas_call(
        functools.partial(pack_kernel, plan, len(stores)),
        out_shape=[pltpu.HBM((len(parts) * rank, width), dtype) for _, parts in plan],
        in_specs=[SMEM, SMEM] + [HBM] * len(stores) + [ANY] * len(order),
        out_specs=[HBM] * len(plan),
        scratch_shapes=[
            pltpu.VMEM((total, rank, width), dtype),
            pltpu.SemaphoreType.DMA((total,)),
            pltpu.SemaphoreType.DMA((total,)),
        ],
        compiler_params=params(mebibytes),
        cost_estimate=cost(0, 4 * total * rank * width),
    )(table, adapters, *stores, *order)


def distance_kernel(held, table_ref, adapters_ref, slot_ref, len_ref, out_ref):
    me = lax.axis_index("group")
    position = lax.broadcasted_iota(jnp.int32, out_ref.shape, 0)
    found = jnp.zeros(out_ref.shape, jnp.int32)
    start = jnp.int32(0)
    for req in range(len_ref.shape[1]):
        place = table_ref[adapters_ref[me, slot_ref[0, req]]]
        dist = lax.div(place, jnp.int32(held)) ^ me
        end = start + len_ref[0, req]
        found = jnp.where((position >= start) & (position < end), dist, found)
        start = end
    out_ref[...] = found


def row_distances(routing, held, rows, lanes):
    return pl.pallas_call(
        functools.partial(distance_kernel, held),
        out_shape=jax.ShapeDtypeStruct((rows, lanes), jnp.int32),
        in_specs=[SMEM] * 4,
        out_specs=VMEM,
        compiler_params=params(4),
        cost_estimate=cost(0, 4 * rows * lanes),
    )(*routing)


def down_kernel(rank, places, found_ref, rows_ref, *refs):
    groups = len(places)
    pieces = refs[:groups]
    out_ref, whole, sems = refs[-3:]
    copies = []
    for dist in range(groups):
        copy = pltpu.make_async_copy(
            pieces[dist].at[pl.ds(places[dist] * rank, rank)], whole.at[pl.ds(dist * rank, rank)], sems.at[dist]
        )
        copy.start()
        copies.append(copy)
    shape = (rows_ref.shape[0], 2 * rank)
    found = found_ref[...]
    high = (lax.broadcasted_iota(jnp.int32, shape, 1) >= rank).astype(jnp.int32)
    for copy in copies:
        copy.wait()
    full = lax.dot_general(
        rows_ref[...], whole[...], (((1,), (1,)), ((), ())), preferred_element_type=jnp.float32
    )
    picked = jnp.zeros(shape, jnp.float32)
    for pair in range(groups // 2):
        piece = full[:, pair * 2 * rank : (pair + 1) * 2 * rank]
        picked = picked + jnp.where(found == 2 * pair + high, piece, 0.0)
    out_ref[...] = picked + pltpu.roll(picked, rank, 1)


def down(found, rank, rows_in, pieces, order=()):
    rows, width = rows_in.shape
    groups = len(pieces)
    return pl.pallas_call(
        functools.partial(down_kernel, rank, [row for _, row in pieces]),
        out_shape=jax.ShapeDtypeStruct((rows, 2 * rank), jnp.float32),
        in_specs=[VMEM] * 2 + [ANY] * (groups + len(order)),
        out_specs=VMEM,
        scratch_shapes=[
            pltpu.VMEM((groups * rank, width), rows_in.dtype),
            pltpu.SemaphoreType.DMA((groups,)),
        ],
        compiler_params=params(12),
        cost_estimate=cost(2 * rows * width * groups * rank, 2 * rows * width + 2 * groups * rank * width),
    )(found, rows_in, *[piece for piece, _ in pieces], *order)


def up_kernel(dists, split, found_ref, down_ref, *refs):
    groups = len(dists)
    pieces = refs[:groups]
    bases = refs[groups : groups + split]
    outs = refs[groups + split : groups + 2 * split]
    terms = refs[-1]
    rank = pieces[0].shape[0]
    rows = down_ref.shape[0]

    @pl.when(pl.program_id(0) == 0)
    def _():
        shape = (rows, 2 * rank)
        found = found_ref[...]
        low = lax.broadcasted_iota(jnp.int32, shape, 1) < rank
        both = down_ref[...] * ADAPTER_SCALE
        first = both.astype(jnp.bfloat16)
        second = (both - first.astype(jnp.float32)).astype(jnp.bfloat16)
        for number, term in enumerate((first, second)):
            for pair in range(groups // 2):
                wanted = jnp.where(low, dists[2 * pair], dists[2 * pair + 1])
                chosen = jnp.where(found == wanted, term.astype(jnp.float32), 0.0)
                start = number * groups * rank + pair * 2 * rank
                terms[:, start : start + 2 * rank] = chosen.astype(jnp.bfloat16)

    whole = jnp.concatenate([piece[...] for piece in pieces] * 2, axis=0)
    total = jnp.dot(terms[...], whole, preferred_element_type=jnp.float32)
    size = rows // split
    for number in range(split):
        value = bases[number][...] + total[number * size : (number + 1) * size]
        outs[number][...] = value.astype(outs[number].dtype)


def up(found, rank, downs, used, dists, bases, out_dtype):
    pieces = [used[dist] for dist in dists]
    groups = len(dists)
    width = pieces[0][0].shape[1]
    rows = downs.shape[0]
    split = len(bases)
    tile = min(512, width)
    column = lambda step: (0, step)
    size = rows // split
    piece_specs = [
        pl.BlockSpec((rank, tile), functools.partial(lambda place, step: (place, step), place)) for _, place in pieces
    ]
    return pl.pallas_call(
        functools.partial(up_kernel, dists, split),
        grid=(width // tile,),
        out_shape=[jax.ShapeDtypeStruct((size, width), out_dtype)] * split,
        in_specs=[pl.BlockSpec(downs.shape, lambda step: (0, 0))] * 2
        + piece_specs
        + [pl.BlockSpec((size, tile), column)] * split,
        out_specs=[pl.BlockSpec((size, tile), column)] * split,
        scratch_shapes=[pltpu.VMEM((rows, 2 * groups * rank), jnp.bfloat16)],
        compiler_params=params(16),
        cost_estimate=cost(4 * rows * width * groups * rank, 8 * rows * width + 2 * groups * rank * width),
    )(found, downs, *[piece for piece, _ in pieces], *bases)


def tile_of(width):
    return min(512, width)


def encode(value, out_ref, step):
    half, tile = value.shape
    width = out_ref.shape[1] - LANES
    peak = jnp.max(jnp.abs(value), axis=1, keepdims=True)
    level = jnp.ceil(jnp.log(jnp.maximum(peak, 1e-30)) * (LEVELS / math.log(2.0)))
    coded = jnp.round(value * (jnp.exp2(level * (-1.0 / LEVELS)) * STEPS))
    coded = jnp.minimum(jnp.maximum(coded, -STEPS), STEPS)
    start = step * tile if isinstance(step, int) else pl.multiple_of(step * tile, tile)
    out_ref[:, pl.ds(start, tile)] = coded.astype(jnp.int32).astype(jnp.int16)
    lane = lax.broadcasted_iota(jnp.int32, (half, LANES), 1)
    kept = jnp.where(lane < step, out_ref[:, width:].astype(jnp.int32), 0)
    out_ref[:, width:] = jnp.where(lane == step, level.astype(jnp.int32), kept).astype(jnp.int16)


def decode(coded_ref, row, half, step, tile):
    width = coded_ref.shape[1] - LANES
    levels = coded_ref[row : row + half, width:].astype(jnp.int32)
    lane = lax.broadcasted_iota(jnp.int32, levels.shape, 1)
    level = jnp.sum(jnp.where(lane == step, levels, 0).astype(jnp.float32), axis=1, keepdims=True)
    value = coded_ref[row : row + half, step * tile : (step + 1) * tile].astype(jnp.int32).astype(jnp.float32)
    return value * (jnp.exp2(level * (1.0 / LEVELS)) * (1.0 / STEPS))


def merge_kernel(places, coded_out, *refs):
    out_ref = refs[-1]
    inputs = refs[:-1]
    for number, rows in enumerate(places):
        base, coded = inputs[0], inputs[1 : 1 + len(rows)]
        inputs = inputs[1 + len(rows) :]
        half, width = base.shape
        tile = tile_of(width)
        for step in range(width // tile):
            columns = slice(step * tile, (step + 1) * tile)
            total = base[:, columns]
            for one, row in zip(coded, rows):
                total = total + decode(one, row, half, step, tile)
            if coded_out:
                encode(total, out_ref, step)
            else:
                out_ref[number * half : (number + 1) * half, columns] = total.astype(out_ref.dtype)


def merge(sums, coded_out):
    half, width = sums[0][0].shape
    places = [[row for _, row in coded] for _, coded in sums]
    if coded_out:
        out_shape = jax.ShapeDtypeStruct((half, width + LANES), jnp.int16)
    else:
        out_shape = jax.ShapeDtypeStruct((len(sums) * half, width), jnp.bfloat16)
    values = []
    for base, coded in sums:
        values = values + [base] + [value for value, _ in coded]
    return pl.pallas_call(
        functools.partial(merge_kernel, places, coded_out),
        out_shape=out_shape,
        in_specs=[VMEM] * len(values),
        out_specs=VMEM,
        compiler_params=params(20),
        cost_estimate=cost(0, 2 * sum(value.size for value in values) + 4 * half * width),
    )(*values)


def o_kernel(block_ref, rows_ref, weight_ref, *refs):
    del block_ref
    outs = refs[-2:]
    total = jnp.dot(rows_ref[...], weight_ref[...], preferred_element_type=jnp.float32)
    half = outs[0].shape[0]
    for number, out_ref in enumerate(outs):
        value = total[number * half : (number + 1) * half]
        if out_ref.dtype == jnp.int16:
            encode(value, out_ref, pl.program_id(0))
        else:
            out_ref[...] = value


def o_block(block, rows_in, weight, width, leaving):
    rows, depth = rows_in.shape
    half = rows // 2
    tile = tile_of(width)
    tiles = width // tile
    shapes, specs, buffers, aliases = [], [], [], {}
    for number, one in enumerate(leaving):
        if one is None:
            shapes.append(jax.ShapeDtypeStruct((half, width), jnp.float32))
            specs.append(pl.BlockSpec((half, tile), lambda step, ref: (0, step)))
            continue
        buffer, place, places = one
        shapes.append(jax.ShapeDtypeStruct((places * half, width + LANES), jnp.int16))
        specs.append(
            pl.BlockSpec((half, width + LANES), functools.partial(lambda place, step, ref: (place, 0), place))
        )
        if buffer is not None:
            aliases[3 + len(buffers)] = number
            buffers.append(buffer)
    return pl.pallas_call(
        o_kernel,
        grid_spec=pltpu.PrefetchScalarGridSpec(
            num_scalar_prefetch=1,
            grid=(tiles,),
            in_specs=[
                pl.BlockSpec((rows, depth), lambda step, ref: (0, 0)),
                pl.BlockSpec((depth, tile), lambda step, ref: (0, ref[0] * tiles + step)),
            ]
            + [ANY] * len(buffers),
            out_specs=specs,
        ),
        out_shape=shapes,
        input_output_aliases=aliases,
        compiler_params=params(36),
        cost_estimate=cost(2 * rows * depth * width, 2 * depth * width + 2 * rows * depth + 4 * rows * width),
    )(block, rows_in, weight, *buffers)


def q_kernel(count, has_total, block_ref, *refs):
    del block_ref
    pieces = refs[:count]
    weight_ref = refs[count]
    out_ref, token_ref = refs[-2:]
    size = pieces[0].shape[0]
    token_ref[...] = jnp.zeros_like(token_ref)
    for number, rows_ref in enumerate(pieces):
        total = jnp.dot(rows_ref[...], weight_ref[...], preferred_element_type=jnp.float32)
        span = slice(number * size, (number + 1) * size)
        if has_total:
            total = total + refs[count + 1][span]
        out_ref[span] = total


def q_block(block, pieces, weight, total):
    count = len(pieces)
    size, depth = pieces[0].shape
    rows = count * size
    width = weight.shape[1]
    tile = tile_of(width)
    has_total = total is not None
    column = pl.BlockSpec((rows, tile), lambda step, ref: (0, step))
    return pl.pallas_call(
        functools.partial(q_kernel, count, has_total),
        grid_spec=pltpu.PrefetchScalarGridSpec(
            num_scalar_prefetch=1,
            grid=(width // tile,),
            in_specs=[pl.BlockSpec((size, depth), lambda step, ref: (0, 0))] * count
            + [pl.BlockSpec((depth, tile), lambda step, ref: (ref[0], step))]
            + [column] * has_total,
            out_specs=[column, pl.BlockSpec((8, LANES), lambda step, ref: (0, 0))],
        ),
        out_shape=[jax.ShapeDtypeStruct((rows, width), jnp.float32), jax.ShapeDtypeStruct((8, LANES), jnp.float32)],
        input_output_aliases={count + 2: 0} if has_total else {},
        compiler_params=params(36),
        cost_estimate=cost(2 * rows * depth * width, 2 * depth * width + 2 * rows * depth + 8 * rows * width),
    )(block, *pieces, weight, *([total] * has_total))


def share(block, chains, *pins):
    whole = {0: block}
    for bit in chains:
        whole[bit] = chains[bit].send(block, bit, *pins)
    return whole


def forward(whole, chains, *pins):
    order = list(chains)
    half = whole[0].shape[0] // 2
    parts = [{}, {}]
    for step in range(len(order)):
        for number in range(2):
            bits_used = order if number == 0 else order[::-1]
            bit = bits_used[step]
            held = [0]
            for used in bits_used[:step]:
                held = held + [dist ^ used for dist in held]
            for dist in held[1:]:
                if dist in whole:
                    piece = whole[dist][number * half : (number + 1) * half]
                else:
                    piece = parts[number][dist]
                parts[number][dist ^ bit] = chains[bit].send(piece, bit, *pins)
    pieces = {dist: [value] for dist, value in whole.items()}
    for dist in parts[0]:
        pieces[dist] = [parts[0][dist], parts[1][dist]]
    return pieces


def place_kernel(blocks, column_ref, *refs):
    out_ref, sems = refs[-2:]
    width = refs[0].shape[1]
    copies = []
    number = 0
    for block, count in enumerate(blocks):
        start = pl.multiple_of(column_ref[block] * width, width)
        for part in range(count):
            size = refs[number].shape[0]
            copy = pltpu.make_async_copy(
                refs[number], out_ref.at[pl.ds(part * size, size), pl.ds(start, width)], sems.at[number]
            )
            copy.start()
            copies.append(copy)
            number += 1
    for copy in copies:
        copy.wait()


def place(columns, blocks, into, out_shape):
    counts = [len(pieces) for pieces in blocks]
    pieces = [piece for block in blocks for piece in block]
    old = [] if into is None else [into]
    return pl.pallas_call(
        functools.partial(place_kernel, counts),
        out_shape=out_shape,
        in_specs=[SMEM] + [VMEM] * len(pieces) + [ANY] * len(old),
        out_specs=ANY,
        scratch_shapes=[pltpu.SemaphoreType.DMA((len(pieces),))],
        input_output_aliases={len(pieces) + 1: 0} if old else {},
        compiler_params=params(10),
        cost_estimate=cost(0, 4 * sum(piece.size for piece in pieces)),
    )(columns, *pieces, *old)


def body(
    hidden_rows,
    attn_rows,
    q_weight,
    o_weight,
    owner_table,
    group_adapters,
    req_slot,
    req_len,
    qa_store,
    qb_store,
    oa_store,
    ob_store,
):
    groups = lax.axis_size("group")
    size = lax.axis_size("tensor")
    mine = lax.axis_index("tensor")
    held, _, rank = qa_store.shape
    rows, _ = hidden_rows.shape
    width = o_weight.shape[1] // size
    half = rows // 2
    routing = (owner_table, group_adapters, req_slot, req_len)
    block = [jnp.reshape(mine ^ dist, (1,)).astype(jnp.int32) for dist in range(size)]
    order = bits(size)

    far = Groups("group", [groups // 2 * 4 * part // 16 for part in (2, 3, 5, 7, 8, 10, 12, 14, 15, 16)])
    near = Chain("group")
    chains = {bit: Chain("tensor") for bit in order}
    far_dists = list(range(groups // 2, groups))
    near_dists = list(range(2, groups // 2))
    all_dists = list(range(groups))
    stores = [jnp.swapaxes(oa_store, 1, 2), ob_store, jnp.swapaxes(qa_store, 1, 2), qb_store]
    used = [{}, {}, {}, {}]

    def packed(plan, mebibytes, *pins):
        wanted = sorted({part for _, parts in plan for part in parts})
        plan = [(dist, [wanted.index(part) for part in parts]) for dist, parts in plan]
        return pack(plan, owner_table, group_adapters, [stores[part] for part in wanted], pins, mebibytes)

    def fetch_far(values, part, dists, *pins):
        for value, dist in zip(values, dists):
            used[part][dist] = (far.send(value, dist, *pins), 0)

    def fetch_near(values, parts, pins, dists):
        for value, dist, some in zip(values, dists, pins):
            arrived = near.send(value, dist, *some)
            for row, part in enumerate(parts):
                used[part][dist] = (arrived, row)

    def pieces_of(part, dists):
        return [used[part][dist] for dist in dists]

    def arrivals():
        return [chain.done[-1] for chain in chains.values()]

    def summed(value, *pins):
        arrived = send(after(value, *pins) if pins else value, "tensor", order[0])
        return value + arrived, arrived

    def summed_on(value, *pins):
        for bit in order[1:]:
            value = value + send(after(value, *pins) if pins else value, "tensor", bit)
        return value

    halving = (order, order[::-1])
    leaving = [sorted((dist for dist in range(size) if dist & halving[number][0]), reverse=True) for number in range(2)]
    buffers = [None, None]
    sums = [{}, {}]

    def o_sums(dist):
        wanted = []
        for number in range(2):
            if dist in leaving[number]:
                wanted.append((buffers[number], leaving[number].index(dist), len(leaving[number])))
            else:
                wanted.append(None)
        values = o_block(block[dist], attn_rows, o_weight, width, wanted)
        for number in range(2):
            if wanted[number] is None:
                sums[number][dist] = (values[number], [])
            else:
                buffers[number] = values[number]

    def reduce_first(*pins):
        for number in range(2):
            bit = halving[number][0]
            arrived = chains[bit].send(buffers[number], bit, *pins)
            for row, dist in enumerate(leaving[number]):
                sums[number][dist ^ bit][1].append((arrived, row * half))

    def reduce_step(step, *pins):
        for number in range(2):
            bit = halving[number][step]
            for dist in sorted((one for one in sums[number] if one & bit), reverse=True):
                arrived = chains[bit].send(merge([sums[number].pop(dist)], True), bit, *pins)
                sums[number][dist ^ bit][1].append((arrived, 0))

    hidden = share(hidden_rows, chains)
    lead, rest = far_dists[:3], far_dists[3:]
    values = packed([(dist, (0,)) for dist in lead] + [(near_dists[0], (0, 1))], 60)
    fetch_far(values[:2], 0, lead[:2])
    third, near_values = values[2:3], values[3:]
    plan = [(dist, (0,)) for dist in rest] + [(dist, (2,)) for dist in far_dists]
    plan = plan + [(dist, (0, 1)) for dist in near_dists[1:]] + [(1, (0, 1, 2, 3)), (0, (0, 1, 2, 3))]
    second = packed(plan, 10, *values)
    found = row_distances(routing, held, rows, 2 * rank)
    dists = sorted(range(1, size), reverse=True)
    for dist in dists[:-1]:
        o_sums(dist)
    pins = [found, *[buffer for buffer in buffers if buffer is not None]]
    fetch_near(near_values, (0, 1), [[*far.upto(0), *pins]], near_dists)
    fetch_far(third, 0, lead[2:], second[0], *pins)
    o_sums(dists[-1])
    beside = send(after(second[-2], *far.upto(0), *pins), "group", 1)
    for part in range(4):
        used[part][1] = (beside, part)
        used[part][0] = (second[-1], part)

    fetch_far(second, 0, rest)
    fetch_far(second[len(rest) :], 2, far_dists[:-1])
    hidden = forward(hidden, chains, *far.upto(1), beside, *buffers)
    o_sums(0)
    fetch_near(second[len(rest) + len(far_dists) : -2], (0, 1), [far.upto(1)], near_dists[1:])
    q_total = None
    q_ready = []
    for dist in range(size):
        q_total, token = q_block(block[dist], hidden[dist], q_weight, q_total)
        q_ready.append(token)
    plan = [(dist, (part,)) for part in (1, 3) for dist in far_dists] + [(dist, (2, 3)) for dist in near_dists]
    values = packed(plan, 10, *far.upto(1))

    reduce_first(*far.upto(2), *near.done[1:], sums[0][0][0], values[0], *q_ready[:1])
    late = values[2 * len(far_dists) :]
    fetch_near(late, (2, 3), [far.upto(2)], near_dists[:1])
    o_half = down(found, rank, attn_rows, pieces_of(0, all_dists), q_ready[1 : size // 2 + 1])
    fetch_far(second[len(rest) + len(far_dists) - 1 :], 2, far_dists[-1:], o_half)
    fetch_near(late[1:], (2, 3), [far.upto(4)], near_dists[1:])
    fetch_far(values, 1, far_dists)
    fetch_far(values[len(far_dists) :], 3, far_dists)
    o_down, o_arrived = summed(o_half, *far.upto(3))
    o_down = summed_on(o_down)

    last = far_dists[-2:]
    first = [dist for dist in all_dists if dist not in last]
    for step in range(1, len(order)):
        reduce_step(step, *far.upto(4), near.done[len(near_dists)], o_arrived)
    q_half = down(found, rank, hidden_rows, pieces_of(2, all_dists), q_ready[-1:])
    q_down = functools.reduce(jnp.add, [send(q_half, "tensor", dist) for dist in range(1, size)], q_half)
    bases = up(found, rank, o_down, used[1], all_dists, [one[0][0] for one in sums], jnp.float32)
    rounded = merge([(base, one[0][1]) for base, one in zip(bases, sums)], False)

    finished = share(rounded, chains, *far.upto(6), q_down)

    finished = forward(finished, chains, *far.upto(8))

    out_shape = jax.ShapeDtypeStruct((rows, width * size), jnp.bfloat16)
    soon = [dist for dist in range(size) if len(finished[dist]) == 1]
    late = [dist for dist in range(size) if len(finished[dist]) > 1]

    def placed(dists, into):
        columns = jnp.concatenate([block[dist] for dist in dists])
        return place(columns, [finished[dist] for dist in dists], into, out_shape)

    attn_out = placed(soon, None)
    (total,) = up(found, rank, q_down, used[3], first, [after(q_total, attn_out)], jnp.float32)
    attn_out = placed(late, attn_out)
    (queries,) = up(found, rank, q_down, used[3], last, [after(total, attn_out)], jnp.bfloat16)
    return (queries, attn_out)


def solution(mesh):
    return jax.shard_map(
        body,
        mesh=mesh,
        in_specs=(
            P("group", "tensor"),
            P("group", "tensor"),
            P(None, "tensor"),
            P("tensor", None),
            P(),
            P(),
            P("group", None),
            P("group", None),
            P("group", "tensor", None),
            P("group", None, "tensor"),
            P("group", "tensor", None),
            P("group", None, "tensor"),
        ),
        out_specs=(P("group", "tensor"), P("group", None)),
        check_vma=False,
    )
```

```python
import functools
import math

import jax
import jax.numpy as jnp
from jax import lax
from jax.experimental import pallas as pl
from jax.experimental.pallas import tpu as pltpu
from jax.sharding import PartitionSpec as P

ADAPTER_SCALE = 0.5
LANES = 128
LEVELS = 8
STEPS = 32767.0
MIB = 1024 * 1024
ANY = pl.BlockSpec(memory_space=pl.ANY)
SMEM = pl.BlockSpec(memory_space=pltpu.SMEM)
VMEM = pl.BlockSpec(memory_space=pltpu.VMEM)
HBM = pl.BlockSpec(memory_space=pltpu.HBM)


def params(mebibytes):
    return pltpu.CompilerParams(vmem_limit_bytes=mebibytes * MIB)


def cost(flops, nbytes):
    return pl.CostEstimate(flops=flops // 1000, bytes_accessed=nbytes // 1000, transcendentals=0)


def send(value, axis, offset):
    size = lax.axis_size(axis)
    return lax.ppermute(value, axis, [(i, i ^ offset) for i in range(size)])


def after(value, *others):
    return lax.optimization_barrier((value, *others))[0]


def at(values, *numbers):
    return [values[number] for number in numbers if number < len(values)]


def tie_kernel(*refs):
    del refs


def tie(value, others):
    return pl.pallas_call(
        tie_kernel,
        out_shape=pltpu.HBM(value.shape, value.dtype),
        in_specs=[ANY] * (1 + len(others)),
        out_specs=HBM,
        input_output_aliases={0: 0},
        compiler_params=params(1),
        cost_estimate=cost(0, 0),
    )(value, *others)


class Chain:
    def __init__(self, axis):
        self.axis = axis
        self.done = []

    def send(self, value, offset, *pins):
        pins = (*self.done[-1:], *pins)
        if pins:
            value = after(value, *pins)
        arrived = send(value, self.axis, offset)
        self.done.append(arrived)
        return arrived


class Groups:
    def __init__(self, axis, ends):
        self.axis = axis
        self.ends = ends
        self.done = []

    def upto(self, step):
        start = self.ends[step - 1] if step else 0
        return self.done[start : self.ends[step]]

    def send(self, value, offset, *pins):
        number = len(self.done)
        step = sum(end <= number for end in self.ends)
        if step:
            value = after(value, *self.upto(step - 1), *pins)
        arrived = send(value, self.axis, offset)
        self.done.append(arrived)
        return arrived


def bits(size):
    out = []
    bit = 1
    while bit < size:
        out.append(bit)
        bit *= 2
    return out


def pack_kernel(plan, count, table_ref, adapters_ref, *refs):
    stores = refs[:count]
    outs = refs[-3 - len(plan) : -3]
    staged, in_sems, out_sems = refs[-3:]
    slots = adapters_ref.shape[1]
    held, rank, _ = stores[0].shape
    me = lax.axis_index("group")
    loads = []
    for dist, parts in plan:
        dest = me ^ dist
        pick = jnp.int32(0)
        for slot in range(slots):
            place = table_ref[adapters_ref[dest, slot]]
            owner = lax.div(place, jnp.int32(held))
            pick = jnp.where(owner == me, place - owner * held, pick)
        for part in parts:
            number = len(loads)
            load = pltpu.make_async_copy(stores[part].at[pick], staged.at[number], in_sems.at[number])
            load.start()
            loads.append(load)
    copies = []
    for out_ref, (_, parts) in zip(outs, plan):
        for row in range(len(parts)):
            number = len(copies)
            loads[number].wait()
            copy = pltpu.make_async_copy(
                staged.at[number], out_ref.at[pl.ds(row * rank, rank)], out_sems.at[number]
            )
            copy.start()
            copies.append(copy)
    for copy in copies:
        copy.wait()


def pack(plan, table, adapters, stores, order, mebibytes):
    _, rank, width = stores[0].shape
    dtype = stores[0].dtype
    total = sum(len(parts) for _, parts in plan)
    return pl.pallas_call(
        functools.partial(pack_kernel, plan, len(stores)),
        out_shape=[pltpu.HBM((len(parts) * rank, width), dtype) for _, parts in plan],
        in_specs=[SMEM, SMEM] + [HBM] * len(stores) + [ANY] * len(order),
        out_specs=[HBM] * len(plan),
        scratch_shapes=[
            pltpu.VMEM((total, rank, width), dtype),
            pltpu.SemaphoreType.DMA((total,)),
            pltpu.SemaphoreType.DMA((total,)),
        ],
        compiler_params=params(mebibytes),
        cost_estimate=cost(0, 4 * total * rank * width),
    )(table, adapters, *stores, *order)


def distance_kernel(held, table_ref, adapters_ref, slot_ref, len_ref, out_ref):
    me = lax.axis_index("group")
    position = lax.broadcasted_iota(jnp.int32, out_ref.shape, 0)
    found = jnp.zeros(out_ref.shape, jnp.int32)
    start = jnp.int32(0)
    for req in range(len_ref.shape[1]):
        place = table_ref[adapters_ref[me, slot_ref[0, req]]]
        dist = lax.div(place, jnp.int32(held)) ^ me
        end = start + len_ref[0, req]
        found = jnp.where((position >= start) & (position < end), dist, found)
        start = end
    out_ref[...] = found


def row_distances(routing, held, rows, lanes):
    return pl.pallas_call(
        functools.partial(distance_kernel, held),
        out_shape=jax.ShapeDtypeStruct((rows, lanes), jnp.int32),
        in_specs=[SMEM] * 4,
        out_specs=VMEM,
        compiler_params=params(4),
        cost_estimate=cost(0, 4 * rows * lanes),
    )(*routing)


def down_kernel(rank, places, found_ref, rows_ref, *refs):
    groups = len(places)
    pieces = refs[:groups]
    out_ref, whole, sems = refs[-3:]
    copies = []
    for dist in range(groups):
        copy = pltpu.make_async_copy(
            pieces[dist].at[pl.ds(places[dist] * rank, rank)], whole.at[pl.ds(dist * rank, rank)], sems.at[dist]
        )
        copy.start()
        copies.append(copy)
    shape = (rows_ref.shape[0], 2 * rank)
    found = found_ref[...]
    high = (lax.broadcasted_iota(jnp.int32, shape, 1) >= rank).astype(jnp.int32)
    for copy in copies:
        copy.wait()
    full = lax.dot_general(
        rows_ref[...], whole[...], (((1,), (1,)), ((), ())), preferred_element_type=jnp.float32
    )
    picked = jnp.zeros(shape, jnp.float32)
    for pair in range(groups // 2):
        piece = full[:, pair * 2 * rank : (pair + 1) * 2 * rank]
        picked = picked + jnp.where(found == 2 * pair + high, piece, 0.0)
    out_ref[...] = picked + pltpu.roll(picked, rank, 1)


def down(found, rank, rows_in, pieces, order=()):
    rows, width = rows_in.shape
    groups = len(pieces)
    return pl.pallas_call(
        functools.partial(down_kernel, rank, [row for _, row in pieces]),
        out_shape=jax.ShapeDtypeStruct((rows, 2 * rank), jnp.float32),
        in_specs=[VMEM] * 2 + [ANY] * (groups + len(order)),
        out_specs=VMEM,
        scratch_shapes=[
            pltpu.VMEM((groups * rank, width), rows_in.dtype),
            pltpu.SemaphoreType.DMA((groups,)),
        ],
        compiler_params=params(12),
        cost_estimate=cost(2 * rows * width * groups * rank, 2 * rows * width + 2 * groups * rank * width),
    )(found, rows_in, *[piece for piece, _ in pieces], *order)


def up_kernel(dists, split, found_ref, down_ref, *refs):
    groups = len(dists)
    pieces = refs[:groups]
    bases = refs[groups : groups + split]
    outs = refs[groups + split : groups + 2 * split]
    terms = refs[-1]
    rank = pieces[0].shape[0]
    rows = down_ref.shape[0]

    @pl.when(pl.program_id(0) == 0)
    def _():
        shape = (rows, 2 * rank)
        found = found_ref[...]
        low = lax.broadcasted_iota(jnp.int32, shape, 1) < rank
        both = down_ref[...] * ADAPTER_SCALE
        first = both.astype(jnp.bfloat16)
        second = (both - first.astype(jnp.float32)).astype(jnp.bfloat16)
        for number, term in enumerate((first, second)):
            for pair in range(groups // 2):
                wanted = jnp.where(low, dists[2 * pair], dists[2 * pair + 1])
                chosen = jnp.where(found == wanted, term.astype(jnp.float32), 0.0)
                start = number * groups * rank + pair * 2 * rank
                terms[:, start : start + 2 * rank] = chosen.astype(jnp.bfloat16)

    whole = jnp.concatenate([piece[...] for piece in pieces] * 2, axis=0)
    total = jnp.dot(terms[...], whole, preferred_element_type=jnp.float32)
    size = rows // split
    for number in range(split):
        value = bases[number][...] + total[number * size : (number + 1) * size]
        outs[number][...] = value.astype(outs[number].dtype)


def up(found, rank, downs, used, dists, bases, out_dtype):
    pieces = [used[dist] for dist in dists]
    groups = len(dists)
    width = pieces[0][0].shape[1]
    rows = downs.shape[0]
    split = len(bases)
    tile = min(512, width)
    column = lambda step: (0, step)
    size = rows // split
    piece_specs = [
        pl.BlockSpec((rank, tile), functools.partial(lambda place, step: (place, step), place)) for _, place in pieces
    ]
    return pl.pallas_call(
        functools.partial(up_kernel, dists, split),
        grid=(width // tile,),
        out_shape=[jax.ShapeDtypeStruct((size, width), out_dtype)] * split,
        in_specs=[pl.BlockSpec(downs.shape, lambda step: (0, 0))] * 2
        + piece_specs
        + [pl.BlockSpec((size, tile), column)] * split,
        out_specs=[pl.BlockSpec((size, tile), column)] * split,
        scratch_shapes=[pltpu.VMEM((rows, 2 * groups * rank), jnp.bfloat16)],
        compiler_params=params(16),
        cost_estimate=cost(4 * rows * width * groups * rank, 8 * rows * width + 2 * groups * rank * width),
    )(found, downs, *[piece for piece, _ in pieces], *bases)


def tile_of(width):
    return min(512, width)


def encode(value, out_ref, step):
    half, tile = value.shape
    width = out_ref.shape[1] - LANES
    peak = jnp.max(jnp.abs(value), axis=1, keepdims=True)
    level = jnp.ceil(jnp.log(jnp.maximum(peak, 1e-30)) * (LEVELS / math.log(2.0)))
    coded = jnp.round(value * (jnp.exp2(level * (-1.0 / LEVELS)) * STEPS))
    coded = jnp.minimum(jnp.maximum(coded, -STEPS), STEPS)
    start = step * tile if isinstance(step, int) else pl.multiple_of(step * tile, tile)
    out_ref[:, pl.ds(start, tile)] = coded.astype(jnp.int32).astype(jnp.int16)
    lane = lax.broadcasted_iota(jnp.int32, (half, LANES), 1)
    kept = jnp.where(lane < step, out_ref[:, width:].astype(jnp.int32), 0)
    out_ref[:, width:] = jnp.where(lane == step, level.astype(jnp.int32), kept).astype(jnp.int16)


def decode(coded_ref, row, half, step, tile):
    width = coded_ref.shape[1] - LANES
    levels = coded_ref[row : row + half, width:].astype(jnp.int32)
    lane = lax.broadcasted_iota(jnp.int32, levels.shape, 1)
    level = jnp.sum(jnp.where(lane == step, levels, 0).astype(jnp.float32), axis=1, keepdims=True)
    value = coded_ref[row : row + half, step * tile : (step + 1) * tile].astype(jnp.int32).astype(jnp.float32)
    return value * (jnp.exp2(level * (1.0 / LEVELS)) * (1.0 / STEPS))


def merge_kernel(places, coded_out, *refs):
    out_ref = refs[-1]
    inputs = refs[:-1]
    for number, rows in enumerate(places):
        base, coded = inputs[0], inputs[1 : 1 + len(rows)]
        inputs = inputs[1 + len(rows) :]
        half, width = base.shape
        tile = tile_of(width)
        for step in range(width // tile):
            columns = slice(step * tile, (step + 1) * tile)
            total = base[:, columns]
            for one, row in zip(coded, rows):
                total = total + decode(one, row, half, step, tile)
            if coded_out:
                encode(total, out_ref, step)
            else:
                out_ref[number * half : (number + 1) * half, columns] = total.astype(out_ref.dtype)


def merge(sums, coded_out):
    half, width = sums[0][0].shape
    places = [[row for _, row in coded] for _, coded in sums]
    if coded_out:
        out_shape = jax.ShapeDtypeStruct((half, width + LANES), jnp.int16)
    else:
        out_shape = jax.ShapeDtypeStruct((len(sums) * half, width), jnp.bfloat16)
    values = []
    for base, coded in sums:
        values = values + [base] + [value for value, _ in coded]
    return pl.pallas_call(
        functools.partial(merge_kernel, places, coded_out),
        out_shape=out_shape,
        in_specs=[VMEM] * len(values),
        out_specs=VMEM,
        compiler_params=params(20),
        cost_estimate=cost(0, 2 * sum(value.size for value in values) + 4 * half * width),
    )(*values)


def o_kernel(block_ref, rows_ref, weight_ref, *refs):
    del block_ref
    outs = refs[-2:]
    total = jnp.dot(rows_ref[...], weight_ref[...], preferred_element_type=jnp.float32)
    half = outs[0].shape[0]
    for number, out_ref in enumerate(outs):
        value = total[number * half : (number + 1) * half]
        if out_ref.dtype == jnp.int16:
            encode(value, out_ref, pl.program_id(0))
        else:
            out_ref[...] = value


def o_block(block, rows_in, weight, width, leaving):
    rows, depth = rows_in.shape
    half = rows // 2
    tile = tile_of(width)
    tiles = width // tile
    shapes, specs, buffers, aliases = [], [], [], {}
    for number, one in enumerate(leaving):
        if one is None:
            shapes.append(jax.ShapeDtypeStruct((half, width), jnp.float32))
            specs.append(pl.BlockSpec((half, tile), lambda step, ref: (0, step)))
            continue
        buffer, place, places = one
        shapes.append(jax.ShapeDtypeStruct((places * half, width + LANES), jnp.int16))
        specs.append(
            pl.BlockSpec((half, width + LANES), functools.partial(lambda place, step, ref: (place, 0), place))
        )
        if buffer is not None:
            aliases[3 + len(buffers)] = number
            buffers.append(buffer)
    return pl.pallas_call(
        o_kernel,
        grid_spec=pltpu.PrefetchScalarGridSpec(
            num_scalar_prefetch=1,
            grid=(tiles,),
            in_specs=[
                pl.BlockSpec((rows, depth), lambda step, ref: (0, 0)),
                pl.BlockSpec((depth, tile), lambda step, ref: (0, ref[0] * tiles + step)),
            ]
            + [ANY] * len(buffers),
            out_specs=specs,
        ),
        out_shape=shapes,
        input_output_aliases=aliases,
        compiler_params=params(36),
        cost_estimate=cost(2 * rows * depth * width, 2 * depth * width + 2 * rows * depth + 4 * rows * width),
    )(block, rows_in, weight, *buffers)


def q_kernel(count, has_total, block_ref, *refs):
    del block_ref
    pieces = refs[:count]
    weight_ref = refs[count]
    out_ref, token_ref = refs[-2:]
    size = pieces[0].shape[0]
    token_ref[...] = jnp.zeros_like(token_ref)
    for number, rows_ref in enumerate(pieces):
        total = jnp.dot(rows_ref[...], weight_ref[...], preferred_element_type=jnp.float32)
        span = slice(number * size, (number + 1) * size)
        if has_total:
            total = total + refs[count + 1][span]
        out_ref[span] = total


def q_block(block, pieces, weight, total):
    count = len(pieces)
    size, depth = pieces[0].shape
    rows = count * size
    width = weight.shape[1]
    tile = tile_of(width)
    has_total = total is not None
    column = pl.BlockSpec((rows, tile), lambda step, ref: (0, step))
    return pl.pallas_call(
        functools.partial(q_kernel, count, has_total),
        grid_spec=pltpu.PrefetchScalarGridSpec(
            num_scalar_prefetch=1,
            grid=(width // tile,),
            in_specs=[pl.BlockSpec((size, depth), lambda step, ref: (0, 0))] * count
            + [pl.BlockSpec((depth, tile), lambda step, ref: (ref[0], step))]
            + [column] * has_total,
            out_specs=[column, pl.BlockSpec((8, LANES), lambda step, ref: (0, 0))],
        ),
        out_shape=[jax.ShapeDtypeStruct((rows, width), jnp.float32), jax.ShapeDtypeStruct((8, LANES), jnp.float32)],
        input_output_aliases={count + 2: 0} if has_total else {},
        compiler_params=params(36),
        cost_estimate=cost(2 * rows * depth * width, 2 * depth * width + 2 * rows * depth + 8 * rows * width),
    )(block, *pieces, weight, *([total] * has_total))


def share(block, chains, *pins):
    whole = {0: block}
    for bit in chains:
        whole[bit] = chains[bit].send(block, bit, *pins)
    return whole


def forward(whole, chains, *pins):
    order = list(chains)
    half = whole[0].shape[0] // 2
    parts = [{}, {}]
    for step in range(len(order)):
        for number in range(2):
            bits_used = order if number == 0 else order[::-1]
            bit = bits_used[step]
            held = [0]
            for used in bits_used[:step]:
                held = held + [dist ^ used for dist in held]
            for dist in held[1:]:
                if dist in whole:
                    piece = whole[dist][number * half : (number + 1) * half]
                else:
                    piece = parts[number][dist]
                parts[number][dist ^ bit] = chains[bit].send(piece, bit, *pins)
    pieces = {dist: [value] for dist, value in whole.items()}
    for dist in parts[0]:
        pieces[dist] = [parts[0][dist], parts[1][dist]]
    return pieces


def place_kernel(blocks, column_ref, *refs):
    out_ref, sems = refs[-2:]
    width = refs[0].shape[1]
    copies = []
    number = 0
    for block, count in enumerate(blocks):
        start = pl.multiple_of(column_ref[block] * width, width)
        for part in range(count):
            size = refs[number].shape[0]
            copy = pltpu.make_async_copy(
                refs[number], out_ref.at[pl.ds(part * size, size), pl.ds(start, width)], sems.at[number]
            )
            copy.start()
            copies.append(copy)
            number += 1
    for copy in copies:
        copy.wait()


def place(columns, blocks, into, out_shape):
    counts = [len(pieces) for pieces in blocks]
    pieces = [piece for block in blocks for piece in block]
    old = [] if into is None else [into]
    return pl.pallas_call(
        functools.partial(place_kernel, counts),
        out_shape=out_shape,
        in_specs=[SMEM] + [VMEM] * len(pieces) + [ANY] * len(old),
        out_specs=ANY,
        scratch_shapes=[pltpu.SemaphoreType.DMA((len(pieces),))],
        input_output_aliases={len(pieces) + 1: 0} if old else {},
        compiler_params=params(10),
        cost_estimate=cost(0, 4 * sum(piece.size for piece in pieces)),
    )(columns, *pieces, *old)


def body(
    hidden_rows,
    attn_rows,
    q_weight,
    o_weight,
    owner_table,
    group_adapters,
    req_slot,
    req_len,
    qa_store,
    qb_store,
    oa_store,
    ob_store,
):
    groups = lax.axis_size("group")
    size = lax.axis_size("tensor")
    mine = lax.axis_index("tensor")
    held, _, rank = qa_store.shape
    rows, _ = hidden_rows.shape
    width = o_weight.shape[1] // size
    half = rows // 2
    routing = (owner_table, group_adapters, req_slot, req_len)
    block = [jnp.reshape(mine ^ dist, (1,)).astype(jnp.int32) for dist in range(size)]
    order = bits(size)

    far = Groups("group", [groups // 2 * 4 * part // 16 for part in (3, 5, 7, 8, 10, 11, 13, 14, 16)])
    near = Chain("group")
    chains = {bit: Chain("tensor") for bit in order}
    far_dists = list(range(groups // 2, groups))
    near_dists = list(range(2, groups // 2))
    all_dists = list(range(groups))
    stores = [jnp.swapaxes(oa_store, 1, 2), ob_store, jnp.swapaxes(qa_store, 1, 2), qb_store]
    used = [{}, {}, {}, {}]

    def packed(plan, mebibytes, *pins):
        wanted = sorted({part for _, parts in plan for part in parts})
        plan = [(dist, [wanted.index(part) for part in parts]) for dist, parts in plan]
        return pack(plan, owner_table, group_adapters, [stores[part] for part in wanted], pins, mebibytes)

    def fetch_far(values, part, dists, *pins):
        for value, dist in zip(values, dists):
            used[part][dist] = (far.send(value, dist, *pins), 0)

    def fetch_near(values, parts, pins, dists):
        for value, dist, some in zip(values, dists, pins):
            arrived = near.send(value, dist, *some)
            for row, part in enumerate(parts):
                used[part][dist] = (arrived, row)

    def pieces_of(part, dists):
        return [used[part][dist] for dist in dists]

    def arrivals():
        return [chain.done[-1] for chain in chains.values()]

    def summed(value, *pins):
        arrived = send(after(value, *pins) if pins else value, "tensor", order[0])
        return value + arrived, arrived

    def summed_on(value, *pins):
        for bit in order[1:]:
            value = value + send(after(value, *pins) if pins else value, "tensor", bit)
        return value

    halving = (order, order[::-1])
    leaving = [sorted((dist for dist in range(size) if dist & halving[number][0]), reverse=True) for number in range(2)]
    buffers = [None, None]
    sums = [{}, {}]

    def o_sums(dist):
        wanted = []
        for number in range(2):
            if dist in leaving[number]:
                wanted.append((buffers[number], leaving[number].index(dist), len(leaving[number])))
            else:
                wanted.append(None)
        values = o_block(block[dist], attn_rows, o_weight, width, wanted)
        for number in range(2):
            if wanted[number] is None:
                sums[number][dist] = (values[number], [])
            else:
                buffers[number] = values[number]

    def reduce_first(*pins):
        for number in range(2):
            bit = halving[number][0]
            arrived = chains[bit].send(buffers[number], bit, *pins)
            for row, dist in enumerate(leaving[number]):
                sums[number][dist ^ bit][1].append((arrived, row * half))

    def reduce_step(step, *pins):
        for number in range(2):
            bit = halving[number][step]
            for dist in sorted((one for one in sums[number] if one & bit), reverse=True):
                arrived = chains[bit].send(merge([sums[number].pop(dist)], True), bit, *pins)
                sums[number][dist ^ bit][1].append((arrived, 0))

    hidden = share(hidden_rows, chains)
    lead, rest = far_dists[:3], far_dists[3:]
    values = packed([(dist, (0,)) for dist in lead], 60)
    fetch_far(values, 0, lead)
    plan = [(dist, (0,)) for dist in rest] + [(dist, (1,)) for dist in far_dists]
    plan = plan + [(dist, (0, 1)) for dist in near_dists] + [(1, (0, 1, 2, 3)), (0, (0, 1, 2, 3))]
    o_values = packed(plan, 57, *values)
    fetch_far(o_values, 0, rest)
    fetch_far(o_values[len(rest) :], 1, far_dists[:3])
    near_values = o_values[len(rest) + len(far_dists) : -2]
    fetch_near(near_values, (0, 1), [far.upto(0)], near_dists[:1])
    found = row_distances(routing, held, rows, 2 * rank)
    for dist in sorted(range(1, size), reverse=True):
        o_sums(dist)

    hidden = forward(hidden, chains, *far.upto(0), *buffers, found, o_values[0])
    o_sums(0)
    q_total = None
    q_ready = []
    for dist in range(size):
        q_total, token = q_block(block[dist], hidden[dist], q_weight, q_total)
        q_ready.append(token)
    plan = [(dist, (part,)) for part in (2, 3) for dist in far_dists] + [(dist, (2, 3)) for dist in near_dists]
    values = packed(plan, 10, *far.upto(0))
    pins = [*far.upto(1), sums[0][0][0], values[0], q_ready[0]]
    fetch_near(near_values[1:], (0, 1), [pins], near_dists[1:])

    reduce_first(*far.upto(1), near.done[0], sums[0][0][0], values[0], *q_ready[:1])
    pins = (near.done[-1], *q_ready[1 : size // 2 + 1])
    beside = send(after(tie(o_values[-2], pins), *far.upto(2)), "group", 1)
    for part in range(4):
        used[part][1] = (beside, part)
        used[part][0] = (o_values[-1], part)
    tied = [tie(value, pins) for value in o_values[len(rest) + 3 : -len(near_dists) - 2]]
    fetch_far(tied, 1, far_dists[3:])
    fetch_far(values, 2, far_dists[:2])
    fetch_far(values[2:], 2, far_dists[2:], q_ready[-1])
    fetch_far(values[len(far_dists) :], 3, far_dists)
    o_half = down(found, rank, attn_rows, pieces_of(0, all_dists))
    o_down, o_arrived = summed(o_half)
    pins = [*far.upto(3), o_arrived]
    o_down = summed_on(o_down, *arrivals())
    for step in range(1, len(order)):
        reduce_step(step, *pins)
    late = values[2 * len(far_dists) :][::-1]
    fetch_near(late, (2, 3), [far.upto(3), far.upto(5)], near_dists[::-1])
    bases = up(found, rank, o_down, used[1], all_dists, [one[0][0] for one in sums], jnp.float32)
    rounded = merge([(base, one[0][1]) for base, one in zip(bases, sums)], False)

    finished = share(rounded, chains, *far.upto(5), near.done[len(near_dists)], q_ready[-1])
    q_half = down(after(found, o_down), rank, hidden_rows, pieces_of(2, all_dists))
    q_down = summed_on(summed(q_half)[0])

    finished = forward(finished, chains, *far.upto(7), q_down)

    out_shape = jax.ShapeDtypeStruct((rows, width * size), jnp.bfloat16)
    soon = [dist for dist in range(size) if len(finished[dist]) == 1]
    late = [dist for dist in range(size) if len(finished[dist]) > 1]

    def placed(dists, into):
        columns = jnp.concatenate([block[dist] for dist in dists])
        return place(columns, [finished[dist] for dist in dists], into, out_shape)

    attn_out = placed(soon, None)
    last = far_dists[-2:]
    first = [dist for dist in all_dists if dist not in last]
    (total,) = up(found, rank, q_down, used[3], first, [after(q_total, attn_out)], jnp.float32)
    attn_out = placed(late, attn_out)
    (queries,) = up(found, rank, q_down, used[3], last, [after(total, attn_out)], jnp.bfloat16)
    return (queries, attn_out)


def solution(mesh):
    return jax.shard_map(
        body,
        mesh=mesh,
        in_specs=(
            P("group", "tensor"),
            P("group", "tensor"),
            P(None, "tensor"),
            P("tensor", None),
            P(),
            P(),
            P("group", None),
            P("group", None),
            P("group", "tensor", None),
            P("group", None, "tensor"),
            P("group", "tensor", None),
            P("group", None, "tensor"),
        ),
        out_specs=(P("group", "tensor"), P("group", None)),
        check_vma=False,
    )
```

```python
import functools
import math

import jax
import jax.numpy as jnp
from jax import lax
from jax.experimental import pallas as pl
from jax.experimental.pallas import tpu as pltpu
from jax.sharding import PartitionSpec as P

ADAPTER_SCALE = 0.5
LANES = 128
LEVELS = 8
STEPS = 32767.0
MIB = 1024 * 1024
ANY = pl.BlockSpec(memory_space=pl.ANY)
SMEM = pl.BlockSpec(memory_space=pltpu.SMEM)
VMEM = pl.BlockSpec(memory_space=pltpu.VMEM)
HBM = pl.BlockSpec(memory_space=pltpu.HBM)


def params(mebibytes):
    return pltpu.CompilerParams(vmem_limit_bytes=mebibytes * MIB)


def cost(flops, nbytes):
    return pl.CostEstimate(flops=flops // 1000, bytes_accessed=nbytes // 1000, transcendentals=0)


def send(value, axis, offset):
    size = lax.axis_size(axis)
    return lax.ppermute(value, axis, [(i, i ^ offset) for i in range(size)])


def after(value, *others):
    return lax.optimization_barrier((value, *others))[0]


def at(values, *numbers):
    return [values[number] for number in numbers if number < len(values)]


def tie_kernel(*refs):
    del refs


def tie(value, others):
    return pl.pallas_call(
        tie_kernel,
        out_shape=pltpu.HBM(value.shape, value.dtype),
        in_specs=[ANY] * (1 + len(others)),
        out_specs=HBM,
        input_output_aliases={0: 0},
        compiler_params=params(1),
        cost_estimate=cost(0, 0),
    )(value, *others)


class Chain:
    def __init__(self, axis):
        self.axis = axis
        self.done = []

    def send(self, value, offset, *pins):
        pins = (*self.done[-1:], *pins)
        if pins:
            value = after(value, *pins)
        arrived = send(value, self.axis, offset)
        self.done.append(arrived)
        return arrived


class Groups:
    def __init__(self, axis, ends):
        self.axis = axis
        self.ends = ends
        self.done = []

    def upto(self, step):
        start = self.ends[step - 1] if step else 0
        return self.done[start : self.ends[step]]

    def send(self, value, offset, *pins):
        number = len(self.done)
        step = sum(end <= number for end in self.ends)
        if step:
            value = after(value, *self.upto(step - 1), *pins)
        arrived = send(value, self.axis, offset)
        self.done.append(arrived)
        return arrived


def bits(size):
    out = []
    bit = 1
    while bit < size:
        out.append(bit)
        bit *= 2
    return out


def pack_kernel(plan, count, table_ref, adapters_ref, *refs):
    stores = refs[:count]
    outs = refs[-3 - len(plan) : -3]
    staged, in_sems, out_sems = refs[-3:]
    slots = adapters_ref.shape[1]
    held, rank, _ = stores[0].shape
    me = lax.axis_index("group")
    loads = []
    for dist, parts in plan:
        dest = me ^ dist
        pick = jnp.int32(0)
        for slot in range(slots):
            place = table_ref[adapters_ref[dest, slot]]
            owner = lax.div(place, jnp.int32(held))
            pick = jnp.where(owner == me, place - owner * held, pick)
        for part in parts:
            number = len(loads)
            load = pltpu.make_async_copy(stores[part].at[pick], staged.at[number], in_sems.at[number])
            load.start()
            loads.append(load)
    copies = []
    for out_ref, (_, parts) in zip(outs, plan):
        for row in range(len(parts)):
            number = len(copies)
            loads[number].wait()
            copy = pltpu.make_async_copy(
                staged.at[number], out_ref.at[pl.ds(row * rank, rank)], out_sems.at[number]
            )
            copy.start()
            copies.append(copy)
    for copy in copies:
        copy.wait()


def pack(plan, table, adapters, stores, order, mebibytes):
    _, rank, width = stores[0].shape
    dtype = stores[0].dtype
    total = sum(len(parts) for _, parts in plan)
    return pl.pallas_call(
        functools.partial(pack_kernel, plan, len(stores)),
        out_shape=[pltpu.HBM((len(parts) * rank, width), dtype) for _, parts in plan],
        in_specs=[SMEM, SMEM] + [HBM] * len(stores) + [ANY] * len(order),
        out_specs=[HBM] * len(plan),
        scratch_shapes=[
            pltpu.VMEM((total, rank, width), dtype),
            pltpu.SemaphoreType.DMA((total,)),
            pltpu.SemaphoreType.DMA((total,)),
        ],
        compiler_params=params(mebibytes),
        cost_estimate=cost(0, 4 * total * rank * width),
    )(table, adapters, *stores, *order)


def distance_kernel(held, table_ref, adapters_ref, slot_ref, len_ref, out_ref):
    me = lax.axis_index("group")
    position = lax.broadcasted_iota(jnp.int32, out_ref.shape, 0)
    found = jnp.zeros(out_ref.shape, jnp.int32)
    start = jnp.int32(0)
    for req in range(len_ref.shape[1]):
        place = table_ref[adapters_ref[me, slot_ref[0, req]]]
        dist = lax.div(place, jnp.int32(held)) ^ me
        end = start + len_ref[0, req]
        found = jnp.where((position >= start) & (position < end), dist, found)
        start = end
    out_ref[...] = found


def row_distances(routing, held, rows, lanes):
    return pl.pallas_call(
        functools.partial(distance_kernel, held),
        out_shape=jax.ShapeDtypeStruct((rows, lanes), jnp.int32),
        in_specs=[SMEM] * 4,
        out_specs=VMEM,
        compiler_params=params(4),
        cost_estimate=cost(0, 4 * rows * lanes),
    )(*routing)


def down_kernel(rank, places, found_ref, rows_ref, *refs):
    groups = len(places)
    pieces = refs[:groups]
    out_ref, whole, sems = refs[-3:]
    copies = []
    for dist in range(groups):
        copy = pltpu.make_async_copy(
            pieces[dist].at[pl.ds(places[dist] * rank, rank)], whole.at[pl.ds(dist * rank, rank)], sems.at[dist]
        )
        copy.start()
        copies.append(copy)
    shape = (rows_ref.shape[0], 2 * rank)
    found = found_ref[...]
    high = (lax.broadcasted_iota(jnp.int32, shape, 1) >= rank).astype(jnp.int32)
    for copy in copies:
        copy.wait()
    full = lax.dot_general(
        rows_ref[...], whole[...], (((1,), (1,)), ((), ())), preferred_element_type=jnp.float32
    )
    picked = jnp.zeros(shape, jnp.float32)
    for pair in range(groups // 2):
        piece = full[:, pair * 2 * rank : (pair + 1) * 2 * rank]
        picked = picked + jnp.where(found == 2 * pair + high, piece, 0.0)
    picked = picked + pltpu.roll(picked, rank, 1)
    half = out_ref.shape[0]
    out_ref[...] = jnp.where(high[:half] == 0, picked[:half], picked[half:])


def down(found, rank, rows_in, pieces, order=()):
    rows, width = rows_in.shape
    groups = len(pieces)
    return pl.pallas_call(
        functools.partial(down_kernel, rank, [row for _, row in pieces]),
        out_shape=jax.ShapeDtypeStruct((rows // 2, 2 * rank), jnp.float32),
        in_specs=[VMEM] * 2 + [ANY] * (groups + len(order)),
        out_specs=VMEM,
        scratch_shapes=[
            pltpu.VMEM((groups * rank, width), rows_in.dtype),
            pltpu.SemaphoreType.DMA((groups,)),
        ],
        compiler_params=params(12),
        cost_estimate=cost(2 * rows * width * groups * rank, 2 * rows * width + 2 * groups * rank * width),
    )(found, rows_in, *[piece for piece, _ in pieces], *order)


def up_kernel(dists, split, found_ref, down_ref, *refs):
    groups = len(dists)
    pieces = refs[:groups]
    bases = refs[groups : groups + split]
    outs = refs[groups + split : groups + 2 * split]
    terms = refs[-1]
    rank = pieces[0].shape[0]
    rows = found_ref.shape[0]

    @pl.when(pl.program_id(0) == 0)
    def _():
        shape = (rows, 2 * rank)
        found = found_ref[...]
        low = lax.broadcasted_iota(jnp.int32, shape, 1) < rank
        folded = down_ref[...] * ADAPTER_SCALE
        turned = pltpu.roll(folded, rank, 1)
        first_half = low[: rows // 2]
        both = jnp.concatenate(
            [jnp.where(first_half, folded, turned), jnp.where(first_half, turned, folded)], axis=0
        )
        first = both.astype(jnp.bfloat16)
        second = (both - first.astype(jnp.float32)).astype(jnp.bfloat16)
        for number, term in enumerate((first, second)):
            for pair in range(groups // 2):
                wanted = jnp.where(low, dists[2 * pair], dists[2 * pair + 1])
                chosen = jnp.where(found == wanted, term.astype(jnp.float32), 0.0)
                start = number * groups * rank + pair * 2 * rank
                terms[:, start : start + 2 * rank] = chosen.astype(jnp.bfloat16)

    whole = jnp.concatenate([piece[...] for piece in pieces] * 2, axis=0)
    total = jnp.dot(terms[...], whole, preferred_element_type=jnp.float32)
    size = rows // split
    for number in range(split):
        value = bases[number][...] + total[number * size : (number + 1) * size]
        outs[number][...] = value.astype(outs[number].dtype)


def up(found, rank, downs, used, dists, bases, out_dtype):
    pieces = [used[dist] for dist in dists]
    groups = len(dists)
    width = pieces[0][0].shape[1]
    rows = found.shape[0]
    split = len(bases)
    tile = min(512, width)
    column = lambda step: (0, step)
    size = rows // split
    piece_specs = [
        pl.BlockSpec((rank, tile), functools.partial(lambda place, step: (place, step), place)) for _, place in pieces
    ]
    return pl.pallas_call(
        functools.partial(up_kernel, dists, split),
        grid=(width // tile,),
        out_shape=[jax.ShapeDtypeStruct((size, width), out_dtype)] * split,
        in_specs=[pl.BlockSpec(found.shape, lambda step: (0, 0)), pl.BlockSpec(downs.shape, lambda step: (0, 0))]
        + piece_specs
        + [pl.BlockSpec((size, tile), column)] * split,
        out_specs=[pl.BlockSpec((size, tile), column)] * split,
        scratch_shapes=[pltpu.VMEM((rows, 2 * groups * rank), jnp.bfloat16)],
        compiler_params=params(16),
        cost_estimate=cost(4 * rows * width * groups * rank, 8 * rows * width + 2 * groups * rank * width),
    )(found, downs, *[piece for piece, _ in pieces], *bases)


def tile_of(width):
    return min(512, width)


def encode(value, out_ref, step):
    half, tile = value.shape
    width = out_ref.shape[1] - LANES
    peak = jnp.max(jnp.abs(value), axis=1, keepdims=True)
    level = jnp.ceil(jnp.log(jnp.maximum(peak, 1e-30)) * (LEVELS / math.log(2.0)))
    coded = jnp.round(value * (jnp.exp2(level * (-1.0 / LEVELS)) * STEPS))
    coded = jnp.minimum(jnp.maximum(coded, -STEPS), STEPS)
    start = step * tile if isinstance(step, int) else pl.multiple_of(step * tile, tile)
    out_ref[:, pl.ds(start, tile)] = coded.astype(jnp.int32).astype(jnp.int16)
    lane = lax.broadcasted_iota(jnp.int32, (half, LANES), 1)
    kept = jnp.where(lane < step, out_ref[:, width:].astype(jnp.int32), 0)
    out_ref[:, width:] = jnp.where(lane == step, level.astype(jnp.int32), kept).astype(jnp.int16)


def decode(coded_ref, row, half, step, tile):
    width = coded_ref.shape[1] - LANES
    levels = coded_ref[row : row + half, width:].astype(jnp.int32)
    lane = lax.broadcasted_iota(jnp.int32, levels.shape, 1)
    level = jnp.sum(jnp.where(lane == step, levels, 0).astype(jnp.float32), axis=1, keepdims=True)
    value = coded_ref[row : row + half, step * tile : (step + 1) * tile].astype(jnp.int32).astype(jnp.float32)
    return value * (jnp.exp2(level * (1.0 / LEVELS)) * (1.0 / STEPS))


def merge_kernel(places, coded_out, *refs):
    out_ref = refs[-1]
    inputs = refs[:-1]
    for number, rows in enumerate(places):
        base, coded = inputs[0], inputs[1 : 1 + len(rows)]
        inputs = inputs[1 + len(rows) :]
        half, width = base.shape
        tile = tile_of(width)
        for step in range(width // tile):
            columns = slice(step * tile, (step + 1) * tile)
            total = base[:, columns]
            for one, row in zip(coded, rows):
                total = total + decode(one, row, half, step, tile)
            if coded_out:
                encode(total, out_ref, step)
            else:
                out_ref[number * half : (number + 1) * half, columns] = total.astype(out_ref.dtype)


def merge(sums, coded_out):
    half, width = sums[0][0].shape
    places = [[row for _, row in coded] for _, coded in sums]
    if coded_out:
        out_shape = jax.ShapeDtypeStruct((half, width + LANES), jnp.int16)
    else:
        out_shape = jax.ShapeDtypeStruct((len(sums) * half, width), jnp.bfloat16)
    values = []
    for base, coded in sums:
        values = values + [base] + [value for value, _ in coded]
    return pl.pallas_call(
        functools.partial(merge_kernel, places, coded_out),
        out_shape=out_shape,
        in_specs=[VMEM] * len(values),
        out_specs=VMEM,
        compiler_params=params(20),
        cost_estimate=cost(0, 2 * sum(value.size for value in values) + 4 * half * width),
    )(*values)


def o_kernel(block_ref, rows_ref, weight_ref, *refs):
    del block_ref
    outs = refs[-2:]
    total = jnp.dot(rows_ref[...], weight_ref[...], preferred_element_type=jnp.float32)
    half = outs[0].shape[0]
    for number, out_ref in enumerate(outs):
        value = total[number * half : (number + 1) * half]
        if out_ref.dtype == jnp.int16:
            encode(value, out_ref, pl.program_id(0))
        else:
            out_ref[...] = value


def o_block(block, rows_in, weight, width, leaving):
    rows, depth = rows_in.shape
    half = rows // 2
    tile = tile_of(width)
    tiles = width // tile
    shapes, specs, buffers, aliases = [], [], [], {}
    for number, one in enumerate(leaving):
        if one is None:
            shapes.append(jax.ShapeDtypeStruct((half, width), jnp.float32))
            specs.append(pl.BlockSpec((half, tile), lambda step, ref: (0, step)))
            continue
        buffer, place, places = one
        shapes.append(jax.ShapeDtypeStruct((places * half, width + LANES), jnp.int16))
        specs.append(
            pl.BlockSpec((half, width + LANES), functools.partial(lambda place, step, ref: (place, 0), place))
        )
        if buffer is not None:
            aliases[3 + len(buffers)] = number
            buffers.append(buffer)
    return pl.pallas_call(
        o_kernel,
        grid_spec=pltpu.PrefetchScalarGridSpec(
            num_scalar_prefetch=1,
            grid=(tiles,),
            in_specs=[
                pl.BlockSpec((rows, depth), lambda step, ref: (0, 0)),
                pl.BlockSpec((depth, tile), lambda step, ref: (0, ref[0] * tiles + step)),
            ]
            + [ANY] * len(buffers),
            out_specs=specs,
        ),
        out_shape=shapes,
        input_output_aliases=aliases,
        compiler_params=params(36),
        cost_estimate=cost(2 * rows * depth * width, 2 * depth * width + 2 * rows * depth + 4 * rows * width),
    )(block, rows_in, weight, *buffers)


def q_kernel(count, has_total, block_ref, *refs):
    del block_ref
    pieces = refs[:count]
    weight_ref = refs[count]
    out_ref, token_ref = refs[-2:]
    size = pieces[0].shape[0]
    token_ref[...] = jnp.zeros_like(token_ref)
    for number, rows_ref in enumerate(pieces):
        total = jnp.dot(rows_ref[...], weight_ref[...], preferred_element_type=jnp.float32)
        span = slice(number * size, (number + 1) * size)
        if has_total:
            total = total + refs[count + 1][span]
        out_ref[span] = total


def q_block(block, pieces, weight, total):
    count = len(pieces)
    size, depth = pieces[0].shape
    rows = count * size
    width = weight.shape[1]
    tile = tile_of(width)
    has_total = total is not None
    column = pl.BlockSpec((rows, tile), lambda step, ref: (0, step))
    return pl.pallas_call(
        functools.partial(q_kernel, count, has_total),
        grid_spec=pltpu.PrefetchScalarGridSpec(
            num_scalar_prefetch=1,
            grid=(width // tile,),
            in_specs=[pl.BlockSpec((size, depth), lambda step, ref: (0, 0))] * count
            + [pl.BlockSpec((depth, tile), lambda step, ref: (ref[0], step))]
            + [column] * has_total,
            out_specs=[column, pl.BlockSpec((8, LANES), lambda step, ref: (0, 0))],
        ),
        out_shape=[jax.ShapeDtypeStruct((rows, width), jnp.float32), jax.ShapeDtypeStruct((8, LANES), jnp.float32)],
        input_output_aliases={count + 2: 0} if has_total else {},
        compiler_params=params(36),
        cost_estimate=cost(2 * rows * depth * width, 2 * depth * width + 2 * rows * depth + 8 * rows * width),
    )(block, *pieces, weight, *([total] * has_total))


def share(block, chains, *pins):
    whole = {0: block}
    for bit in chains:
        whole[bit] = chains[bit].send(block, bit, *pins)
    return whole


def forward(whole, chains, *pins):
    order = list(chains)
    half = whole[0].shape[0] // 2
    parts = [{}, {}]
    for step in range(len(order)):
        for number in range(2):
            bits_used = order if number == 0 else order[::-1]
            bit = bits_used[step]
            held = [0]
            for used in bits_used[:step]:
                held = held + [dist ^ used for dist in held]
            for dist in held[1:]:
                if dist in whole:
                    piece = whole[dist][number * half : (number + 1) * half]
                else:
                    piece = parts[number][dist]
                parts[number][dist ^ bit] = chains[bit].send(piece, bit, *pins)
    pieces = {dist: [value] for dist, value in whole.items()}
    for dist in parts[0]:
        pieces[dist] = [parts[0][dist], parts[1][dist]]
    return pieces


def place_kernel(blocks, column_ref, *refs):
    out_ref, sems = refs[-2:]
    width = refs[0].shape[1]
    copies = []
    number = 0
    for block, count in enumerate(blocks):
        start = pl.multiple_of(column_ref[block] * width, width)
        for part in range(count):
            size = refs[number].shape[0]
            copy = pltpu.make_async_copy(
                refs[number], out_ref.at[pl.ds(part * size, size), pl.ds(start, width)], sems.at[number]
            )
            copy.start()
            copies.append(copy)
            number += 1
    for copy in copies:
        copy.wait()


def place(columns, blocks, into, out_shape):
    counts = [len(pieces) for pieces in blocks]
    pieces = [piece for block in blocks for piece in block]
    old = [] if into is None else [into]
    return pl.pallas_call(
        functools.partial(place_kernel, counts),
        out_shape=out_shape,
        in_specs=[SMEM] + [VMEM] * len(pieces) + [ANY] * len(old),
        out_specs=ANY,
        scratch_shapes=[pltpu.SemaphoreType.DMA((len(pieces),))],
        input_output_aliases={len(pieces) + 1: 0} if old else {},
        compiler_params=params(10),
        cost_estimate=cost(0, 4 * sum(piece.size for piece in pieces)),
    )(columns, *pieces, *old)


def body(
    hidden_rows,
    attn_rows,
    q_weight,
    o_weight,
    owner_table,
    group_adapters,
    req_slot,
    req_len,
    qa_store,
    qb_store,
    oa_store,
    ob_store,
):
    groups = lax.axis_size("group")
    size = lax.axis_size("tensor")
    mine = lax.axis_index("tensor")
    held, _, rank = qa_store.shape
    rows, _ = hidden_rows.shape
    width = o_weight.shape[1] // size
    half = rows // 2
    routing = (owner_table, group_adapters, req_slot, req_len)
    block = [jnp.reshape(mine ^ dist, (1,)).astype(jnp.int32) for dist in range(size)]
    order = bits(size)

    far = Groups("group", [groups // 2 * 4 * part // 16 for part in (3, 5, 7, 8, 10, 11, 13, 14, 16)])
    near = Chain("group")
    chains = {bit: Chain("tensor") for bit in order}
    far_dists = list(range(groups // 2, groups))
    near_dists = list(range(2, groups // 2))
    all_dists = list(range(groups))
    stores = [jnp.swapaxes(oa_store, 1, 2), ob_store, jnp.swapaxes(qa_store, 1, 2), qb_store]
    used = [{}, {}, {}, {}]

    def packed(plan, mebibytes, *pins):
        wanted = sorted({part for _, parts in plan for part in parts})
        plan = [(dist, [wanted.index(part) for part in parts]) for dist, parts in plan]
        return pack(plan, owner_table, group_adapters, [stores[part] for part in wanted], pins, mebibytes)

    def fetch_far(values, part, dists, *pins):
        for value, dist in zip(values, dists):
            used[part][dist] = (far.send(value, dist, *pins), 0)

    def fetch_near(values, parts, pins, dists):
        for value, dist, some in zip(values, dists, pins):
            arrived = near.send(value, dist, *some)
            for row, part in enumerate(parts):
                used[part][dist] = (arrived, row)

    def pieces_of(part, dists):
        return [used[part][dist] for dist in dists]

    def arrivals():
        return [chain.done[-1] for chain in chains.values()]

    def summed(value, *pins):
        arrived = send(after(value, *pins) if pins else value, "tensor", order[0])
        return value + arrived, arrived

    def summed_on(value, *pins):
        for bit in order[1:]:
            value = value + send(after(value, *pins) if pins else value, "tensor", bit)
        return value

    halving = (order, order[::-1])
    leaving = [sorted((dist for dist in range(size) if dist & halving[number][0]), reverse=True) for number in range(2)]
    buffers = [None, None]
    sums = [{}, {}]

    def o_sums(dist):
        wanted = []
        for number in range(2):
            if dist in leaving[number]:
                wanted.append((buffers[number], leaving[number].index(dist), len(leaving[number])))
            else:
                wanted.append(None)
        values = o_block(block[dist], attn_rows, o_weight, width, wanted)
        for number in range(2):
            if wanted[number] is None:
                sums[number][dist] = (values[number], [])
            else:
                buffers[number] = values[number]

    def reduce_first(*pins):
        for number in range(2):
            bit = halving[number][0]
            arrived = chains[bit].send(buffers[number], bit, *pins)
            for row, dist in enumerate(leaving[number]):
                sums[number][dist ^ bit][1].append((arrived, row * half))

    def reduce_step(step, *pins):
        for number in range(2):
            bit = halving[number][step]
            for dist in sorted((one for one in sums[number] if one & bit), reverse=True):
                arrived = chains[bit].send(merge([sums[number].pop(dist)], True), bit, *pins)
                sums[number][dist ^ bit][1].append((arrived, 0))

    hidden = share(hidden_rows, chains)
    lead, rest = far_dists[:3], far_dists[3:]
    values = packed([(dist, (0,)) for dist in lead], 60)
    fetch_far(values, 0, lead)
    plan = [(dist, (0,)) for dist in rest] + [(dist, (1,)) for dist in far_dists]
    plan = plan + [(dist, (0, 1)) for dist in near_dists] + [(1, (0, 1, 2, 3)), (0, (0, 1, 2, 3))]
    o_values = packed(plan, 57, *values)
    fetch_far(o_values, 0, rest)
    fetch_far(o_values[len(rest) :], 1, far_dists[:3])
    near_values = o_values[len(rest) + len(far_dists) : -2]
    fetch_near(near_values, (0, 1), [far.upto(0)], near_dists[:1])
    found = row_distances(routing, held, rows, 2 * rank)
    for dist in sorted(range(1, size), reverse=True):
        o_sums(dist)

    hidden = forward(hidden, chains, *far.upto(0), *buffers, found, o_values[0])
    o_sums(0)
    q_total = None
    q_ready = []
    for dist in range(size):
        q_total, token = q_block(block[dist], hidden[dist], q_weight, q_total)
        q_ready.append(token)
    plan = [(dist, (part,)) for part in (2, 3) for dist in far_dists] + [(dist, (2, 3)) for dist in near_dists]
    values = packed(plan, 10, *far.upto(0))
    pins = [*far.upto(1), sums[0][0][0], values[0], q_ready[0]]
    fetch_near(near_values[1:], (0, 1), [pins], near_dists[1:])

    reduce_first(*far.upto(1), near.done[0], sums[0][0][0], values[0], *q_ready[:1])
    pins = (near.done[-1], *q_ready[1 : size // 2 + 1])
    beside = send(after(tie(o_values[-2], pins), *far.upto(2)), "group", 1)
    for part in range(4):
        used[part][1] = (beside, part)
        used[part][0] = (o_values[-1], part)
    tied = [tie(value, pins) for value in o_values[len(rest) + 3 : -len(near_dists) - 2]]
    fetch_far(tied, 1, far_dists[3:])
    fetch_far(values, 2, far_dists[:2])
    fetch_far(values[2:], 2, far_dists[2:], q_ready[-1])
    fetch_far(values[len(far_dists) :], 3, far_dists)
    o_half = down(found, rank, attn_rows, pieces_of(0, all_dists))
    o_down, o_arrived = summed(o_half)
    pins = [*far.upto(3), o_arrived]
    o_down = summed_on(o_down, *arrivals())
    for step in range(1, len(order)):
        reduce_step(step, *pins)
    late = values[2 * len(far_dists) :][::-1]
    fetch_near(late, (2, 3), [far.upto(3), far.upto(5)], near_dists[::-1])
    bases = up(found, rank, o_down, used[1], all_dists, [one[0][0] for one in sums], jnp.float32)
    rounded = merge([(base, one[0][1]) for base, one in zip(bases, sums)], False)

    finished = share(rounded, chains, *far.upto(5), near.done[len(near_dists)], q_ready[-1])
    q_half = down(after(found, o_down), rank, hidden_rows, pieces_of(2, all_dists))
    q_down = summed_on(summed(q_half)[0])

    finished = forward(finished, chains, *far.upto(7), q_down)

    out_shape = jax.ShapeDtypeStruct((rows, width * size), jnp.bfloat16)
    soon = [dist for dist in range(size) if len(finished[dist]) == 1]
    late = [dist for dist in range(size) if len(finished[dist]) > 1]

    def placed(dists, into):
        columns = jnp.concatenate([block[dist] for dist in dists])
        return place(columns, [finished[dist] for dist in dists], into, out_shape)

    attn_out = placed(soon, None)
    last = far_dists[-2:]
    first = [dist for dist in all_dists if dist not in last]
    (total,) = up(found, rank, q_down, used[3], first, [after(q_total, attn_out)], jnp.float32)
    attn_out = placed(late, attn_out)
    (queries,) = up(found, rank, q_down, used[3], last, [after(total, attn_out)], jnp.bfloat16)
    return (queries, attn_out)


def solution(mesh):
    return jax.shard_map(
        body,
        mesh=mesh,
        in_specs=(
            P("group", "tensor"),
            P("group", "tensor"),
            P(None, "tensor"),
            P("tensor", None),
            P(),
            P(),
            P("group", None),
            P("group", None),
            P("group", "tensor", None),
            P("group", None, "tensor"),
            P("group", "tensor", None),
            P("group", None, "tensor"),
        ),
        out_specs=(P("group", "tensor"), P("group", None)),
        check_vma=False,
    )
```

```python
import functools
import math

import jax
import jax.numpy as jnp
from jax import lax
from jax.experimental import pallas as pl
from jax.experimental.pallas import tpu as pltpu
from jax.sharding import PartitionSpec as P

ADAPTER_SCALE = 0.5
LANES = 128
LEVELS = 8
STEPS = 32767.0
MIB = 1024 * 1024
ANY = pl.BlockSpec(memory_space=pl.ANY)
SMEM = pl.BlockSpec(memory_space=pltpu.SMEM)
VMEM = pl.BlockSpec(memory_space=pltpu.VMEM)
HBM = pl.BlockSpec(memory_space=pltpu.HBM)


def params(mebibytes):
    return pltpu.CompilerParams(vmem_limit_bytes=mebibytes * MIB)


def cost(flops, nbytes):
    return pl.CostEstimate(flops=flops // 1000, bytes_accessed=nbytes // 1000, transcendentals=0)


def send(value, axis, offset):
    size = lax.axis_size(axis)
    return lax.ppermute(value, axis, [(i, i ^ offset) for i in range(size)])


def after(value, *others):
    return lax.optimization_barrier((value, *others))[0]


def at(values, *numbers):
    return [values[number] for number in numbers if number < len(values)]


def tie_kernel(*refs):
    del refs


def tie(value, others):
    return pl.pallas_call(
        tie_kernel,
        out_shape=pltpu.HBM(value.shape, value.dtype),
        in_specs=[ANY] * (1 + len(others)),
        out_specs=HBM,
        input_output_aliases={0: 0},
        compiler_params=params(1),
        cost_estimate=cost(0, 0),
    )(value, *others)


class Chain:
    def __init__(self, axis):
        self.axis = axis
        self.done = []

    def send(self, value, offset, *pins):
        pins = (*self.done[-1:], *pins)
        if pins:
            value = after(value, *pins)
        arrived = send(value, self.axis, offset)
        self.done.append(arrived)
        return arrived


class Groups:
    def __init__(self, axis, ends):
        self.axis = axis
        self.ends = ends
        self.done = []

    def upto(self, step):
        start = self.ends[step - 1] if step else 0
        return self.done[start : self.ends[step]]

    def send(self, value, offset, *pins):
        number = len(self.done)
        step = sum(end <= number for end in self.ends)
        if step:
            value = after(value, *self.upto(step - 1), *pins)
        arrived = send(value, self.axis, offset)
        self.done.append(arrived)
        return arrived


def bits(size):
    out = []
    bit = 1
    while bit < size:
        out.append(bit)
        bit *= 2
    return out


def pack_kernel(plan, count, table_ref, adapters_ref, *refs):
    stores = refs[:count]
    outs = refs[-3 - len(plan) : -3]
    staged, in_sems, out_sems = refs[-3:]
    slots = adapters_ref.shape[1]
    held, rank, _ = stores[0].shape
    me = lax.axis_index("group")
    loads = []
    for dist, parts in plan:
        dest = me ^ dist
        pick = jnp.int32(0)
        for slot in range(slots):
            place = table_ref[adapters_ref[dest, slot]]
            owner = lax.div(place, jnp.int32(held))
            pick = jnp.where(owner == me, place - owner * held, pick)
        for part in parts:
            number = len(loads)
            load = pltpu.make_async_copy(stores[part].at[pick], staged.at[number], in_sems.at[number])
            load.start()
            loads.append(load)
    copies = []
    for out_ref, (_, parts) in zip(outs, plan):
        for row in range(len(parts)):
            number = len(copies)
            loads[number].wait()
            copy = pltpu.make_async_copy(
                staged.at[number], out_ref.at[pl.ds(row * rank, rank)], out_sems.at[number]
            )
            copy.start()
            copies.append(copy)
    for copy in copies:
        copy.wait()


def pack(plan, table, adapters, stores, order, mebibytes):
    _, rank, width = stores[0].shape
    dtype = stores[0].dtype
    total = sum(len(parts) for _, parts in plan)
    return pl.pallas_call(
        functools.partial(pack_kernel, plan, len(stores)),
        out_shape=[pltpu.HBM((len(parts) * rank, width), dtype) for _, parts in plan],
        in_specs=[SMEM, SMEM] + [HBM] * len(stores) + [ANY] * len(order),
        out_specs=[HBM] * len(plan),
        scratch_shapes=[
            pltpu.VMEM((total, rank, width), dtype),
            pltpu.SemaphoreType.DMA((total,)),
            pltpu.SemaphoreType.DMA((total,)),
        ],
        compiler_params=params(mebibytes),
        cost_estimate=cost(0, 4 * total * rank * width),
    )(table, adapters, *stores, *order)


def distance_kernel(held, table_ref, adapters_ref, slot_ref, len_ref, out_ref):
    me = lax.axis_index("group")
    position = lax.broadcasted_iota(jnp.int32, out_ref.shape, 0)
    found = jnp.zeros(out_ref.shape, jnp.int32)
    start = jnp.int32(0)
    for req in range(len_ref.shape[1]):
        place = table_ref[adapters_ref[me, slot_ref[0, req]]]
        dist = lax.div(place, jnp.int32(held)) ^ me
        end = start + len_ref[0, req]
        found = jnp.where((position >= start) & (position < end), dist, found)
        start = end
    out_ref[...] = found


def row_distances(routing, held, rows, lanes):
    return pl.pallas_call(
        functools.partial(distance_kernel, held),
        out_shape=jax.ShapeDtypeStruct((rows, lanes), jnp.int32),
        in_specs=[SMEM] * 4,
        out_specs=VMEM,
        compiler_params=params(4),
        cost_estimate=cost(0, 4 * rows * lanes),
    )(*routing)


def down_kernel(rank, places, found_ref, rows_ref, *refs):
    groups = len(places)
    pieces = refs[:groups]
    out_ref, whole, sems = refs[-3:]
    copies = []
    for dist in range(groups):
        copy = pltpu.make_async_copy(
            pieces[dist].at[pl.ds(places[dist] * rank, rank)], whole.at[pl.ds(dist * rank, rank)], sems.at[dist]
        )
        copy.start()
        copies.append(copy)
    shape = (rows_ref.shape[0], 2 * rank)
    found = found_ref[...]
    high = (lax.broadcasted_iota(jnp.int32, shape, 1) >= rank).astype(jnp.int32)
    for copy in copies:
        copy.wait()
    full = lax.dot_general(
        rows_ref[...], whole[...], (((1,), (1,)), ((), ())), preferred_element_type=jnp.float32
    )
    picked = jnp.zeros(shape, jnp.float32)
    for pair in range(groups // 2):
        piece = full[:, pair * 2 * rank : (pair + 1) * 2 * rank]
        picked = picked + jnp.where(found == 2 * pair + high, piece, 0.0)
    picked = picked + pltpu.roll(picked, rank, 1)
    half = out_ref.shape[0]
    out_ref[...] = jnp.where(high[:half] == 0, picked[:half], picked[half:])


def down(found, rank, rows_in, pieces, order=()):
    rows, width = rows_in.shape
    groups = len(pieces)
    return pl.pallas_call(
        functools.partial(down_kernel, rank, [row for _, row in pieces]),
        out_shape=jax.ShapeDtypeStruct((rows // 2, 2 * rank), jnp.float32),
        in_specs=[VMEM] * 2 + [ANY] * (groups + len(order)),
        out_specs=VMEM,
        scratch_shapes=[
            pltpu.VMEM((groups * rank, width), rows_in.dtype),
            pltpu.SemaphoreType.DMA((groups,)),
        ],
        compiler_params=params(12),
        cost_estimate=cost(2 * rows * width * groups * rank, 2 * rows * width + 2 * groups * rank * width),
    )(found, rows_in, *[piece for piece, _ in pieces], *order)


def up_kernel(dists, split, found_ref, down_ref, *refs):
    groups = len(dists)
    pieces = refs[:groups]
    bases = refs[groups : groups + split]
    outs = refs[groups + split : groups + 2 * split]
    terms = refs[-1]
    rank = pieces[0].shape[0]
    rows = found_ref.shape[0]

    @pl.when(pl.program_id(0) == 0)
    def _():
        shape = (rows, 2 * rank)
        found = found_ref[...]
        low = lax.broadcasted_iota(jnp.int32, shape, 1) < rank
        folded = down_ref[...] * ADAPTER_SCALE
        turned = pltpu.roll(folded, rank, 1)
        first_half = low[: rows // 2]
        both = jnp.concatenate(
            [jnp.where(first_half, folded, turned), jnp.where(first_half, turned, folded)], axis=0
        )
        first = both.astype(jnp.bfloat16)
        second = (both - first.astype(jnp.float32)).astype(jnp.bfloat16)
        for number, term in enumerate((first, second)):
            for pair in range(groups // 2):
                wanted = jnp.where(low, dists[2 * pair], dists[2 * pair + 1])
                chosen = jnp.where(found == wanted, term.astype(jnp.float32), 0.0)
                start = number * groups * rank + pair * 2 * rank
                terms[:, start : start + 2 * rank] = chosen.astype(jnp.bfloat16)

    whole = jnp.concatenate([piece[...] for piece in pieces] * 2, axis=0)
    total = jnp.dot(terms[...], whole, preferred_element_type=jnp.float32)
    size = rows // split
    for number in range(split):
        value = bases[number][...] + total[number * size : (number + 1) * size]
        outs[number][...] = value.astype(outs[number].dtype)


def up(found, rank, downs, used, dists, bases, out_dtype):
    pieces = [used[dist] for dist in dists]
    groups = len(dists)
    width = pieces[0][0].shape[1]
    rows = found.shape[0]
    split = len(bases)
    tile = min(512, width)
    column = lambda step: (0, step)
    size = rows // split
    piece_specs = [
        pl.BlockSpec((rank, tile), functools.partial(lambda place, step: (place, step), place)) for _, place in pieces
    ]
    return pl.pallas_call(
        functools.partial(up_kernel, dists, split),
        grid=(width // tile,),
        out_shape=[jax.ShapeDtypeStruct((size, width), out_dtype)] * split,
        in_specs=[pl.BlockSpec(found.shape, lambda step: (0, 0)), pl.BlockSpec(downs.shape, lambda step: (0, 0))]
        + piece_specs
        + [pl.BlockSpec((size, tile), column)] * split,
        out_specs=[pl.BlockSpec((size, tile), column)] * split,
        scratch_shapes=[pltpu.VMEM((rows, 2 * groups * rank), jnp.bfloat16)],
        compiler_params=params(16),
        cost_estimate=cost(4 * rows * width * groups * rank, 8 * rows * width + 2 * groups * rank * width),
    )(found, downs, *[piece for piece, _ in pieces], *bases)


def tile_of(width):
    return min(512, width)


def encode(value, out_ref, step):
    half, tile = value.shape
    width = out_ref.shape[1] - LANES
    peak = jnp.max(jnp.abs(value), axis=1, keepdims=True)
    level = jnp.ceil(jnp.log(jnp.maximum(peak, 1e-30)) * (LEVELS / math.log(2.0)))
    coded = jnp.round(value * (jnp.exp2(level * (-1.0 / LEVELS)) * STEPS))
    coded = jnp.minimum(jnp.maximum(coded, -STEPS), STEPS)
    start = step * tile if isinstance(step, int) else pl.multiple_of(step * tile, tile)
    out_ref[:, pl.ds(start, tile)] = coded.astype(jnp.int32).astype(jnp.int16)
    lane = lax.broadcasted_iota(jnp.int32, (half, LANES), 1)
    kept = jnp.where(lane < step, out_ref[:, width:].astype(jnp.int32), 0)
    out_ref[:, width:] = jnp.where(lane == step, level.astype(jnp.int32), kept).astype(jnp.int16)


def decode(coded_ref, row, half, step, tile):
    width = coded_ref.shape[1] - LANES
    levels = coded_ref[row : row + half, width:].astype(jnp.int32)
    lane = lax.broadcasted_iota(jnp.int32, levels.shape, 1)
    level = jnp.sum(jnp.where(lane == step, levels, 0).astype(jnp.float32), axis=1, keepdims=True)
    value = coded_ref[row : row + half, step * tile : (step + 1) * tile].astype(jnp.int32).astype(jnp.float32)
    return value * (jnp.exp2(level * (1.0 / LEVELS)) * (1.0 / STEPS))


def merge_kernel(places, coded_out, *refs):
    out_ref = refs[-1]
    inputs = refs[:-1]
    for number, rows in enumerate(places):
        base, coded = inputs[0], inputs[1 : 1 + len(rows)]
        inputs = inputs[1 + len(rows) :]
        half, width = base.shape
        tile = tile_of(width)
        for step in range(width // tile):
            columns = slice(step * tile, (step + 1) * tile)
            total = base[:, columns]
            for one, row in zip(coded, rows):
                total = total + decode(one, row, half, step, tile)
            if coded_out:
                encode(total, out_ref, step)
            else:
                out_ref[number * half : (number + 1) * half, columns] = total.astype(out_ref.dtype)


def merge(sums, coded_out):
    half, width = sums[0][0].shape
    places = [[row for _, row in coded] for _, coded in sums]
    if coded_out:
        out_shape = jax.ShapeDtypeStruct((half, width + LANES), jnp.int16)
    else:
        out_shape = jax.ShapeDtypeStruct((len(sums) * half, width), jnp.bfloat16)
    values = []
    for base, coded in sums:
        values = values + [base] + [value for value, _ in coded]
    return pl.pallas_call(
        functools.partial(merge_kernel, places, coded_out),
        out_shape=out_shape,
        in_specs=[VMEM] * len(values),
        out_specs=VMEM,
        compiler_params=params(20),
        cost_estimate=cost(0, 2 * sum(value.size for value in values) + 4 * half * width),
    )(*values)


def o_kernel(block_ref, rows_ref, weight_ref, *refs):
    del block_ref
    outs = refs[-2:]
    total = jnp.dot(rows_ref[...], weight_ref[...], preferred_element_type=jnp.float32)
    half = outs[0].shape[0]
    for number, out_ref in enumerate(outs):
        value = total[number * half : (number + 1) * half]
        if out_ref.dtype == jnp.int16:
            encode(value, out_ref, pl.program_id(0))
        else:
            out_ref[...] = value


def o_block(block, rows_in, weight, width, leaving):
    rows, depth = rows_in.shape
    half = rows // 2
    tile = tile_of(width)
    tiles = width // tile
    shapes, specs, buffers, aliases = [], [], [], {}
    for number, one in enumerate(leaving):
        if one is None:
            shapes.append(jax.ShapeDtypeStruct((half, width), jnp.float32))
            specs.append(pl.BlockSpec((half, tile), lambda step, ref: (0, step)))
            continue
        buffer, place, places = one
        shapes.append(jax.ShapeDtypeStruct((places * half, width + LANES), jnp.int16))
        specs.append(
            pl.BlockSpec((half, width + LANES), functools.partial(lambda place, step, ref: (place, 0), place))
        )
        if buffer is not None:
            aliases[3 + len(buffers)] = number
            buffers.append(buffer)
    return pl.pallas_call(
        o_kernel,
        grid_spec=pltpu.PrefetchScalarGridSpec(
            num_scalar_prefetch=1,
            grid=(tiles,),
            in_specs=[
                pl.BlockSpec((rows, depth), lambda step, ref: (0, 0)),
                pl.BlockSpec((depth, tile), lambda step, ref: (0, ref[0] * tiles + step)),
            ]
            + [ANY] * len(buffers),
            out_specs=specs,
        ),
        out_shape=shapes,
        input_output_aliases=aliases,
        compiler_params=params(36),
        cost_estimate=cost(2 * rows * depth * width, 2 * depth * width + 2 * rows * depth + 4 * rows * width),
    )(block, rows_in, weight, *buffers)


def q_kernel(count, has_total, block_ref, *refs):
    del block_ref
    pieces = refs[:count]
    weight_ref = refs[count]
    out_ref, token_ref = refs[-2:]
    size = pieces[0].shape[0]
    token_ref[...] = jnp.zeros_like(token_ref)
    for number, rows_ref in enumerate(pieces):
        total = jnp.dot(rows_ref[...], weight_ref[...], preferred_element_type=jnp.float32)
        span = slice(number * size, (number + 1) * size)
        if has_total:
            total = total + refs[count + 1][span]
        out_ref[span] = total


def q_block(block, pieces, weight, total):
    count = len(pieces)
    size, depth = pieces[0].shape
    rows = count * size
    width = weight.shape[1]
    tile = tile_of(width)
    has_total = total is not None
    column = pl.BlockSpec((rows, tile), lambda step, ref: (0, step))
    return pl.pallas_call(
        functools.partial(q_kernel, count, has_total),
        grid_spec=pltpu.PrefetchScalarGridSpec(
            num_scalar_prefetch=1,
            grid=(width // tile,),
            in_specs=[pl.BlockSpec((size, depth), lambda step, ref: (0, 0))] * count
            + [pl.BlockSpec((depth, tile), lambda step, ref: (ref[0], step))]
            + [column] * has_total,
            out_specs=[column, pl.BlockSpec((8, LANES), lambda step, ref: (0, 0))],
        ),
        out_shape=[jax.ShapeDtypeStruct((rows, width), jnp.float32), jax.ShapeDtypeStruct((8, LANES), jnp.float32)],
        input_output_aliases={count + 2: 0} if has_total else {},
        compiler_params=params(36),
        cost_estimate=cost(2 * rows * depth * width, 2 * depth * width + 2 * rows * depth + 8 * rows * width),
    )(block, *pieces, weight, *([total] * has_total))


def share(block, chains, *pins):
    whole = {0: block}
    for bit in chains:
        whole[bit] = chains[bit].send(block, bit, *pins)
    return whole


def forward(whole, chains, *pins):
    order = list(chains)
    half = whole[0].shape[0] // 2
    parts = [{}, {}]
    for step in range(len(order)):
        for number in range(2):
            bits_used = order if number == 0 else order[::-1]
            bit = bits_used[step]
            held = [0]
            for used in bits_used[:step]:
                held = held + [dist ^ used for dist in held]
            for dist in held[1:]:
                if dist in whole:
                    piece = whole[dist][number * half : (number + 1) * half]
                else:
                    piece = parts[number][dist]
                parts[number][dist ^ bit] = chains[bit].send(piece, bit, *pins)
    pieces = {dist: [value] for dist, value in whole.items()}
    for dist in parts[0]:
        pieces[dist] = [parts[0][dist], parts[1][dist]]
    return pieces


def place_kernel(blocks, column_ref, *refs):
    out_ref, sems = refs[-2:]
    width = refs[0].shape[1]
    copies = []
    number = 0
    for block, count in enumerate(blocks):
        start = pl.multiple_of(column_ref[block] * width, width)
        for part in range(count):
            size = refs[number].shape[0]
            copy = pltpu.make_async_copy(
                refs[number], out_ref.at[pl.ds(part * size, size), pl.ds(start, width)], sems.at[number]
            )
            copy.start()
            copies.append(copy)
            number += 1
    for copy in copies:
        copy.wait()


def place(columns, blocks, into, out_shape):
    counts = [len(pieces) for pieces in blocks]
    pieces = [piece for block in blocks for piece in block]
    old = [] if into is None else [into]
    return pl.pallas_call(
        functools.partial(place_kernel, counts),
        out_shape=out_shape,
        in_specs=[SMEM] + [VMEM] * len(pieces) + [ANY] * len(old),
        out_specs=ANY,
        scratch_shapes=[pltpu.SemaphoreType.DMA((len(pieces),))],
        input_output_aliases={len(pieces) + 1: 0} if old else {},
        compiler_params=params(10),
        cost_estimate=cost(0, 4 * sum(piece.size for piece in pieces)),
    )(columns, *pieces, *old)


def body(
    hidden_rows,
    attn_rows,
    q_weight,
    o_weight,
    owner_table,
    group_adapters,
    req_slot,
    req_len,
    qa_store,
    qb_store,
    oa_store,
    ob_store,
):
    groups = lax.axis_size("group")
    size = lax.axis_size("tensor")
    mine = lax.axis_index("tensor")
    held, _, rank = qa_store.shape
    rows, _ = hidden_rows.shape
    width = o_weight.shape[1] // size
    half = rows // 2
    routing = (owner_table, group_adapters, req_slot, req_len)
    block = [jnp.reshape(mine ^ dist, (1,)).astype(jnp.int32) for dist in range(size)]
    order = bits(size)

    far = Groups("group", [groups // 2 * 4 * part // 16 for part in (3, 5, 7, 8, 10, 11, 13, 14, 16)])
    near = Chain("group")
    chains = {bit: Chain("tensor") for bit in order}
    far_dists = list(range(groups // 2, groups))
    near_dists = list(range(2, groups // 2))
    all_dists = list(range(groups))
    stores = [jnp.swapaxes(oa_store, 1, 2), ob_store, jnp.swapaxes(qa_store, 1, 2), qb_store]
    used = [{}, {}, {}, {}]

    def packed(plan, mebibytes, *pins):
        wanted = sorted({part for _, parts in plan for part in parts})
        plan = [(dist, [wanted.index(part) for part in parts]) for dist, parts in plan]
        return pack(plan, owner_table, group_adapters, [stores[part] for part in wanted], pins, mebibytes)

    def fetch_far(values, part, dists, *pins):
        for value, dist in zip(values, dists):
            used[part][dist] = (far.send(value, dist, *pins), 0)

    def fetch_near(values, parts, pins, dists):
        for value, dist, some in zip(values, dists, pins):
            arrived = near.send(value, dist, *some)
            for row, part in enumerate(parts):
                used[part][dist] = (arrived, row)

    def pieces_of(part, dists):
        return [used[part][dist] for dist in dists]

    def arrivals():
        return [chain.done[-1] for chain in chains.values()]

    def summed(value, *pins):
        arrived = send(after(value, *pins) if pins else value, "tensor", order[0])
        return value + arrived, arrived

    def summed_on(value, *pins):
        for bit in order[1:]:
            value = value + send(after(value, *pins) if pins else value, "tensor", bit)
        return value

    halving = (order, order[::-1])
    leaving = [sorted((dist for dist in range(size) if dist & halving[number][0]), reverse=True) for number in range(2)]
    buffers = [None, None]
    sums = [{}, {}]

    def o_sums(dist):
        wanted = []
        for number in range(2):
            if dist in leaving[number]:
                wanted.append((buffers[number], leaving[number].index(dist), len(leaving[number])))
            else:
                wanted.append(None)
        values = o_block(block[dist], attn_rows, o_weight, width, wanted)
        for number in range(2):
            if wanted[number] is None:
                sums[number][dist] = (values[number], [])
            else:
                buffers[number] = values[number]

    def reduce_first(*pins):
        for number in range(2):
            bit = halving[number][0]
            arrived = chains[bit].send(buffers[number], bit, *pins)
            for row, dist in enumerate(leaving[number]):
                sums[number][dist ^ bit][1].append((arrived, row * half))

    def reduce_step(step, *pins):
        for number in range(2):
            bit = halving[number][step]
            for dist in sorted((one for one in sums[number] if one & bit), reverse=True):
                arrived = chains[bit].send(merge([sums[number].pop(dist)], True), bit, *pins)
                sums[number][dist ^ bit][1].append((arrived, 0))

    hidden = share(hidden_rows, chains)
    lead, rest = far_dists[:3], far_dists[3:]
    values = packed([(dist, (0,)) for dist in lead], 60)
    fetch_far(values, 0, lead)
    plan = [(dist, (0,)) for dist in rest] + [(dist, (1,)) for dist in far_dists]
    plan = plan + [(dist, (0, 1)) for dist in near_dists] + [(1, (0, 1, 2, 3)), (0, (0, 1, 2, 3))]
    o_values = packed(plan, 57, *values)
    fetch_far(o_values, 0, rest)
    fetch_far(o_values[len(rest) :], 1, far_dists[:3])
    near_values = o_values[len(rest) + len(far_dists) : -2]
    fetch_near(near_values, (0, 1), [far.upto(0)], near_dists[:1])
    found = row_distances(routing, held, rows, 2 * rank)
    for dist in sorted(range(1, size), reverse=True):
        o_sums(dist)

    o_sums(0)
    hidden = forward(hidden, chains, *far.upto(0), *buffers, found, o_values[0], sums[0][0][0])
    q_total = None
    q_ready = []
    for dist in range(size):
        q_total, token = q_block(block[dist], hidden[dist], q_weight, q_total)
        q_ready.append(token)
    plan = [(dist, (part,)) for part in (2, 3) for dist in far_dists] + [(dist, (2, 3)) for dist in near_dists]
    values = packed(plan, 10, *far.upto(0))
    fetch_near(near_values[1:], (0, 1), [far.upto(0)], near_dists[1:])

    reduce_first(near.done[0])
    pins = (near.done[-1], q_ready[1], values[0])
    beside = send(after(tie(o_values[-2], pins), *far.upto(2)), "group", 1)
    for part in range(4):
        used[part][1] = (beside, part)
        used[part][0] = (o_values[-1], part)
    tied = [tie(value, pins) for value in o_values[len(rest) + 3 : -len(near_dists) - 2]]
    fetch_far(tied, 1, far_dists[3:])
    fetch_far(values, 2, far_dists[:2])
    fetch_far(values[2:], 2, far_dists[2:], q_ready[-1])
    fetch_far(values[len(far_dists) :], 3, far_dists)
    o_half = down(found, rank, attn_rows, pieces_of(0, all_dists))
    o_down, o_arrived = summed(o_half)
    pins = [*far.upto(3), o_arrived]
    o_down = summed_on(o_down, *arrivals())
    for step in range(1, len(order)):
        reduce_step(step, *pins)
    late = values[2 * len(far_dists) :][::-1]
    fetch_near(late, (2, 3), [far.upto(3), far.upto(5)], near_dists[::-1])
    bases = up(found, rank, o_down, used[1], all_dists, [one[0][0] for one in sums], jnp.float32)
    rounded = merge([(base, one[0][1]) for base, one in zip(bases, sums)], False)

    finished = share(rounded, chains, *far.upto(5), near.done[len(near_dists)], q_ready[-1])
    q_half = down(after(found, o_down), rank, hidden_rows, pieces_of(2, all_dists))
    q_down = summed_on(summed(q_half)[0])

    finished = forward(finished, chains, *far.upto(7), q_down)

    out_shape = jax.ShapeDtypeStruct((rows, width * size), jnp.bfloat16)
    soon = [dist for dist in range(size) if len(finished[dist]) == 1]
    late = [dist for dist in range(size) if len(finished[dist]) > 1]

    def placed(dists, into):
        columns = jnp.concatenate([block[dist] for dist in dists])
        return place(columns, [finished[dist] for dist in dists], into, out_shape)

    attn_out = placed(soon, None)
    last = far_dists[-2:]
    first = [dist for dist in all_dists if dist not in last]
    (total,) = up(found, rank, q_down, used[3], first, [after(q_total, attn_out)], jnp.float32)
    attn_out = placed(late, attn_out)
    (queries,) = up(found, rank, q_down, used[3], last, [after(total, attn_out)], jnp.bfloat16)
    return (queries, attn_out)


def solution(mesh):
    return jax.shard_map(
        body,
        mesh=mesh,
        in_specs=(
            P("group", "tensor"),
            P("group", "tensor"),
            P(None, "tensor"),
            P("tensor", None),
            P(),
            P(),
            P("group", None),
            P("group", None),
            P("group", "tensor", None),
            P("group", None, "tensor"),
            P("group", "tensor", None),
            P("group", None, "tensor"),
        ),
        out_specs=(P("group", "tensor"), P("group", None)),
        check_vma=False,
    )
```
